128 devices in a mesh: pipe: 4 (over x), chan: 8 (over y_hi, z), dp: 4 (over y_lo, core).
Axes of the slice: x: 4, y: 4 (y_hi: 2, y_lo: 2; y = y_hi * 2 + y_lo), z: 4, core: 2. Of those that a mesh axis runs over, the one named last changes fastest.
Arguments:
- tokens: bfloat16 [2, 1152, 512], P(None, 'dp', 'chan'), may hold values from -6 to 6
- seq_lengths: int32 [2, 2], replicated, may hold values from 1 to 1151, as said below
- out_cot: bfloat16 [2, 1152, 512], P(None, 'dp', 'chan'), may hold values from -6 to 6
- s4_vectors: float32 [4, 4, 512], P('pipe', None, 'chan'), may hold values from -7 to 2, as said below
- s4_modes: float32 [4, 8, 512, 32], P('pipe', None, 'chan'), may hold values from -4 to 128, as said below
- glu_weight: bfloat16 [4, 512, 2, 512], P('pipe', None, None, 'chan'), may hold values from -0.5 to 0.5
- glu_bias: float32 [4, 2, 512], P('pipe', None, 'chan'), may hold values from -3 to 3
- ffn_vectors: float32 [4, 3, 512], P('pipe', None, 'chan'), may hold values from -1 to 2, as said below
- up_weight: bfloat16 [4, 512, 2048], P('pipe', None, 'chan'), may hold values from -0.25 to 0.25
- up_bias: bfloat16 [4, 2048], P('pipe', 'chan'), may hold values from -3 to 3
- down_weight: bfloat16 [4, 2048, 512], P('pipe', 'chan'), may hold values from -0.125 to 0.125
Outputs:
- hidden_states: bfloat16 [4, 2, 1152, 512], P('pipe', None, 'dp', 'chan')
- input_grads: bfloat16 [4, 2, 1152, 512], P('pipe', None, 'dp', 'chan')
- grad_s4_vectors: float32 [4, 4, 512], P('pipe', None, 'chan')
- grad_s4_modes: float32 [4, 8, 512, 32], P('pipe', None, 'chan')
- grad_glu_weight: float32 [4, 512, 2, 512], P('pipe', None, None, 'chan')
- grad_glu_bias: float32 [4, 2, 512], P('pipe', None, 'chan')
- grad_ffn_vectors: float32 [4, 3, 512], P('pipe', None, 'chan')
- grad_up_weight: float32 [4, 512, 2048], P('pipe', None, 'chan')
- grad_up_bias: float32 [4, 2048], P('pipe', 'chan')
- grad_down_weight: float32 [4, 2048, 512], P('pipe', 'chan')
The draws below stay inside these ranges and needn't reach their ends.
Inputs may be any that keep to these rules, and one draw needn't show every extreme that they name: `seq_lengths`: the 2 lengths of each micro-batch sum to 1152; in each micro-batch one of the sequences has 1080 tokens or more, so it has tokens on every index of dp. `s4_vectors`: row 2 lies between log(0.001) and log(0.01); row 0 lies between 0.5 and 2. `s4_modes`: row 0 lies between 0.3 and 10, row 1 between 0 and pi * 32. `ffn_vectors`: row 0 lies between 0.5 and 2.
All inputs are finite; a program needn't handle non-finite values.
Results may differ from the reference program's by a relative error of at most 0.033.
Values may be sent and summed in bfloat16 or wider, within the bound.
A program may use at most 192 MiB of HBM per device.

```python
import math
import jax
import jax.numpy as jnp
from jax import lax

D = 512
FF = 2048
NH = 32
TOK_DEV = 288
MICRO = 2
LAYERS = 4
MB_TOK = 1152


def draw_seq_lengths(key, part):
    key = jax.random.fold_in(key, 11)
    short_most = TOK_DEV // 4
    chosen = jax.random.randint(key, (MICRO,), 0, 2 * short_most)
    first_len = jnp.where(chosen < short_most, chosen + 1, MB_TOK - short_most + (chosen - short_most))
    return jnp.stack([first_len, MB_TOK - first_len], axis=1).astype(jnp.int32)


def draw_s4_vectors(key, part):
    key = jax.random.fold_in(key, 23)
    subkeys = jax.random.split(key, 4)
    row_shape = (LAYERS, D)
    gains = jnp.exp(jax.random.uniform(subkeys[0], row_shape, jnp.float32, math.log(0.5), math.log(2.0)))
    biases = 0.5 * jnp.clip(jax.random.normal(subkeys[1], row_shape, jnp.float32), -2.0, 2.0)
    steps_log = jax.random.uniform(subkeys[2], row_shape, jnp.float32, math.log(0.001), math.log(0.01))
    skips = jax.random.uniform(subkeys[3], row_shape, jnp.float32, -1.0, 1.0)
    return jnp.stack([gains, biases, steps_log, skips], axis=1)


def draw_s4_modes(key, part):
    key = jax.random.fold_in(key, 29)
    subkeys = jax.random.split(key, 3)
    mode_shape = (LAYERS, D, NH)
    decays = jnp.exp(jax.random.uniform(subkeys[0], mode_shape, jnp.float32, math.log(0.3), math.log(10.0)))
    others = jnp.clip(jax.random.normal(subkeys[2], (6,) + mode_shape, jnp.float32), -4.0, 4.0)
    rates = math.pi * (jnp.arange(NH, dtype=jnp.float32) + jax.random.uniform(subkeys[1], mode_shape, jnp.float32))
    scales = jnp.array([0.7, 0.7, 1.0, 1.0, 1.0, 1.0], jnp.float32)[:, None, None, None]
    return jnp.concatenate([decays[:, None], rates[:, None], jnp.moveaxis(others * scales, 0, 1)], axis=1)


def draw_ffn_vectors(key, part):
    key = jax.random.fold_in(key, 31)
    subkeys = jax.random.split(key, 3)
    row_shape = (LAYERS, D)
    gains = jnp.exp(jax.random.uniform(subkeys[0], row_shape, jnp.float32, math.log(0.5), math.log(2.0)))
    biases = 0.5 * jnp.clip(jax.random.normal(subkeys[1], row_shape, jnp.float32), -2.0, 2.0)
    outer = 0.5 * jnp.clip(jax.random.normal(subkeys[2], row_shape, jnp.float32), -2.0, 2.0)
    return jnp.stack([gains, biases, outer], axis=1)


def levels(key, shape, pieces, least, high):
    level, own = 1.0, jax.random.fold_in(key, 6)
    for position, blocks in pieces:
        heights = jnp.exp(jax.random.uniform(jax.random.fold_in(own, position), (blocks,), jnp.float32, least / len(pieces), high / len(pieces)))
        level = level * jnp.repeat(heights, shape[position] // blocks).reshape([-1 if axis == position else 1 for axis in range(len(shape))])
    return level


def gaussian(own_key, dims, deviation, most, pieces=(), kind=jnp.bfloat16):
    drawn = deviation * jax.random.normal(own_key, dims, jnp.float32)
    if pieces:
        drawn = drawn * levels(own_key, dims, pieces, -0.22, 0.18)
    return jnp.clip(drawn, -most, most).astype(kind)


def setup_inputs(seed: int = 0) -> dict:
    streams_of = jax.random.split(jax.random.key(seed), 12)
    return {
        "tokens": gaussian(streams_of[0], (MICRO, MB_TOK, D), 1.0, 6.0, ((1, 4), (2, 8))),
        "seq_lengths": draw_seq_lengths(jax.random.fold_in(streams_of[11], 71), 0),
        "out_cot": gaussian(streams_of[2], (MICRO, MB_TOK, D), 1.0, 6.0, ((1, 4), (2, 8))),
        "s4_vectors": draw_s4_vectors(jax.random.fold_in(streams_of[11], 71), 0),
        "s4_modes": draw_s4_modes(jax.random.fold_in(streams_of[11], 71), 0),
        "glu_weight": gaussian(streams_of[5], (LAYERS, D, 2, D), (D // 4) ** -0.5, 0.5, ((0, 4), (3, 8))),
        "glu_bias": gaussian(streams_of[6], (LAYERS, 2, D), 0.5, 3.0, ((0, 4), (2, 8)), jnp.float32),
        "ffn_vectors": draw_ffn_vectors(jax.random.fold_in(streams_of[11], 71), 0),
        "up_weight": gaussian(streams_of[8], (LAYERS, D, FF), D ** -0.5, 0.25, ((0, 4), (2, 8))),
        "up_bias": gaussian(streams_of[9], (LAYERS, FF), 0.5, 3.0, ((0, 4), (1, 8))),
        "down_weight": gaussian(streams_of[10], (LAYERS, FF, D), FF ** -0.5, 0.125, ((0, 4), (1, 8))),
    }


norm_eps = 1e-05
highest = lax.Precision.HIGHEST

@jax.custom_vjp
def low(v):
    return lax.optimization_barrier(v.astype(jnp.bfloat16)).astype(jnp.float32)

@jax.custom_vjp
def low_back(v):
    return v

def low_keep(v):
    return (low(v), None)

def low_pass(kept, grad):
    return (grad,)

def back_keep(v):
    return (v, None)

def back_low(kept, grad):
    return (low(grad),)
low.defvjp(low_keep, low_pass)
low_back.defvjp(back_keep, back_low)

def complex_mul(left_real, left_imag, right_real, right_imag):
    return (left_real * right_real - left_imag * right_imag, left_real * right_imag + left_imag * right_real)

def complex_div(left_real, left_imag, right_real, right_imag):
    modulus = right_real * right_real + right_imag * right_imag
    return ((left_real * right_real + left_imag * right_imag) / modulus, (left_imag * right_real - left_real * right_imag) / modulus)

def cauchy_spectrum(steps_log, mode_values, length):
    step_size = jnp.exp(steps_log)[:, None, None]
    angles = 2.0 * math.pi / length * jnp.arange(length, dtype=jnp.float32)
    cosine = jnp.cos(angles)
    sine_vals = jnp.sin(angles)
    decays = mode_values[0][:, :, None]
    rotate = mode_values[1][:, :, None]
    rank_real, rank_imag = (mode_values[2][:, :, None], mode_values[3][:, :, None])
    input_real, input_imag = (mode_values[4][:, :, None], mode_values[5][:, :, None])
    output_real, output_imag = (mode_values[6][:, :, None], mode_values[7][:, :, None])
    coeffs = [complex_mul(output_real, output_imag, input_real, input_imag), complex_mul(output_real, output_imag, rank_real, rank_imag), complex_mul(rank_real, -rank_imag, input_real, input_imag), (rank_real * rank_real + rank_imag * rank_imag, jnp.zeros_like(rank_real))]
    sums_real = [0.0, 0.0, 0.0, 0.0]
    sums_imag = [0.0, 0.0, 0.0, 0.0]
    for conj_sign in (1.0, -1.0):
        imag_rate = conj_sign * rotate
        den_real = 2.0 / step_size * (1.0 - cosine) + (1.0 + cosine) * decays - sine_vals * imag_rate
        den_imag = 2.0 / step_size * sine_vals - (1.0 + cosine) * imag_rate - sine_vals * decays
        for number in range(4):
            term_real, term_imag = complex_div(2.0 * coeffs[number][0], 2.0 * conj_sign * coeffs[number][1], den_real, den_imag)
            sums_real[number] = sums_real[number] + lax.optimization_barrier(jnp.sum(term_real, axis=1))
            sums_imag[number] = sums_imag[number] + lax.optimization_barrier(jnp.sum(term_imag, axis=1))
    half_real = (1.0 + cosine) / 2.0
    half_imag = -sine_vals / 2.0
    weight_real, weight_imag = complex_mul(half_real, half_imag, sums_real[3], sums_imag[3])
    cross_real, cross_imag = complex_mul(sums_real[1], sums_imag[1], sums_real[2], sums_imag[2])
    numer_real, numer_imag = complex_mul(half_real, half_imag, cross_real, cross_imag)
    fix_real, fix_imag = complex_div(numer_real, numer_imag, 1.0 + weight_real, weight_imag)
    return (sums_real[0] - fix_real, sums_imag[0] - fix_imag)

def layer_kernel(steps_log, mode_values, length, block_size):
    block_count = steps_log.shape[0] // block_size

    def one_block(operands):
        spec_real, spec_imag = cauchy_spectrum(operands[0], operands[1], length)
        return jnp.real(jnp.fft.ifft(lax.complex(spec_real, spec_imag), axis=-1))
    blocked_modes = jnp.moveaxis(mode_values.reshape(8, block_count, block_size, mode_values.shape[2]), 1, 0)
    kernels = lax.map(jax.checkpoint(one_block), (steps_log.reshape(block_count, block_size), blocked_modes))
    return kernels.reshape(block_count * block_size, length)

def norm_rows(values, gain_vec, bias_vec):
    average = lax.optimization_barrier(jnp.mean(values, axis=-1, keepdims=True))
    spread = lax.optimization_barrier(jnp.mean(values * values, axis=-1, keepdims=True)) - average * average
    return (values - average) * lax.rsqrt(spread + norm_eps) * gain_vec + bias_vec

def convolve(signal, kernel, seg_masks):
    length = signal.shape[0]
    kernel_spec = jnp.fft.rfft(kernel, n=2 * length, axis=-1)
    summed = jnp.zeros_like(signal)
    for segment in range(seg_masks.shape[0]):
        masked = (signal * seg_masks[segment][:, None]).T
        spectrum = jnp.fft.rfft(masked, n=2 * length, axis=-1) * kernel_spec
        inverse = jnp.fft.irfft(spectrum, n=2 * length, axis=-1)[:, :length]
        summed = summed + seg_masks[segment][:, None] * inverse.T
    return summed

def layer_apply(residual, kernel, vectors, glu_matrix, glu_offset, ffn_params, up_matrix, up_offset, down_matrix, seg_masks):
    model_width = residual.shape[1]
    normed = low(norm_rows(residual, vectors[0], vectors[1]))
    conv_out = convolve(normed, kernel, seg_masks) + vectors[3] * normed
    gated = low(jax.nn.gelu(conv_out))
    glu_pre = low_back(jnp.dot(gated, glu_matrix.reshape(model_width, 2 * model_width), precision=highest) + glu_offset.reshape(2 * model_width))
    residual_mid = residual + glu_pre[:, :model_width] * jax.nn.sigmoid(glu_pre[:, model_width:])
    ffn_in = low(norm_rows(residual_mid, ffn_params[0], ffn_params[1]))
    hidden = low_back(jnp.dot(ffn_in, up_matrix, precision=highest) + up_offset)
    active = low(jax.nn.gelu(hidden))
    branch = low_back(jnp.dot(active, down_matrix, precision=highest))
    return residual_mid + branch + ffn_params[2]

def reference(tokens, seq_lengths, out_cot, s4_vectors, s4_modes, glu_weight, glu_bias, ffn_vectors, up_weight, up_bias, down_weight):
    length = tokens.shape[1]
    ends = jnp.cumsum(seq_lengths, axis=1)
    begins = ends - seq_lengths
    positions = jnp.arange(length, dtype=jnp.int32)
    seg_masks = ((positions[None, None, :] >= begins[:, :, None]) & (positions[None, None, :] < ends[:, :, None])).astype(jnp.float32)

    def forward(inputs, vectors, modes, glu_matrix, glu_offset, ffn_params, up_matrix, up_offset, down_matrix, probes):
        block_size = math.gcd(D, 64)
        kernels = [layer_kernel(vectors[layer_idx, 2], modes[layer_idx], length, block_size) for layer_idx in range(LAYERS)]
        residuals = [inputs[micro_idx] for micro_idx in range(MICRO)]
        results = []
        for layer_idx in range(LAYERS):
            layer_rows = []
            for micro_idx in range(MICRO):
                entering = low_back(residuals[micro_idx] + probes[layer_idx, micro_idx])
                layer_out = low(layer_apply(entering, kernels[layer_idx], vectors[layer_idx], glu_matrix[layer_idx], glu_offset[layer_idx], ffn_params[layer_idx], up_matrix[layer_idx], up_offset[layer_idx], down_matrix[layer_idx], seg_masks[micro_idx]))
                residuals[micro_idx] = layer_out
                layer_rows.append(layer_out)
            results.append(jnp.stack(layer_rows))
        return jnp.stack(results)
    probes = jnp.zeros((LAYERS,) + tokens.shape, jnp.float32)
    primals = (tokens.astype(jnp.float32), s4_vectors, s4_modes, glu_weight.astype(jnp.float32), glu_bias, ffn_vectors, up_weight.astype(jnp.float32), up_bias.astype(jnp.float32), down_weight.astype(jnp.float32), probes)
    outputs, pullback = jax.vjp(forward, *primals)
    cot_seed = jnp.zeros_like(outputs).at[LAYERS - 1].set(out_cot.astype(jnp.float32))
    gradients = pullback(cot_seed)
    return (outputs.astype(jnp.bfloat16), gradients[9].astype(jnp.bfloat16), gradients[1], gradients[2], gradients[3], gradients[4], gradients[5], gradients[6], gradients[7], gradients[8])
```

```python
import math

import jax
import jax.numpy as jnp
import numpy as np
from jax import lax
from jax.experimental import pallas as pl
from jax.experimental.pallas import tpu as pltpu
from jax.sharding import PartitionSpec as P

norm_eps = 1e-05
highest = lax.Precision.HIGHEST
f32 = jnp.float32
bf16 = jnp.bfloat16
LANES = 128


def fourier_table(length, padded):
    half = length // 2
    freq = np.arange(padded, dtype=np.int64)[:, None]
    time = np.arange(length, dtype=np.int64)[None, :]
    angle = (freq * (2 * time + 1) % (2 * length)) * (np.pi / length)
    weight = np.where(freq <= half, np.where((freq == 0) | (freq == half), 1.0, 2.0), 0.0) / length
    table = np.concatenate([np.cos(angle) * weight, -np.sin(angle) * weight], axis=0)
    return table.astype(np.float32)


def half_angles(length, padded):
    angle = np.minimum(np.arange(padded), length // 2) * (np.pi / length)
    cosine = np.cos(angle)
    cosine[length // 2 :] = 0.0
    return cosine.astype(np.float32), np.sin(angle).astype(np.float32)


def kernel_of(log_step, modes, length, padded):
    cosine, sine = half_angles(length, padded)
    cosine, sine = jnp.asarray(cosine), jnp.asarray(sine)
    decay, rate = modes[0], modes[1]
    rank_r, rank_i, in_r, in_i, out_r, out_i = (modes[i] for i in range(2, 8))
    vals = [
        (out_r * in_r - out_i * in_i, out_r * in_i + out_i * in_r),
        (out_r * rank_r - out_i * rank_i, out_r * rank_i + out_i * rank_r),
        (rank_r * in_r + rank_i * in_i, rank_r * in_i - rank_i * in_r),
        (rank_r * rank_r + rank_i * rank_i, jnp.zeros_like(rank_r)),
    ]
    rise = (2.0 * jnp.exp(-log_step))[:, None] * sine[None, :]
    square = cosine * cosine
    den_r = (decay * decay + rate * rate)[:, :, None] * square - (rise * rise)[:, None, :]
    den_i = 2.0 * decay[:, :, None] * (cosine * rise)[:, None, :]
    inverse = 1.0 / (den_r * den_r + den_i * den_i)
    den = jnp.concatenate([den_r * inverse, den_i * inverse], axis=2)
    alpha = jnp.stack([decay * v_r - rate * v_i for v_r, v_i in vals], axis=1)
    beta = jnp.stack([v_r for v_r, v_i in vals], axis=1)
    sums = jnp.einsum(
        "hvn,hnj->hvj", jnp.concatenate([alpha, beta], axis=1), den, precision=highest
    )
    parts = []
    for v in range(4):
        a_u, a_w = sums[:, v, :padded], sums[:, v, padded:]
        b_u, b_w = sums[:, 4 + v, :padded], sums[:, 4 + v, padded:]
        parts.append((2.0 * (cosine * a_u + rise * b_w), 2.0 * (rise * b_u - cosine * a_w)))
    (m0r, m0i), (m1r, m1i), (m2r, m2i), (m3r, m3i) = parts
    top_r = cosine * (m1r * m2r - m1i * m2i)
    top_i = cosine * (m1r * m2i + m1i * m2r)
    low_r = 1.0 + cosine * m3r
    low_i = cosine * m3i
    size = 1.0 / (low_r * low_r + low_i * low_i)
    spec_r = m0r - (top_r * low_r + top_i * low_i) * size
    spec_i = m0i - (top_i * low_r - top_r * low_i) * size
    table = jnp.asarray(fourier_table(length, padded))
    return jnp.dot(jnp.concatenate([spec_r, spec_i], axis=1), table, precision=highest)


def shifted(x, by):
    size = x.shape[-1]
    by = by % size
    if by == 0:
        return x
    return pltpu.roll(x, by, x.ndim - 1)


def toeplitz_kernel(blocks, kern_ref, near_ref, far_ref):
    channels = kern_ref.shape[0]
    wide = kern_ref.shape[1]

    def step(h, carry):
        row = kern_ref[pl.ds(h, 1), :]
        full = jnp.broadcast_to(row, (LANES, wide))
        full = pltpu.roll(full, 0, 1, stride=1, stride_axis=0)
        low = full.astype(bf16)
        far_ref[h] = low[:, : blocks * LANES]
        for d in range(blocks):
            near_ref[h, d * LANES : (d + 1) * LANES, :] = low[:, d * LANES : (d + 1) * LANES]
        return carry

    lax.fori_loop(0, channels, step, 0)


def lag_kernel(blocks, x_ref, g_ref, out_ref):
    channels, groups = 16, 4
    stride = channels
    rows = 40
    wide = (blocks + 1) * LANES

    def step(h, carry):
        x = x_ref[pl.ds((blocks - 1) * groups * stride + h, rows, stride=stride), :]
        parts = [
            g_ref[pl.ds(d * groups * stride + h, rows, stride=stride), :] for d in range(blocks)
        ]
        g = jnp.concatenate(parts, axis=1)
        prod = lax.dot_general(
            x.astype(bf16), g.astype(bf16), (((0,), (0,)), ((), ())), preferred_element_type=f32
        )
        prod = jnp.concatenate([prod, jnp.zeros((LANES, LANES), f32)], axis=1)
        size = LANES // 2
        while size >= 8:
            prod = prod[:size] + shifted(prod[size:], wide - size)
            size //= 2
        row = prod[0:1]
        for a in range(1, 8):
            row = row + shifted(prod[a : a + 1], wide - a)
        out_ref[pl.ds(h, 1), :] = row
        return carry

    lax.fori_loop(0, channels, step, 0)


def gelu(x):
    return 0.5 * x * (1.0 + jnp.tanh(math.sqrt(2.0 / math.pi) * (x + 0.044715 * x * x * x)))


def gelu_slope(x):
    scale = math.sqrt(2.0 / math.pi)
    t = jnp.tanh(scale * (x + 0.044715 * x * x * x))
    return 0.5 * (1.0 + t) + 0.5 * x * (1.0 - t * t) * scale * (1.0 + 3.0 * 0.044715 * x * x)


def dot(a, b):
    return lax.dot_general(a, b, (((1,), (0,)), ((), ())), preferred_element_type=f32)


def dot_nt(a, b):
    return lax.dot_general(a, b, (((1,), (1,)), ((), ())), preferred_element_type=f32)


def dot_tn(a, b):
    return lax.dot_general(a, b, (((0,), (0,)), ((), ())), preferred_element_type=f32)


class Sizes:
    def __init__(self, sections, peers, groups, tok_rows, chan_width, model_width, hidden):
        self.sections, self.peers, self.groups = sections, peers, groups
        self.micros = 2
        self.segments = 2
        self.quarters = peers // self.micros
        self.tok = tok_rows // self.quarters
        self.rows = -(-self.tok // 16) * 16
        self.length = tok_rows * groups
        self.blocks = self.length // LANES
        self.width = model_width
        self.cw = chan_width
        self.hid = hidden
        self.members = peers * groups
        self.ch = model_width // self.members
        self.slots = self.quarters * groups
        self.gr = self.micros * self.segments
        self.stack = (2 * self.blocks) * self.gr * self.ch


def main_kernel(z, *refs):
    (tok_tx, cot_tx, vec_tx, glu_loc, up_loc, down_loc, near, far, skip, masks) = refs[:10]
    (hid_out, ig_out, dglu, dup, ddown, vec_out, xs, gs) = refs[10:18]
    (
        vec_all, glu_all, up_all, down_all, tok_rx, cot_rx, res, gtop,
        tx1, rx1, tx2, rx2, tx3, rx3, tx4, rx4,
        conv_out, ys, hat1_s, inv1_s, hat2_s, inv2_s, val_s, sig_s, hidden_s,
        gated_s, ffn_s, act_s, gh_s, gp_s, lay_s, res_tx, ig_s, ig_tx, vg_s,
        ga, fi, ac, bg, gh, gp, vrx, send, recv,
    ) = refs[18:]
    pipe = lax.axis_index("pipe")
    chan = lax.axis_index("chan")
    data = lax.axis_index("dp")
    me = chan * z.groups + data
    slot_me = (chan // z.quarters) * z.slots + data * z.quarters + lax.rem(chan, z.quarters)
    rows, width, tok = z.rows, z.width, z.tok
    lane = lax.broadcasted_iota(jnp.int32, (1, LANES), 1)
    first_half = lane < (LANES // 2)
    row_ok = lax.broadcasted_iota(jnp.int32, (rows, 1), 0) < tok

    def slot_of(p):
        c, d = p // z.groups, lax.rem(p, z.groups)
        return (c // z.quarters) * z.slots + d * z.quarters + lax.rem(c, z.quarters)

    def member(p):
        return {"pipe": pipe, "chan": p // z.groups, "dp": lax.rem(p, z.groups)}

    def remote(src, dst, phase, where):
        return pltpu.make_async_remote_copy(
            src_ref=src,
            dst_ref=dst,
            send_sem=send.at[phase],
            recv_sem=recv.at[phase],
            device_id=where,
            device_id_type=pl.DeviceIdType.MESH,
        )

    def wait_bytes(ref, sem):
        pltpu.make_async_copy(ref, ref, sem).wait()

    def to_peers(src_of, dst, phase):
        def step(k, carry):
            c = lax.rem(chan + k, z.peers)
            remote(src_of(c), dst.at[chan], phase, {"pipe": pipe, "chan": c, "dp": data}).start()
            return carry

        lax.fori_loop(1, z.peers, step, 0)
        pltpu.make_async_copy(src_of(chan), dst.at[chan], recv.at[phase]).start()

    def to_members(src_of, dst, slot, phase):
        def step(k, carry):
            p = lax.rem(me + k, z.members)
            remote(src_of(p), dst.at[slot], phase, member(p)).start()
            return carry

        lax.fori_loop(1, z.members, step, 0)
        pltpu.make_async_copy(src_of(me), dst.at[slot], recv.at[phase]).start()

    (VEC, GLU, UP, DOWN, TOK, COT, A1, A2, A3, A4, RES, GTOP, HID, IG, GA, FI, AC, BG, GH, GP, VG) = range(21)

    barrier = pltpu.get_barrier_semaphore()

    def greet(k, carry):
        p = lax.rem(me + k, z.members)
        pl.semaphore_signal(
            barrier, inc=1, device_id=member(p), device_id_type=pl.DeviceIdType.MESH
        )
        return carry

    lax.fori_loop(1, z.members, greet, 0)
    later = {"pipe": lax.rem(pipe + 1, z.sections), "chan": chan, "dp": data}
    earlier = {"pipe": lax.rem(pipe + z.sections - 1, z.sections), "chan": chan, "dp": data}
    for neighbour in (later, earlier):
        pl.semaphore_signal(
            barrier, inc=1, device_id=neighbour, device_id_type=pl.DeviceIdType.MESH
        )
    pl.semaphore_wait(barrier, z.members - 1 + 2)

    to_peers(lambda c: vec_tx, vec_all, VEC)

    @pl.when(pipe == 0)
    def _():
        to_peers(lambda c: tok_tx.at[c], tok_rx, TOK)

    @pl.when(pipe == z.sections - 1)
    def _():
        to_peers(lambda c: cot_tx.at[c], cot_rx, COT)

    to_peers(lambda c: glu_loc, glu_all, GLU)
    to_peers(lambda c: up_loc, up_all, UP)
    to_peers(lambda c: down_loc, down_all, DOWN)

    pad_rows = (z.blocks - 1) * z.gr * z.ch
    data_rows = z.blocks * z.gr * z.ch
    xs[0:pad_rows, :] = jnp.zeros((pad_rows, LANES), f32)
    xs[pad_rows + data_rows : z.stack, :] = jnp.zeros(
        (z.stack - pad_rows - data_rows, LANES), f32
    )
    gs[data_rows : z.stack, :] = jnp.zeros((z.stack - data_rows, LANES), f32)

    wait_bytes(vec_all, recv.at[VEC])

    def full_row(r):
        tiles = [
            jnp.where(first_half, vec_all[2 * j, r : r + 1, :], vec_all[2 * j + 1, r : r + 1, :])
            for j in range(z.peers // 2)
        ]
        return jnp.concatenate(tiles, axis=1)

    gain1, bias1, gain2, bias2, out_bias = (full_row(r) for r in range(5))

    def norm_stats(v):
        mean = jnp.sum(v, axis=1, keepdims=True) * (1.0 / width)
        spread = jnp.sum(v * v, axis=1, keepdims=True) * (1.0 / width) - mean * mean
        inv = lax.rsqrt(spread + norm_eps)
        return (v - mean) * inv, inv

    def norm_back(e, hat, inv, gain):
        dh = e * gain
        first = jnp.sum(dh, axis=1, keepdims=True) * (1.0 / width)
        second = jnp.sum(dh * hat, axis=1, keepdims=True) * (1.0 / width)
        return inv * (dh - first - hat * second)

    def turn_out(v, ref):
        tall = jnp.concatenate([v, jnp.zeros((LANES - rows, width), f32)], axis=0)
        ref[...] = tall.T.astype(bf16).reshape(z.members, z.ch, LANES)

    def turn_in(ref):
        return ref[...].reshape(width, LANES).astype(f32).T[:rows]

    def lane_tiles(ref, m):
        tiles = []
        for i in range(z.blocks):
            lo, hi = i * LANES, (i + 1) * LANES
            tile = None
            for k in range(lo // tok, -(-hi // tok)):
                piece = shifted(ref[m * z.slots + k].astype(f32), k * tok - lo)
                first = max(0, k * tok - lo)
                if tile is None:
                    tile = piece
                else:
                    tile = jnp.where(lane >= first, piece, tile)
            tiles.append(tile)
        return tiles

    def lane_pieces(tiles, m, ref):
        for k in range(z.slots):
            i, off = divmod(k * tok, LANES)
            piece = shifted(tiles[i], LANES - off)
            if off + tok > LANES:
                piece = jnp.where(lane < LANES - off, piece, shifted(tiles[i + 1], LANES - off))
            ref[m * z.slots + k] = piece.astype(bf16)

    def row_at(i, g):
        return (i * z.gr + g) * z.ch

    def masked_store(ref, base, m, i, tile):
        for q in range(z.segments):
            g = m * z.segments + q
            at = base + row_at(i, g)
            ref[at : at + z.ch, :] = tile * masks[i * z.gr + g : i * z.gr + g + 1, :]

    def masked_sum(m, i):
        total = None
        for q in range(z.segments):
            g = m * z.segments + q
            at = row_at(i, g)
            part = ys[at : at + z.ch, :] * masks[i * z.gr + g : i * z.gr + g + 1, :]
            total = part if total is None else total + part
        return total

    conv_rows = -(-(z.blocks * z.gr) // 8) * 8

    @pl.when(pipe == 0)
    def _():
        wait_bytes(tok_rx, recv.at[TOK])
        for j in range(z.peers // 2):
            res[:, j * LANES : (j + 1) * LANES] = jnp.where(
                first_half, tok_rx[2 * j].astype(f32), tok_rx[2 * j + 1].astype(f32)
            ).astype(bf16)

    @pl.when(pipe > 0)
    def _():
        wait_bytes(res, recv.at[RES])

    hat1, inv1 = norm_stats(res[...].astype(f32))
    hat1_s[...] = hat1
    inv1_s[...] = jnp.broadcast_to(inv1, (rows, LANES))
    turn_out(hat1 * gain1 + bias1, tx1)
    to_members(lambda p: tx1.at[p], rx1, slot_me, A1)
    wait_bytes(rx1, recv.at[A1])
    for m in range(z.micros):
        for i, tile in enumerate(lane_tiles(rx1, m)):
            masked_store(xs, pad_rows, m, i, tile)

    def conv_step(h, carry):
        parts = [
            xs[pl.ds((z.blocks - 1 - d) * z.gr * z.ch + h, conv_rows, stride=z.ch), :]
            for d in range(z.blocks)
        ]
        windows = jnp.concatenate(parts, axis=1).astype(bf16)
        ys[pl.ds(h, conv_rows, stride=z.ch), :] = dot(windows, near[h])
        return carry

    lax.fori_loop(0, z.ch, conv_step, 0)
    for m in range(z.micros):
        tiles = []
        for i in range(z.blocks):
            own = None
            for q in range(z.segments):
                at = pad_rows + row_at(i, m * z.segments + q)
                own = xs[at : at + z.ch, :] if own is None else own + xs[at : at + z.ch, :]
            tile = masked_sum(m, i) + skip[...] * own
            conv_out[m * z.blocks + i] = tile
            tiles.append(gelu(tile))
        lane_pieces(tiles, m, tx2)
    to_members(lambda p: tx2.at[slot_of(p)], rx2, me, A2)
    wait_bytes(rx2, recv.at[A2])
    gated_s[...] = turn_in(rx2).astype(bf16)
    wait_bytes(glu_all, recv.at[GLU])
    gated = gated_s[...]
    values, gates = [], []
    for j in range(z.peers // 2):
        even = dot(gated, glu_all[2 * j]) + vec_all[2 * j, 5:6, :]
        odd = dot(gated, glu_all[2 * j + 1]) + vec_all[2 * j + 1, 5:6, :]
        values.append(jnp.where(first_half, even, odd))
        gates.append(shifted(jnp.where(first_half, odd, even), LANES // 2))
    value = jnp.concatenate(values, axis=1)
    sig = jax.nn.sigmoid(jnp.concatenate(gates, axis=1))
    val_s[...] = value
    sig_s[...] = sig
    mid = res[...].astype(f32) + value * sig
    hat2, inv2 = norm_stats(mid)
    hat2_s[...] = hat2
    inv2_s[...] = jnp.broadcast_to(inv2, (rows, LANES))
    ffn_s[...] = (hat2 * gain2 + bias2).astype(bf16)
    wait_bytes(up_all, recv.at[UP])
    wait_bytes(down_all, recv.at[DOWN])
    ffn_in = ffn_s[...]
    total = mid + out_bias
    per = z.hid // LANES
    for c in range(z.peers):
        offset = jnp.concatenate([vec_all[c, 6 + r : 7 + r, :] for r in range(per)], axis=1)
        hidden = dot(ffn_in, up_all[c]) + offset
        hidden_s[c] = hidden
        active = gelu(hidden).astype(bf16)
        act_s[c] = active
        total = total + dot(active, down_all[c])
    layer_out = jnp.where(row_ok, total, 0.0).astype(bf16)
    res_tx[...] = layer_out

    @pl.when(pipe < z.sections - 1)
    def _():
        remote(res_tx, res, RES, later).start()

    for j in range(z.peers // 2):
        lay_s[j] = layer_out[:, j * LANES : (j + 1) * LANES]
    to_peers(lambda c: lay_s.at[c // 2], hid_out, HID)
    to_peers(lambda c: gated_s, ga, GA)
    to_peers(lambda c: ffn_s, fi, FI)
    to_peers(lambda c: act_s.at[c], ac, AC)

    @pl.when(pipe == z.sections - 1)
    def _():
        wait_bytes(cot_rx, recv.at[COT])
        for j in range(z.peers // 2):
            gtop[:, j * LANES : (j + 1) * LANES] = jnp.where(
                first_half, cot_rx[2 * j].astype(f32), cot_rx[2 * j + 1].astype(f32)
            ).astype(bf16)

    @pl.when(pipe < z.sections - 1)
    def _():
        wait_bytes(gtop, recv.at[GTOP])

    grad_low = gtop[...]
    grad_top = grad_low.astype(f32)
    grad_ffn = None
    for c in range(z.peers):
        grad_active = dot_nt(grad_low, down_all[c])
        grad_hidden = (grad_active * gelu_slope(hidden_s[c])).astype(bf16)
        gh_s[c] = grad_hidden
        part = dot_nt(grad_hidden, up_all[c])
        grad_ffn = part if grad_ffn is None else grad_ffn + part
    hat2 = hat2_s[...]
    grad_mid = grad_top + norm_back(grad_ffn, hat2, inv2_s[:, 0:1], gain2)
    sig = sig_s[...]
    grad_value = grad_mid * sig
    grad_gate = grad_value * val_s[...] * (1.0 - sig)
    grad_gated = None
    for j in range(z.peers // 2):
        gv = grad_value[:, j * LANES : (j + 1) * LANES]
        gg = shifted(grad_gate[:, j * LANES : (j + 1) * LANES], LANES // 2)
        pair = (jnp.where(first_half, gv, gg), jnp.where(first_half, gg, gv))
        for half in range(2):
            low = pair[half].astype(bf16)
            gp_s[2 * j + half] = low
            part = dot_nt(low, glu_all[2 * j + half])
            grad_gated = part if grad_gated is None else grad_gated + part
    turn_out(grad_gated, tx3)
    to_members(lambda p: tx3.at[p], rx3, slot_me, A3)
    to_peers(lambda c: gtop, bg, BG)
    to_peers(lambda c: gh_s.at[c], gh, GH)
    to_peers(lambda c: gp_s.at[c], gp, GP)
    wait_bytes(rx3, recv.at[A3])
    for m in range(z.micros):
        for i, tile in enumerate(lane_tiles(rx3, m)):
            masked_store(gs, 0, m, i, tile * gelu_slope(conv_out[m * z.blocks + i]))

    def back_step(h, carry):
        parts = [
            gs[pl.ds(d * z.gr * z.ch + h, conv_rows, stride=z.ch), :] for d in range(z.blocks)
        ]
        windows = jnp.concatenate(parts, axis=1).astype(bf16)
        ys[pl.ds(h, conv_rows, stride=z.ch), :] = dot_nt(windows, far[h])
        return carry

    lax.fori_loop(0, z.ch, back_step, 0)
    for m in range(z.micros):
        tiles = []
        for i in range(z.blocks):
            own = None
            for q in range(z.segments):
                at = row_at(i, m * z.segments + q)
                own = gs[at : at + z.ch, :] if own is None else own + gs[at : at + z.ch, :]
            tiles.append(masked_sum(m, i) + skip[...] * own)
        lane_pieces(tiles, m, tx4)
    to_members(lambda p: tx4.at[slot_of(p)], rx4, me, A4)
    wait_bytes(rx4, recv.at[A4])
    grad_conv_in = jnp.where(row_ok, turn_in(rx4), 0.0)
    hat1 = hat1_s[...]
    grad_res = grad_mid + norm_back(grad_conv_in, hat1, inv1_s[:, 0:1], gain1)
    grad_res_low = grad_res.astype(bf16)
    ig_tx[...] = grad_res_low

    @pl.when(pipe > 0)
    def _():
        remote(ig_tx, gtop, GTOP, earlier).start()

    for j in range(z.peers // 2):
        ig_s[j] = grad_res_low[:, j * LANES : (j + 1) * LANES]
    to_peers(lambda c: ig_s.at[c // 2], ig_out, IG)

    rows_of = [
        jnp.sum(grad_conv_in * hat1, axis=0, keepdims=True),
        jnp.sum(grad_conv_in, axis=0, keepdims=True),
        jnp.sum(grad_ffn * hat2, axis=0, keepdims=True),
        jnp.sum(grad_ffn, axis=0, keepdims=True),
        jnp.sum(grad_top, axis=0, keepdims=True),
    ]
    for c in range(z.peers):
        j = c // 2
        for r, row in enumerate(rows_of):
            vg_s[c, r : r + 1, :] = row[:, j * LANES : (j + 1) * LANES]
        vg_s[c, 5:6, :] = jnp.sum(gp_s[c].astype(f32), axis=0, keepdims=True)
        up_row = jnp.sum(gh_s[c].astype(f32), axis=0, keepdims=True)
        for r in range(per):
            vg_s[c, 6 + r : 7 + r, :] = up_row[:, r * LANES : (r + 1) * LANES]
    to_peers(lambda c: vg_s.at[c], vrx, VG)
    wait_bytes(ga, recv.at[GA])
    wait_bytes(gp, recv.at[GP])
    many = z.peers * rows
    dglu[...] = dot_tn(ga[...].reshape(many, width), gp[...].reshape(many, 2 * z.cw))
    wait_bytes(fi, recv.at[FI])
    wait_bytes(gh, recv.at[GH])
    dup[...] = dot_tn(fi[...].reshape(many, width), gh[...].reshape(many, z.hid))
    wait_bytes(ac, recv.at[AC])
    wait_bytes(bg, recv.at[BG])
    ddown[...] = dot_tn(ac[...].reshape(many, z.hid), bg[...].reshape(many, width))
    wait_bytes(vrx, recv.at[VG])
    summed = vrx[0]
    for c in range(1, z.peers):
        summed = summed + vrx[c]
    vec_out[...] = summed
    wait_bytes(hid_out, recv.at[HID])
    wait_bytes(ig_out, recv.at[IG])

    for ref, phase in (
        (vec_all, VEC), (glu_all, GLU), (up_all, UP), (down_all, DOWN), (hid_out, HID),
        (ig_out, IG), (ga, GA), (fi, FI), (ac, AC), (bg, BG), (gh, GH), (gp, GP), (vrx, VG),
    ):
        wait_bytes(ref.at[pl.ds(0, z.peers - 1)], send.at[phase])
    for ref, phase in ((rx1, A1), (rx2, A2), (rx3, A3), (rx4, A4)):
        wait_bytes(ref.at[pl.ds(0, z.members - 1)], send.at[phase])

    @pl.when(pipe == 0)
    def _():
        wait_bytes(tok_rx.at[pl.ds(0, z.peers - 1)], send.at[TOK])

    @pl.when(pipe == z.sections - 1)
    def _():
        wait_bytes(cot_rx.at[pl.ds(0, z.peers - 1)], send.at[COT])

    @pl.when(pipe < z.sections - 1)
    def _():
        wait_bytes(res_tx, send.at[RES])

    @pl.when(pipe > 0)
    def _():
        wait_bytes(ig_tx, send.at[GTOP])


def body(
    tokens,
    seq_lengths,
    out_cot,
    s4_vectors,
    s4_modes,
    glu_weight,
    glu_bias,
    ffn_vectors,
    up_weight,
    up_bias,
    down_weight,
):
    chan = lax.axis_index("chan")
    data = lax.axis_index("dp")
    micros, tok_rows, chan_width = tokens.shape
    width = glu_weight.shape[1]
    hidden = up_weight.shape[2]
    z = Sizes(
        lax.axis_size("pipe"), lax.axis_size("chan"), lax.axis_size("dp"),
        tok_rows, chan_width, width, hidden,
    )
    odd = lax.rem(chan, 2) == 1
    length = z.length
    padded = -(-(length // 2 + 1) // LANES) * LANES
    vectors = s4_vectors[0]
    own_vectors = lax.dynamic_slice_in_dim(vectors, data * z.ch, z.ch, 1)
    own_modes = lax.dynamic_slice_in_dim(s4_modes[0], data * z.ch, z.ch, 1)

    def spectrum_of(log_step, modes):
        return kernel_of(log_step, modes, length, padded)

    kern, pull = jax.vjp(spectrum_of, own_vectors[2], own_modes)
    kern_wide = jnp.pad(kern, ((0, 0), (0, LANES)))
    near, far = pl.pallas_call(
        lambda *refs: toeplitz_kernel(z.blocks, *refs),
        out_shape=(
            jax.ShapeDtypeStruct((z.ch, length, LANES), bf16),
            jax.ShapeDtypeStruct((z.ch, LANES, length), bf16),
        ),
        in_specs=[pl.BlockSpec(memory_space=pltpu.VMEM)],
        out_specs=[pl.BlockSpec(memory_space=pltpu.VMEM)] * 2,
        compiler_params=pltpu.CompilerParams(vmem_limit_bytes=40 * 2**20),
        name="toeplitz",
    )(kern_wide)

    def blocks_of(x):
        x = x.reshape(z.peers, z.tok, chan_width)
        x = jnp.pad(x, ((0, 0), (0, z.rows - z.tok), (0, 0)))
        return jnp.concatenate([x, x], axis=2)

    def swap(value, gate):
        return jnp.where(
            odd, jnp.concatenate([gate, value], -1), jnp.concatenate([value, gate], -1)
        )

    ffn = ffn_vectors[0]
    twice = jnp.stack([vectors[0], vectors[1], ffn[0], ffn[1], ffn[2]])
    vec = jnp.concatenate(
        [
            jnp.concatenate([twice, twice], axis=1),
            swap(glu_bias[0, 0], glu_bias[0, 1])[None],
            up_bias[0].astype(f32).reshape(hidden // LANES, LANES),
        ],
        axis=0,
    )
    glu_loc = swap(glu_weight[0, :, 0, :], glu_weight[0, :, 1, :])
    ends = jnp.cumsum(seq_lengths, axis=1)
    begins = ends - seq_lengths
    positions = jnp.arange(length, dtype=jnp.int32)
    masks = (
        (positions[None, None, :] >= begins[:, :, None])
        & (positions[None, None, :] < ends[:, :, None])
    ).astype(f32)
    masks = masks.reshape(z.gr, z.blocks, LANES).transpose(1, 0, 2).reshape(-1, LANES)
    skip = jnp.broadcast_to(own_vectors[3][:, None], (z.ch, LANES))

    vmem = pl.BlockSpec(memory_space=pltpu.VMEM)
    n, r, w = z.peers, z.rows, width

    def s(shape, kind=bf16):
        return jax.ShapeDtypeStruct(shape, kind)

    def v(shape, kind=bf16):
        return pltpu.VMEM(shape, kind)

    exchange = (z.members, z.ch, LANES)
    hid_blocks, ig_blocks, dglu, dup, ddown, vec_sum, xs, gs = pl.pallas_call(
        lambda *refs: main_kernel(z, *refs),
        out_shape=(
            s((n, r, LANES)), s((n, r, LANES)), s((w, 2 * chan_width), f32), s((w, hidden), f32),
            s((hidden, w), f32), s((8, LANES), f32), s((z.stack, LANES), f32),
            s((z.stack, LANES), f32),
        ),
        in_specs=[vmem] * 10,
        out_specs=[vmem] * 8,
        scratch_shapes=[
            v((n, 8, LANES), f32), v((n, w, 2 * chan_width)), v((n, w, hidden)),
            v((n, hidden, w)), v((n, r, LANES)), v((n, r, LANES)), v((r, w)), v((r, w)),
        ]
        + [v(exchange)] * 8
        + [
            v((z.micros * z.blocks, z.ch, LANES), f32),
            v((-(-(z.blocks * z.gr) // 8) * 8 * z.ch, LANES), f32),
            v((r, w), f32), v((r, LANES), f32), v((r, w), f32), v((r, LANES), f32),
            v((r, w), f32), v((r, w), f32), v((n, r, hidden), f32),
            v((r, w)), v((r, w)), v((n, r, hidden)), v((n, r, hidden)), v((n, r, LANES)),
            v((n // 2, r, LANES)), v((r, w)), v((n // 2, r, LANES)), v((r, w)),
            v((n, 8, LANES), f32),
            v((n, r, w)), v((n, r, w)), v((n, r, hidden)), v((n, r, w)), v((n, r, hidden)),
            v((n, r, LANES)), v((n, 8, LANES), f32),
            pltpu.SemaphoreType.DMA((21,)), pltpu.SemaphoreType.DMA((21,)),
        ],
        compiler_params=pltpu.CompilerParams(
            collective_id=0, has_side_effects=True, vmem_limit_bytes=60 * 2**20
        ),
        name="layers",
    )(
        blocks_of(tokens), blocks_of(out_cot), vec, glu_loc, up_weight[0], down_weight[0],
        near, far, skip, masks,
    )

    lags = pl.pallas_call(
        lambda *refs: lag_kernel(z.blocks, *refs),
        out_shape=s((z.ch, (z.blocks + 1) * LANES), f32),
        in_specs=[vmem] * 2,
        out_specs=vmem,
        name="lags",
    )(xs, gs)
    grad_kern = lags[:, :length]
    step_grad, mode_grad = pull(grad_kern)

    def whole(blocks):
        x = jnp.where(odd, blocks[:, : z.tok, chan_width:], blocks[:, : z.tok, :chan_width])
        return x.reshape(1, micros, tok_rows, chan_width)

    reduced = lax.psum((dglu, dup, ddown, vec_sum), "dp")
    red_glu, red_up, red_down, red_vec = reduced
    extra = jnp.stack([step_grad, grad_kern[:, 0]])
    packed = jnp.concatenate([mode_grad.transpose(1, 0, 2).reshape(z.ch, -1), extra.T], axis=1)
    gathered = lax.all_gather(packed, "dp", axis=0, tiled=True)
    split = gathered.shape[1] - 2
    mode_full = gathered[:, :split].reshape(chan_width, 8, -1).transpose(1, 0, 2)
    first, second = red_vec[:, :chan_width], red_vec[:, chan_width:]
    mine = jnp.where(odd, second, first)
    other = jnp.where(odd, first, second)
    grad_vectors = jnp.stack([mine[0], mine[1], gathered[:, split], gathered[:, split + 1]])[None]
    glu_first, glu_second = red_glu[:, :chan_width], red_glu[:, chan_width:]
    grad_glu = jnp.stack(
        [jnp.where(odd, glu_second, glu_first), jnp.where(odd, glu_first, glu_second)], axis=1
    )
    return (
        whole(hid_blocks),
        whole(ig_blocks),
        grad_vectors,
        mode_full[None],
        grad_glu[None],
        jnp.stack([mine[5], other[5]])[None],
        mine[2:5][None],
        red_up[None],
        red_vec[6:].reshape(1, hidden),
        red_down[None],
    )


def solution(mesh):
    placed = (
        P(None, "dp", "chan"),
        P(),
        P(None, "dp", "chan"),
        P("pipe", None, "chan"),
        P("pipe", None, "chan", None),
        P("pipe", None, None, "chan"),
        P("pipe", None, "chan"),
        P("pipe", None, "chan"),
        P("pipe", None, "chan"),
        P("pipe", "chan"),
        P("pipe", "chan", None),
    )
    return jax.shard_map(
        body,
        mesh=mesh,
        in_specs=placed,
        out_specs=(
            P("pipe", None, "dp", "chan"),
            P("pipe", None, "dp", "chan"),
            P("pipe", None, "chan"),
            P("pipe", None, "chan", None),
            P("pipe", None, None, "chan"),
            P("pipe", None, "chan"),
            P("pipe", None, "chan"),
            P("pipe", None, "chan"),
            P("pipe", "chan"),
            P("pipe", "chan", None),
        ),
        check_vma=False,
    )
```

```python
import math

import jax
import jax.numpy as jnp
import ml_dtypes
import numpy as np
from jax import lax
from jax.experimental import pallas as pl
from jax.experimental.pallas import tpu as pltpu
from jax.sharding import PartitionSpec as P

norm_eps = 1e-05
f32 = jnp.float32
bf16 = jnp.bfloat16
LANES = 128


def fourier_table(length, padded):
    half = length // 2
    freq = np.arange(padded, dtype=np.int64)[:, None]
    time = np.arange(length, dtype=np.int64)[None, :]
    angle = (freq * (2 * time + 1) % (2 * length)) * (np.pi / length)
    weight = np.where(freq <= half, np.where((freq == 0) | (freq == half), 1.0, 2.0), 0.0) / length
    table = np.concatenate([np.cos(angle) * weight, -np.sin(angle) * weight], axis=0)
    return table.astype(np.float32)


def half_angles(length, padded):
    angle = np.minimum(np.arange(padded), length // 2) * (np.pi / length)
    rows = np.zeros((8, padded), np.float32)
    rows[0] = np.where(np.arange(padded) < length // 2, np.cos(angle), 0.0)
    rows[1] = np.sin(angle)
    return rows


def shifted(x, by):
    size = x.shape[-1]
    by = by % size
    if by == 0:
        return x
    return pltpu.roll(x, by, x.ndim - 1)


def gelu(x):
    return 0.5 * x * (1.0 + jnp.tanh(math.sqrt(2.0 / math.pi) * (x + 0.044715 * x * x * x)))


def gelu_slope(x):
    scale = math.sqrt(2.0 / math.pi)
    t = jnp.tanh(scale * (x + 0.044715 * x * x * x))
    return 0.5 * (1.0 + t) + 0.5 * x * (1.0 - t * t) * scale * (1.0 + 3.0 * 0.044715 * x * x)


def dot(a, b):
    return lax.dot_general(a, b, (((1,), (0,)), ((), ())), preferred_element_type=f32)


def dot_nt(a, b):
    return lax.dot_general(a, b, (((1,), (1,)), ((), ())), preferred_element_type=f32)


def dot_tn(a, b):
    return lax.dot_general(a, b, (((0,), (0,)), ((), ())), preferred_element_type=f32)


class Sizes:
    def __init__(self, sections, peers, groups, tok_rows, chan_width, model_width, hidden):
        self.sections, self.peers, self.groups = sections, peers, groups
        self.micros = 2
        self.segments = 2
        self.quarters = peers // self.micros
        self.tok = tok_rows // self.quarters
        self.rows = -(-self.tok // 16) * 16
        self.length = tok_rows * groups
        self.blocks = self.length // LANES
        self.width = model_width
        self.cw = chan_width
        self.hid = hidden
        self.members = peers * groups
        self.ch = model_width // self.members
        self.slots = self.quarters * groups
        self.gr = self.micros * self.segments
        self.stack = (2 * self.blocks) * self.gr * self.ch


def main_kernel(z, *refs):
    (
        lengths, tokens, out_cot, vectors, modes, glu_loc, glu_bias, ffn_vec, up_loc, up_bias,
        down_loc, angles, table_in,
    ) = refs[:13]
    (
        hid_out, ig_out, vec_out, modes_out, dglu, glub_out, ffn_out, dup, upb_out, ddown,
    ) = refs[13:23]
    (
        tok_tx, cot_tx, vec_tx, near, far, skip, masks, hid_rx, ig_rx, xs, gs,
        table, turn_s, cols, rise_s, sums_s, gsum_s, slope_s, kern_s, lag_s, gcol_s, gstep_s,
        modes_tx, modes_rx, pglu, pup, pdown, kglu, kup, kdown, sglu, sup, sdown,
        lglu, lup, ldown,
        vec_all, glu_all, up_all, down_all, tok_rx, cot_rx, res, gtop,
        tx1, rx1, tx2, rx2, tx3, rx3, tx4, rx4,
        conv_out, ys, hat1_s, inv1_s, hat2_s, inv2_s, val_s, sig_s, hidden_s,
        gated_s, ffn_s, act_s, gh_s, gp_s, lay_s, res_tx, ig_s, ig_tx, vg_s,
        ga, fi, ac, bg, gh, gp, vrx, send, recv,
    ) = refs[23:]
    pipe = lax.axis_index("pipe")
    chan = lax.axis_index("chan")
    data = lax.axis_index("dp")
    me = chan * z.groups + data
    slot_me = (chan // z.quarters) * z.slots + data * z.quarters + lax.rem(chan, z.quarters)
    rows, width, tok = z.rows, z.width, z.tok
    lane = lax.broadcasted_iota(jnp.int32, (1, LANES), 1)
    first_half = lane < (LANES // 2)
    row_ok = lax.broadcasted_iota(jnp.int32, (rows, 1), 0) < tok

    def slot_of(p):
        c, d = p // z.groups, lax.rem(p, z.groups)
        return (c // z.quarters) * z.slots + d * z.quarters + lax.rem(c, z.quarters)

    def member(p):
        return {"pipe": pipe, "chan": p // z.groups, "dp": lax.rem(p, z.groups)}

    def remote(src, dst, phase, where):
        return pltpu.make_async_remote_copy(
            src_ref=src,
            dst_ref=dst,
            send_sem=send.at[phase],
            recv_sem=recv.at[phase],
            device_id=where,
            device_id_type=pl.DeviceIdType.MESH,
        )

    def wait_bytes(ref, sem):
        pltpu.make_async_copy(ref, ref, sem).wait()

    def to_peers(src_of, dst, phase):
        def step(k, carry):
            c = lax.rem(chan + k, z.peers)
            remote(src_of(c), dst.at[chan], phase, {"pipe": pipe, "chan": c, "dp": data}).start()
            return carry

        lax.fori_loop(1, z.peers, step, 0)
        pltpu.make_async_copy(src_of(chan), dst.at[chan], recv.at[phase]).start()

    def to_members(src_of, dst, slot, phase):
        def step(k, carry):
            p = lax.rem(me + k, z.members)
            remote(src_of(p), dst.at[slot], phase, member(p)).start()
            return carry

        lax.fori_loop(1, z.members, step, 0)
        pltpu.make_async_copy(src_of(me), dst.at[slot], recv.at[phase]).start()

    (VEC, TOK, COT, A1, A2, A3, A4, RES, GTOP, HID, IG, GA, FI, AC, BG, GH, GP, VG) = range(18)
    GLU, UP, DOWN = 18, 24, 30
    TABLE, MODES, GRADS = 36, 37, 38

    high, deep = chan // z.quarters, lax.rem(chan, z.quarters)
    low, core = data // 2, lax.rem(data, 2)
    weight_of = {GLU: (glu_loc, glu_all), UP: (up_loc, up_all), DOWN: (down_loc, down_all)}
    own_side, far_side = high * z.quarters, (1 - high) * z.quarters

    def place(c, d):
        return {"pipe": pipe, "chan": c, "dp": d}

    def weights_ring(t):
        loc, whole = weight_of[t]
        half = loc.shape[0] // 2
        part = pl.ds(pl.multiple_of(core * half, half), half)
        for k in range(1, z.quarters):
            c = own_side + lax.rem(deep + k, z.quarters)
            remote(loc.at[part], whole.at[chan, part], t, place(c, data)).start()
        pltpu.make_async_copy(loc, whole.at[chan], recv.at[t + 5]).start()

    def weights_across(t):
        loc, whole = weight_of[t]
        half = loc.shape[0] // 2
        fourth = half // 2
        wait_bytes(whole.at[pl.ds(0, z.quarters - 1), pl.ds(0, half)], recv.at[t])
        wait_bytes(loc, recv.at[t + 5])
        quarter = pl.ds(pl.multiple_of(core * half + low * fourth, fourth), fourth)
        piece = whole.at[pl.ds(own_side, z.quarters), quarter]
        remote(piece, piece, t + 1, place(far_side + deep, (1 - low) * 2 + core)).start()
        part = pl.ds(pl.multiple_of(core * half, half), half)
        for k in range(1, z.quarters):
            piece = whole.at[own_side + lax.rem(deep + k, z.quarters), part]
            remote(piece, piece, t + 3, place(chan, low * 2 + 1 - core)).start()

    def weights_beside(t):
        loc, whole = weight_of[t]
        half = loc.shape[0] // 2
        fourth = half // 2
        wait_bytes(whole.at[pl.ds(0, z.quarters), pl.ds(0, fourth)], recv.at[t + 1])
        quarter = pl.ds(pl.multiple_of(core * half + (1 - low) * fourth, fourth), fourth)
        piece = whole.at[pl.ds(far_side, z.quarters), quarter]
        remote(piece, piece, t + 2, place(chan, (1 - low) * 2 + core)).start()

    def weights_core(t):
        loc, whole = weight_of[t]
        half = loc.shape[0] // 2
        fourth = half // 2
        wait_bytes(whole.at[pl.ds(0, z.quarters), pl.ds(0, fourth)], recv.at[t + 2])
        part = pl.ds(pl.multiple_of(core * half, half), half)
        piece = whole.at[pl.ds(far_side, z.quarters), part]
        remote(piece, piece, t + 4, place(chan, low * 2 + 1 - core)).start()

    def weights_here(t):
        loc, whole = weight_of[t]
        half = loc.shape[0] // 2
        wait_bytes(whole.at[pl.ds(0, z.quarters - 1), pl.ds(0, half)], recv.at[t + 3])
        wait_bytes(whole.at[pl.ds(0, z.quarters), pl.ds(0, half)], recv.at[t + 4])

    def weights_sent(t):
        loc, whole = weight_of[t]
        half = loc.shape[0] // 2
        for stage, count, size in (
            (0, z.quarters - 1, half), (1, z.quarters, half // 2), (2, z.quarters, half // 2),
            (3, z.quarters - 1, half), (4, z.quarters, half),
        ):
            wait_bytes(whole.at[pl.ds(0, count), pl.ds(0, size)], send.at[t + stage])

    barrier = pltpu.get_barrier_semaphore()

    def greet(k, carry):
        p = lax.rem(me + k, z.members)
        pl.semaphore_signal(
            barrier, inc=1, device_id=member(p), device_id_type=pl.DeviceIdType.MESH
        )
        return carry

    lax.fori_loop(1, z.members, greet, 0)
    later = {"pipe": lax.rem(pipe + 1, z.sections), "chan": chan, "dp": data}
    earlier = {"pipe": lax.rem(pipe + z.sections - 1, z.sections), "chan": chan, "dp": data}
    for neighbour in (later, earlier):
        pl.semaphore_signal(
            barrier, inc=1, device_id=neighbour, device_id_type=pl.DeviceIdType.MESH
        )
    pltpu.make_async_copy(table_in, table, recv.at[TABLE]).start()
    odd = lax.rem(chan, 2)

    def fill_blocks(source, target):
        for m in range(z.micros):
            x = source[m].astype(f32)
            x = jnp.concatenate([x, x], axis=1)
            for q in range(z.quarters):
                block = x[q * tok : (q + 1) * tok]
                block = jnp.concatenate([block, jnp.zeros((rows - tok, LANES), f32)], axis=0)
                target[m * z.quarters + q] = block.astype(bf16)

    def own_half(x):
        return pltpu.roll(x, odd * (LANES // 2), x.ndim - 1)

    per = z.hid // LANES
    vec_rows = [vectors[0:1, :], vectors[1:2, :]] + [ffn_vec[r : r + 1, :] for r in range(3)]
    for r, row in enumerate(vec_rows):
        vec_tx[r : r + 1, :] = jnp.concatenate([row, row], axis=1)
    vec_tx[5:6, :] = own_half(jnp.concatenate([glu_bias[0:1, :], glu_bias[1:2, :]], axis=1))
    for r in range(per):
        vec_tx[6 + r : 7 + r, :] = up_bias[:, r * LANES : (r + 1) * LANES].astype(f32)
    pl.when(pipe == 0)(lambda: fill_blocks(tokens, tok_tx))
    pl.when(pipe == z.sections - 1)(lambda: fill_blocks(out_cot, cot_tx))
    pl.semaphore_wait(barrier, z.members - 1 + 2)

    to_peers(lambda c: vec_tx, vec_all, VEC)

    @pl.when(pipe == 0)
    def _():
        to_peers(lambda c: tok_tx.at[c], tok_rx, TOK)

    @pl.when(pipe == z.sections - 1)
    def _():
        to_peers(lambda c: cot_tx.at[c], cot_rx, COT)

    for t in (GLU, UP, DOWN):
        weights_ring(t)

    pad_rows = (z.blocks - 1) * z.gr * z.ch
    data_rows = z.blocks * z.gr * z.ch
    xs[0:pad_rows, :] = jnp.zeros((pad_rows, LANES), f32)
    xs[pad_rows + data_rows : z.stack, :] = jnp.zeros(
        (z.stack - pad_rows - data_rows, LANES), f32
    )
    gs[data_rows : z.stack, :] = jnp.zeros((z.stack - data_rows, LANES), f32)

    spot = lax.broadcasted_iota(jnp.int32, (1, LANES), 1)
    masks[z.blocks * z.gr :, :] = jnp.zeros((masks.shape[0] - z.blocks * z.gr, LANES), f32)
    for m in range(z.micros):
        first_len, second_len = lengths[m, 0], lengths[m, 1]
        for i in range(z.blocks):
            at = i * z.gr + m * z.segments
            where = spot + i * LANES
            masks[at : at + 1, :] = jnp.where(where < first_len, 1.0, 0.0)
            inside = jnp.where(where < first_len + second_len, 1.0, 0.0)
            masks[at + 1 : at + 2, :] = jnp.where(where >= first_len, inside, 0.0)

    ch, nh = z.ch, modes.shape[2]
    mine = pl.ds(pl.multiple_of(data * ch, ch), ch)
    decay, rate, rank_r, rank_i, in_r, in_i, out_r, out_i = (modes[p, mine, :] for p in range(8))
    pairs = [
        (out_r * in_r - out_i * in_i, out_r * in_i + out_i * in_r),
        (out_r * rank_r - out_i * rank_i, out_r * rank_i + out_i * rank_r),
        (rank_r * in_r + rank_i * in_i, rank_r * in_i - rank_i * in_r),
        (rank_r * rank_r + rank_i * rank_i, None),
    ]
    turn_s[...] = jnp.zeros(turn_s.shape, f32)
    for v, (v_r, v_i) in enumerate(pairs):
        alpha = decay * v_r if v_i is None else decay * v_r - rate * v_i
        turn_s[0, v * ch : (v + 1) * ch, 0:nh] = alpha
        turn_s[0, (4 + v) * ch : (5 + v) * ch, 0:nh] = v_r
    turn_s[1, 0:ch, 0:nh] = decay * decay + rate * rate
    turn_s[1, ch : 2 * ch, 0:nh] = 2.0 * decay
    turn_s[1, 2 * ch : 2 * ch + 4, 0 : z.cw] = vectors[...]
    cols[0] = turn_s[0].T[0:nh]
    turned = turn_s[1].T
    cols[1] = turned[0:nh]
    turn_s[1] = turned
    side = turn_s[1, mine, 2 * ch : 2 * ch + 4]
    rise_s[...] = jnp.broadcast_to(2.0 * jnp.exp(-side[:, 2:3]), (ch, LANES))
    skip[...] = jnp.broadcast_to(side[:, 3:4], (ch, LANES))
    cosine, sine = angles[0:1, :], angles[1:2, :]
    padded = angles.shape[1]

    def column_of(k, h):
        return pltpu.roll(cols[k], lax.rem(LANES - h, LANES), 1)

    def modes_at(h):
        two = column_of(1, h)
        square, double = two[:, 0:1], two[:, ch : ch + 1]
        y = rise_s[pl.ds(h, 1), 0:1] * sine
        cy = cosine * y
        den_r = square * (cosine * cosine) - y * y
        den_i = double * cy
        inverse = 1.0 / (den_r * den_r + den_i * den_i)
        return double, y, cy, den_r * inverse, den_i * inverse

    def cauchy_step(h, carry):
        _, _, _, u, w = modes_at(h)
        column = column_of(0, h)
        for v in range(4):
            a = column[:, v * ch : v * ch + 1]
            b = column[:, (4 + v) * ch : (4 + v) * ch + 1]
            sums_s[v, pl.ds(h, 1), :] = jnp.sum(a * u, axis=0, keepdims=True)
            sums_s[4 + v, pl.ds(h, 1), :] = jnp.sum(a * w, axis=0, keepdims=True)
            sums_s[8 + v, pl.ds(h, 1), :] = jnp.sum(b * u, axis=0, keepdims=True)
            sums_s[12 + v, pl.ds(h, 1), :] = jnp.sum(b * w, axis=0, keepdims=True)
        return carry

    def times(a, b):
        return a[0] * b[0] - a[1] * b[1], a[0] * b[1] + a[1] * b[0]

    def conj(a):
        return a[0], -a[1]

    def moments():
        y_all = rise_s[:, 0:1] * sine
        ms = [
            (
                2.0 * (cosine * sums_s[v] + y_all * sums_s[12 + v]),
                2.0 * (y_all * sums_s[8 + v] - cosine * sums_s[4 + v]),
            )
            for v in range(4)
        ]
        low_r, low_i = 1.0 + cosine * ms[3][0], cosine * ms[3][1]
        size = 1.0 / (low_r * low_r + low_i * low_i)
        return y_all, ms, times(ms[1], ms[2]), (low_r * size, -low_i * size)

    def high_low(x):
        high_part = x.astype(bf16)
        low_part = (x - high_part.astype(f32)).astype(bf16)
        return jnp.concatenate([high_part, low_part], axis=0)

    lax.fori_loop(0, ch, cauchy_step, 0)
    weights_across(GLU)
    y_all, ms, cross, over = moments()
    fix = times(cross, over)
    spec = jnp.concatenate([ms[0][0] - cosine * fix[0], ms[0][1] - cosine * fix[1]], axis=1)
    wait_bytes(table, recv.at[TABLE])
    both = dot(high_low(spec), table[...])
    wide = (z.blocks + 1) * LANES
    kern_s[:, 0 : z.length] = both[0:ch] + both[ch : 2 * ch]
    kern_s[:, z.length : wide] = jnp.zeros((ch, wide - z.length), f32)
    weights_across(UP)
    weights_beside(GLU)

    def toeplitz_step(h, carry):
        full = jnp.broadcast_to(kern_s[pl.ds(h, 1), :], (LANES, wide))
        full = pltpu.roll(full, 0, 1, stride=1, stride_axis=0).astype(bf16)
        far[h] = full[:, : z.length]
        for d in range(z.blocks):
            near[h, d * LANES : (d + 1) * LANES, :] = full[:, d * LANES : (d + 1) * LANES]
        return carry

    lax.fori_loop(0, ch, toeplitz_step, 0)
    weights_across(DOWN)
    weights_core(GLU)
    weights_beside(UP)

    wait_bytes(vec_all, recv.at[VEC])

    def full_row(r):
        tiles = [
            jnp.where(first_half, vec_all[2 * j, r : r + 1, :], vec_all[2 * j + 1, r : r + 1, :])
            for j in range(z.peers // 2)
        ]
        return jnp.concatenate(tiles, axis=1)

    gain1, bias1, gain2, bias2, out_bias = (full_row(r) for r in range(5))

    def norm_stats(v):
        mean = jnp.sum(v, axis=1, keepdims=True) * (1.0 / width)
        spread = jnp.sum(v * v, axis=1, keepdims=True) * (1.0 / width) - mean * mean
        inv = lax.rsqrt(spread + norm_eps)
        return (v - mean) * inv, inv

    def norm_back(e, hat, inv, gain):
        dh = e * gain
        first = jnp.sum(dh, axis=1, keepdims=True) * (1.0 / width)
        second = jnp.sum(dh * hat, axis=1, keepdims=True) * (1.0 / width)
        return inv * (dh - first - hat * second)

    def turn_out(v, ref):
        tall = jnp.concatenate([v, jnp.zeros((LANES - rows, width), f32)], axis=0)
        ref[...] = tall.T.astype(bf16).reshape(z.members, z.ch, LANES)

    def turn_in(ref):
        return ref[...].reshape(width, LANES).astype(f32).T[:rows]

    def lane_tiles(ref, m):
        tiles = []
        for i in range(z.blocks):
            lo, hi = i * LANES, (i + 1) * LANES
            tile = None
            for k in range(lo // tok, -(-hi // tok)):
                piece = shifted(ref[m * z.slots + k].astype(f32), k * tok - lo)
                first = max(0, k * tok - lo)
                if tile is None:
                    tile = piece
                else:
                    tile = jnp.where(lane >= first, piece, tile)
            tiles.append(tile)
        return tiles

    def lane_pieces(tiles, m, ref):
        for k in range(z.slots):
            i, off = divmod(k * tok, LANES)
            piece = shifted(tiles[i], LANES - off)
            if off + tok > LANES:
                piece = jnp.where(lane < LANES - off, piece, shifted(tiles[i + 1], LANES - off))
            ref[m * z.slots + k] = piece.astype(bf16)

    def row_at(i, g):
        return (i * z.gr + g) * z.ch

    def masked_store(ref, base, m, i, tile):
        for q in range(z.segments):
            g = m * z.segments + q
            at = base + row_at(i, g)
            ref[at : at + z.ch, :] = tile * masks[i * z.gr + g : i * z.gr + g + 1, :]

    def masked_sum(m, i):
        total = None
        for q in range(z.segments):
            g = m * z.segments + q
            at = row_at(i, g)
            part = ys[at : at + z.ch, :] * masks[i * z.gr + g : i * z.gr + g + 1, :]
            total = part if total is None else total + part
        return total

    conv_rows = -(-(z.blocks * z.gr) // 8) * 8

    @pl.when(pipe == 0)
    def _():
        wait_bytes(tok_rx, recv.at[TOK])
        for j in range(z.peers // 2):
            res[:, j * LANES : (j + 1) * LANES] = jnp.where(
                first_half, tok_rx[2 * j].astype(f32), tok_rx[2 * j + 1].astype(f32)
            ).astype(bf16)

    @pl.when(pipe > 0)
    def _():
        wait_bytes(res, recv.at[RES])

    hat1, inv1 = norm_stats(res[...].astype(f32))
    hat1_s[...] = hat1
    inv1_s[...] = jnp.broadcast_to(inv1, (rows, LANES))
    turn_out(hat1 * gain1 + bias1, tx1)
    to_members(lambda p: tx1.at[p], rx1, slot_me, A1)
    weights_beside(DOWN)
    weights_core(UP)
    wait_bytes(rx1, recv.at[A1])
    for m in range(z.micros):
        for i, tile in enumerate(lane_tiles(rx1, m)):
            masked_store(xs, pad_rows, m, i, tile)

    def conv_step(h, carry):
        parts = [
            xs[pl.ds((z.blocks - 1 - d) * z.gr * z.ch + h, conv_rows, stride=z.ch), :]
            for d in range(z.blocks)
        ]
        windows = jnp.concatenate(parts, axis=1).astype(bf16)
        ys[pl.ds(h, conv_rows, stride=z.ch), :] = dot(windows, near[h])
        return carry

    lax.fori_loop(0, z.ch, conv_step, 0)
    for m in range(z.micros):
        tiles = []
        for i in range(z.blocks):
            own = None
            for q in range(z.segments):
                at = pad_rows + row_at(i, m * z.segments + q)
                own = xs[at : at + z.ch, :] if own is None else own + xs[at : at + z.ch, :]
            tile = masked_sum(m, i) + skip[...] * own
            conv_out[m * z.blocks + i] = tile
            tiles.append(gelu(tile))
        lane_pieces(tiles, m, tx2)
    to_members(lambda p: tx2.at[slot_of(p)], rx2, me, A2)
    weights_core(DOWN)
    wait_bytes(rx2, recv.at[A2])
    gated_s[...] = turn_in(rx2).astype(bf16)
    weights_here(GLU)
    gated = gated_s[...]
    values, gates = [], []
    for j in range(z.peers // 2):
        lead = dot(gated, glu_all[2 * j]) + vec_all[2 * j, 5:6, :]
        tail = dot(gated, glu_all[2 * j + 1]) + vec_all[2 * j + 1, 5:6, :]
        values.append(jnp.where(first_half, lead, tail))
        gates.append(shifted(jnp.where(first_half, tail, lead), LANES // 2))
    value = jnp.concatenate(values, axis=1)
    sig = jax.nn.sigmoid(jnp.concatenate(gates, axis=1))
    val_s[...] = value
    sig_s[...] = sig
    mid = res[...].astype(f32) + value * sig
    hat2, inv2 = norm_stats(mid)
    hat2_s[...] = hat2
    inv2_s[...] = jnp.broadcast_to(inv2, (rows, LANES))
    ffn_s[...] = (hat2 * gain2 + bias2).astype(bf16)
    weights_here(UP)
    weights_here(DOWN)
    ffn_in = ffn_s[...]
    total = mid + out_bias
    for c in range(z.peers):
        offset = jnp.concatenate([vec_all[c, 6 + r : 7 + r, :] for r in range(per)], axis=1)
        hidden = dot(ffn_in, up_all[c]) + offset
        hidden_s[c] = hidden
        active = gelu(hidden).astype(bf16)
        act_s[c] = active
        total = total + dot(active, down_all[c])
    layer_out = jnp.where(row_ok, total, 0.0).astype(bf16)
    res_tx[...] = layer_out

    @pl.when(pipe < z.sections - 1)
    def _():
        remote(res_tx, res, RES, later).start()

    for j in range(z.peers // 2):
        lay_s[j] = layer_out[:, j * LANES : (j + 1) * LANES]
    to_peers(lambda c: lay_s.at[c // 2], hid_rx, HID)

    def forward_rows():
        to_peers(lambda c: gated_s, ga, GA)
        to_peers(lambda c: ffn_s, fi, FI)
        to_peers(lambda c: act_s.at[c], ac, AC)

    def backward_rows():
        to_peers(lambda c: gtop, bg, BG)
        to_peers(lambda c: gh_s.at[c], gh, GH)
        to_peers(lambda c: gp_s.at[c], gp, GP)

    pl.when(pipe < z.sections - 1)(forward_rows)

    @pl.when(pipe == z.sections - 1)
    def _():
        wait_bytes(cot_rx, recv.at[COT])
        for j in range(z.peers // 2):
            gtop[:, j * LANES : (j + 1) * LANES] = jnp.where(
                first_half, cot_rx[2 * j].astype(f32), cot_rx[2 * j + 1].astype(f32)
            ).astype(bf16)

    @pl.when(pipe < z.sections - 1)
    def _():
        wait_bytes(gtop, recv.at[GTOP])

    grad_low = gtop[...]
    grad_top = grad_low.astype(f32)
    grad_ffn = None
    for c in range(z.peers):
        grad_active = dot_nt(grad_low, down_all[c])
        grad_hidden = (grad_active * gelu_slope(hidden_s[c])).astype(bf16)
        gh_s[c] = grad_hidden
        part = dot_nt(grad_hidden, up_all[c])
        grad_ffn = part if grad_ffn is None else grad_ffn + part
    hat2 = hat2_s[...]
    grad_mid = grad_top + norm_back(grad_ffn, hat2, inv2_s[:, 0:1], gain2)
    sig = sig_s[...]
    grad_value = grad_mid * sig
    grad_gate = grad_value * val_s[...] * (1.0 - sig)
    grad_gated = None
    for j in range(z.peers // 2):
        gv = grad_value[:, j * LANES : (j + 1) * LANES]
        gg = shifted(grad_gate[:, j * LANES : (j + 1) * LANES], LANES // 2)
        pair = (jnp.where(first_half, gv, gg), jnp.where(first_half, gg, gv))
        for half in range(2):
            narrow = pair[half].astype(bf16)
            gp_s[2 * j + half] = narrow
            part = dot_nt(narrow, glu_all[2 * j + half])
            grad_gated = part if grad_gated is None else grad_gated + part
    turn_out(grad_gated, tx3)
    to_members(lambda p: tx3.at[p], rx3, slot_me, A3)
    pl.when(pipe == 0)(backward_rows)
    wait_bytes(rx3, recv.at[A3])
    for m in range(z.micros):
        for i, tile in enumerate(lane_tiles(rx3, m)):
            masked_store(gs, 0, m, i, tile * gelu_slope(conv_out[m * z.blocks + i]))

    def back_step(h, carry):
        parts = [
            gs[pl.ds(d * z.gr * z.ch + h, conv_rows, stride=z.ch), :] for d in range(z.blocks)
        ]
        windows = jnp.concatenate(parts, axis=1).astype(bf16)
        ys[pl.ds(h, conv_rows, stride=z.ch), :] = dot_nt(windows, far[h])
        return carry

    lax.fori_loop(0, z.ch, back_step, 0)
    for m in range(z.micros):
        tiles = []
        for i in range(z.blocks):
            own = None
            for q in range(z.segments):
                at = row_at(i, m * z.segments + q)
                own = gs[at : at + z.ch, :] if own is None else own + gs[at : at + z.ch, :]
            tiles.append(masked_sum(m, i) + skip[...] * own)
        lane_pieces(tiles, m, tx4)
    to_members(lambda p: tx4.at[slot_of(p)], rx4, me, A4)

    def lag_step(h, carry):
        x = xs[pl.ds(pad_rows + h, conv_rows, stride=z.ch), :]
        parts = [
            gs[pl.ds(d * z.gr * z.ch + h, conv_rows, stride=z.ch), :] for d in range(z.blocks)
        ]
        prod = dot_tn(x.astype(bf16), jnp.concatenate(parts, axis=1).astype(bf16))
        prod = jnp.concatenate([prod, jnp.zeros((LANES, LANES), f32)], axis=1)
        size = LANES // 2
        while size >= 8:
            prod = prod[:size] + shifted(prod[size:], wide - size)
            size //= 2
        row = prod[0:1]
        for a in range(1, 8):
            row = row + shifted(prod[a : a + 1], wide - a)
        lag_s[pl.ds(h, 1), :] = row
        return carry

    def lags():
        lax.fori_loop(0, ch, lag_step, 0)

    pl.when(pipe == 0)(lags)
    wait_bytes(rx4, recv.at[A4])
    grad_conv_in = jnp.where(row_ok, turn_in(rx4), 0.0)
    hat1 = hat1_s[...]
    grad_res = grad_mid + norm_back(grad_conv_in, hat1, inv1_s[:, 0:1], gain1)
    grad_res_low = grad_res.astype(bf16)
    ig_tx[...] = grad_res_low

    @pl.when(pipe > 0)
    def _():
        remote(ig_tx, gtop, GTOP, earlier).start()
        backward_rows()

    pl.when(pipe == z.sections - 1)(forward_rows)

    for j in range(z.peers // 2):
        ig_s[j] = grad_res_low[:, j * LANES : (j + 1) * LANES]
    to_peers(lambda c: ig_s.at[c // 2], ig_rx, IG)

    rows_of = [
        jnp.sum(grad_conv_in * hat1, axis=0, keepdims=True),
        jnp.sum(grad_conv_in, axis=0, keepdims=True),
        jnp.sum(grad_ffn * hat2, axis=0, keepdims=True),
        jnp.sum(grad_ffn, axis=0, keepdims=True),
        jnp.sum(grad_top, axis=0, keepdims=True),
    ]
    for c in range(z.peers):
        j = c // 2
        for r, row in enumerate(rows_of):
            vg_s[c, r : r + 1, :] = row[:, j * LANES : (j + 1) * LANES]
        vg_s[c, 5:6, :] = jnp.sum(gp_s[c].astype(f32), axis=0, keepdims=True)
        up_row = jnp.sum(gh_s[c].astype(f32), axis=0, keepdims=True)
        for r in range(per):
            vg_s[c, 6 + r : 7 + r, :] = up_row[:, r * LANES : (r + 1) * LANES]
    to_members(lambda p: vg_s.at[p // z.groups], vrx, me, VG)
    many = z.peers * rows
    grads = (
        (ac, AC, bg, BG, z.hid, width, pdown, kdown, sdown, ldown, ddown),
        (fi, FI, gh, GH, width, z.hid, pup, kup, sup, lup, dup),
        (ga, GA, gp, GP, width, 2 * z.cw, pglu, kglu, sglu, lglu, dglu),
    )
    sibling, across = place(chan, low * 2 + 1 - core), place(chan, (1 - low) * 2 + core)
    for t, (left, lp, right, rp, n_left, n_right, part, krx, *_) in enumerate(grads):
        wait_bytes(left, recv.at[lp])
        wait_bytes(right, recv.at[rp])
        part[...] = dot_tn(left[...].reshape(many, n_left), right[...].reshape(many, n_right))
        half = n_left // 2
        other = pl.ds(pl.multiple_of((1 - core) * half, half), half)
        remote(part.at[other], krx, GRADS + 3 * t, sibling).start()
    pl.when(pipe > 0)(lags)
    for t, (_, _, _, _, n_left, _, part, krx, lsend, lrx, _) in enumerate(grads):
        half = n_left // 2
        own = pl.ds(pl.multiple_of(core * half, half), half)
        wait_bytes(krx, recv.at[GRADS + 3 * t])
        lsend[...] = (part[own, :] + krx[...]).astype(bf16)
        remote(lsend, lrx, GRADS + 3 * t + 1, across).start()

    lag_low = high_low(lag_s[:, 0 : z.length])
    both = dot_nt(lag_low, table[...])
    grad_spec = both[0:ch] + both[ch : 2 * ch]
    gk = (grad_spec[:, 0:padded], grad_spec[:, padded : 2 * padded])
    y_all, ms, cross, over = moments()
    g_top = times(conj(over), gk)
    g_top = (-cosine * g_top[0], -cosine * g_top[1])
    g_low = times(conj(times(times(cross, over), over)), gk)
    g_three = (cosine * cosine * g_low[0], cosine * cosine * g_low[1])
    g_ms = [gk, times(conj(ms[2]), g_top), times(conj(ms[1]), g_top), g_three]
    g_rise = None
    for v, (g_r, g_i) in enumerate(g_ms):
        gsum_s[v] = 2.0 * cosine * g_r
        gsum_s[4 + v] = -2.0 * cosine * g_i
        gsum_s[8 + v] = 2.0 * y_all * g_i
        gsum_s[12 + v] = 2.0 * y_all * g_r
        part = 2.0 * (sums_s[12 + v] * g_r + sums_s[8 + v] * g_i)
        g_rise = part if g_rise is None else g_rise + part
    slope_s[...] = g_rise
    gcol_s[...] = jnp.zeros(gcol_s.shape, f32)

    def mode_step(h, carry):
        double, y, cy, u, w = modes_at(h)
        column = column_of(0, h)
        gu, gw = 0.0, 0.0
        acc = gcol_s[0, 0:nh, :]
        for v in range(4):
            a = column[:, v * ch : v * ch + 1]
            b = column[:, (4 + v) * ch : (4 + v) * ch + 1]
            au, aw = gsum_s[v, pl.ds(h, 1), :], gsum_s[4 + v, pl.ds(h, 1), :]
            bu, bw = gsum_s[8 + v, pl.ds(h, 1), :], gsum_s[12 + v, pl.ds(h, 1), :]
            gu = gu + a * au + b * bu
            gw = gw + a * aw + b * bw
            ga_col = jnp.sum(u * au + w * aw, axis=1, keepdims=True)
            gb_col = jnp.sum(u * bu + w * bw, axis=1, keepdims=True)
            acc = jnp.where(spot == v * ch + h, ga_col, acc)
            acc = jnp.where(spot == (4 + v) * ch + h, gb_col, acc)
        gcol_s[0, 0:nh, :] = acc
        even, cross_uw = u * u - w * w, 2.0 * u * w
        g_den_r = -(even * gu + cross_uw * gw)
        g_den_i = even * gw - cross_uw * gu
        acc = gcol_s[1, 0:nh, :]
        ge = jnp.sum(cosine * cosine * g_den_r, axis=1, keepdims=True)
        gf = jnp.sum(cy * g_den_i, axis=1, keepdims=True)
        acc = jnp.where(spot == h, ge, acc)
        gcol_s[1, 0:nh, :] = jnp.where(spot == ch + h, gf, acc)
        gy = slope_s[pl.ds(h, 1), :] + jnp.sum(
            double * cosine * g_den_i - 2.0 * y * g_den_r, axis=0, keepdims=True
        )
        total_y = jnp.sum(y * gy, axis=1, keepdims=True)
        gstep_s[pl.ds(h, 1), :] = jnp.broadcast_to(-total_y, (1, LANES))
        return carry

    lax.fori_loop(0, ch, mode_step, 0)
    back = gcol_s[0].T[:, 0:nh]
    g_alpha = [back[v * ch : (v + 1) * ch] for v in range(4)]
    g_beta = [back[(4 + v) * ch : (5 + v) * ch] for v in range(4)]
    back = gcol_s[1].T[:, 0:nh]
    g_square, g_double = back[0:ch], back[ch : 2 * ch]
    g_decay = 2.0 * decay * g_square + 2.0 * g_double
    g_rate = 2.0 * rate * g_square
    g_pairs = []
    for v, (v_r, v_i) in enumerate(pairs):
        g_decay = g_decay + g_alpha[v] * v_r
        if v_i is not None:
            g_rate = g_rate - g_alpha[v] * v_i
        g_pairs.append((decay * g_alpha[v] + g_beta[v], -rate * g_alpha[v]))
    c_b, c_p, p_b = g_pairs[0], g_pairs[1], g_pairs[2]
    p_p = g_pairs[3][0]
    rank, into, out = (rank_r, rank_i), (in_r, in_i), (out_r, out_i)

    def plus(*terms):
        return sum(t[0] for t in terms), sum(t[1] for t in terms)

    g_out = plus(times(conj(into), c_b), times(conj(rank), c_p))
    g_in = plus(times(conj(out), c_b), times(rank, p_b))
    g_rank = plus(
        times(conj(out), c_p),
        times(into, conj(p_b)),
        (2.0 * rank_r * p_p, 2.0 * rank_i * p_p),
    )
    for p, value in enumerate((g_decay, g_rate, *g_rank, *g_in, *g_out)):
        modes_tx[p, :, 0:nh] = value
    modes_tx[8] = jnp.where(spot == 0, gstep_s[...], lag_s[:, 0:LANES])
    modes_tx[9] = lag_s[:, 0:LANES]
    for k in range(1, z.groups):
        remote(modes_tx, modes_rx.at[data], MODES, place(chan, lax.rem(data + k, z.groups))).start()
    pltpu.make_async_copy(modes_tx, modes_rx.at[data], recv.at[MODES]).start()

    for t, (_, _, _, _, n_left, _, _, _, lsend, lrx, final) in enumerate(grads):
        half = n_left // 2
        own = pl.ds(pl.multiple_of(core * half, half), half)
        wait_bytes(lrx, recv.at[GRADS + 3 * t + 1])
        final[own, :] = lsend[...].astype(f32) + lrx[...].astype(f32)
        remote(final.at[own], final.at[own], GRADS + 3 * t + 2, sibling).start()

    def collect(source, target):
        for m in range(z.micros):
            parts = [
                own_half(source[m * z.quarters + q].astype(f32))[0:tok] for q in range(z.quarters)
            ]
            target[m] = jnp.concatenate(parts, axis=0)[:, 0 : z.cw].astype(bf16)

    wait_bytes(hid_rx, recv.at[HID])
    collect(hid_rx, hid_out)
    wait_bytes(ig_rx, recv.at[IG])
    collect(ig_rx, ig_out)
    wait_bytes(vrx, recv.at[VG])
    summed = vrx[0]
    for p in range(1, z.members):
        summed = summed + vrx[p]
    upb_out[...] = jnp.concatenate([summed[6 + r : 7 + r, :] for r in range(per)], axis=1)
    summed = own_half(summed)
    ffn_out[...] = summed[2:5, 0 : z.cw]
    glub_out[0:1, :] = summed[5:6, 0 : z.cw]
    glub_out[1:2, :] = shifted(summed[5:6], LANES // 2)[:, 0 : z.cw]
    vec_out[0:2, :] = summed[0:2, 0 : z.cw]
    wait_bytes(modes_rx, recv.at[MODES])
    for p in range(8):
        for d in range(z.groups):
            modes_out[p, d * ch : (d + 1) * ch, :] = modes_rx[d, p, :, 0:nh]
    for d in range(z.groups):
        turn_s[0, d * ch : (d + 1) * ch, :] = modes_rx[d, 8]
        turn_s[1, d * ch : (d + 1) * ch, :] = modes_rx[d, 9]
    vec_out[2:3, :] = turn_s[0].T[0:1, 0 : z.cw]
    vec_out[3:4, :] = turn_s[1].T[0:1, 0 : z.cw]
    for t, (_, _, _, _, n_left, _, _, _, _, _, final) in enumerate(grads):
        half = n_left // 2
        other = pl.ds(pl.multiple_of((1 - core) * half, half), half)
        wait_bytes(final.at[other], recv.at[GRADS + 3 * t + 2])

    for t in (GLU, UP, DOWN):
        weights_sent(t)
    for ref, phase in (
        (vec_all, VEC), (hid_rx, HID),
        (ig_rx, IG), (ga, GA), (fi, FI), (ac, AC), (bg, BG), (gh, GH), (gp, GP),
    ):
        wait_bytes(ref.at[pl.ds(0, z.peers - 1)], send.at[phase])
    for ref, phase in ((rx1, A1), (rx2, A2), (rx3, A3), (rx4, A4), (vrx, VG)):
        wait_bytes(ref.at[pl.ds(0, z.members - 1)], send.at[phase])
    wait_bytes(modes_rx.at[pl.ds(0, z.groups - 1)], send.at[MODES])
    for t, (_, _, _, _, n_left, _, _, krx, lsend, _, final) in enumerate(grads):
        wait_bytes(krx, send.at[GRADS + 3 * t])
        wait_bytes(lsend, send.at[GRADS + 3 * t + 1])
        wait_bytes(final.at[pl.ds(0, n_left // 2)], send.at[GRADS + 3 * t + 2])

    @pl.when(pipe == 0)
    def _():
        wait_bytes(tok_rx.at[pl.ds(0, z.peers - 1)], send.at[TOK])

    @pl.when(pipe == z.sections - 1)
    def _():
        wait_bytes(cot_rx.at[pl.ds(0, z.peers - 1)], send.at[COT])

    @pl.when(pipe < z.sections - 1)
    def _():
        wait_bytes(res_tx, send.at[RES])

    @pl.when(pipe > 0)
    def _():
        wait_bytes(ig_tx, send.at[GTOP])


def body(
    tokens,
    seq_lengths,
    out_cot,
    s4_vectors,
    s4_modes,
    glu_weight,
    glu_bias,
    ffn_vectors,
    up_weight,
    up_bias,
    down_weight,
):
    chan = lax.axis_index("chan")
    micros, tok_rows, chan_width = tokens.shape
    width = glu_weight.shape[1]
    hidden = up_weight.shape[2]
    z = Sizes(
        lax.axis_size("pipe"), lax.axis_size("chan"), lax.axis_size("dp"),
        tok_rows, chan_width, width, hidden,
    )
    odd = lax.rem(chan, 2) == 1
    length = z.length
    padded = -(-(length // 2 + 1) // LANES) * LANES
    nh = s4_modes.shape[3]

    def swap(value, gate):
        return jnp.where(
            odd, jnp.concatenate([gate, value], -1), jnp.concatenate([value, gate], -1)
        )

    glu_loc = swap(glu_weight[0, :, 0, :], glu_weight[0, :, 1, :])
    table = jnp.asarray(fourier_table(length, padded).astype(ml_dtypes.bfloat16))
    angles = jnp.asarray(half_angles(length, padded))

    vmem = pl.BlockSpec(memory_space=pltpu.VMEM)
    smem = pl.BlockSpec(memory_space=pltpu.SMEM)
    anywhere = pl.BlockSpec(memory_space=pl.ANY)
    n, r, w, ch = z.peers, z.rows, width, z.ch

    def s(shape, kind=f32):
        return jax.ShapeDtypeStruct(shape, kind)

    def v(shape, kind=bf16):
        return pltpu.VMEM(shape, kind)

    exchange = (z.members, z.ch, LANES)
    conv_rows = -(-(z.blocks * z.gr) // 8) * 8
    wide = (z.blocks + 1) * LANES
    hid, ig, vec, modes, dglu, glub, ffn, dup, upb, ddown = pl.pallas_call(
        lambda *refs: main_kernel(z, *refs),
        out_shape=(
            s((micros, tok_rows, chan_width), bf16), s((micros, tok_rows, chan_width), bf16),
            s((4, chan_width)), s((8, chan_width, nh)), s((w, 2 * chan_width)),
            s((2, chan_width)), s((3, chan_width)), s((w, hidden)), s((1, hidden)),
            s((hidden, w)),
        ),
        in_specs=[smem] + [vmem] * 11 + [anywhere],
        out_specs=[vmem] * 10,
        scratch_shapes=[
            v((n, r, LANES)), v((n, r, LANES)), v((8, LANES), f32), v((ch, length, LANES)),
            v((ch, LANES, length)), v((ch, LANES), f32), v((conv_rows, LANES), f32),
            v((n, r, LANES)), v((n, r, LANES)), v((z.stack, LANES), f32),
            v((z.stack, LANES), f32),
            v((2 * padded, length)), v((2, LANES, LANES), f32), v((2, nh, LANES), f32),
            v((ch, LANES), f32), v((16, ch, padded), f32), v((16, ch, padded), f32),
            v((ch, padded), f32), v((ch, wide), f32), v((ch, wide), f32),
            v((2, LANES, LANES), f32), v((ch, LANES), f32),
            v((10, ch, LANES), f32), v((z.groups, 10, ch, LANES), f32),
            v((w, 2 * chan_width), f32), v((w, hidden), f32), v((hidden, w), f32),
            v((w // 2, 2 * chan_width), f32), v((w // 2, hidden), f32), v((hidden // 2, w), f32),
            v((w // 2, 2 * chan_width)), v((w // 2, hidden)), v((hidden // 2, w)),
            v((w // 2, 2 * chan_width)), v((w // 2, hidden)), v((hidden // 2, w)),
            v((n, 8, LANES), f32), v((n, w, 2 * chan_width)), v((n, w, hidden)),
            v((n, hidden, w)), v((n, r, LANES)), v((n, r, LANES)), v((r, w)), v((r, w)),
        ]
        + [v(exchange)] * 8
        + [
            v((z.micros * z.blocks, z.ch, LANES), f32), v((conv_rows * z.ch, LANES), f32),
            v((r, w), f32), v((r, LANES), f32), v((r, w), f32), v((r, LANES), f32),
            v((r, w), f32), v((r, w), f32), v((n, r, hidden), f32),
            v((r, w)), v((r, w)), v((n, r, hidden)), v((n, r, hidden)), v((n, r, LANES)),
            v((n // 2, r, LANES)), v((r, w)), v((n // 2, r, LANES)), v((r, w)),
            v((n, 8, LANES), f32),
            v((n, r, w)), v((n, r, w)), v((n, r, hidden)), v((n, r, w)), v((n, r, hidden)),
            v((n, r, LANES)), v((z.members, 8, LANES), f32),
            pltpu.SemaphoreType.DMA((48,)), pltpu.SemaphoreType.DMA((48,)),
        ],
        compiler_params=pltpu.CompilerParams(
            collective_id=0, has_side_effects=True, vmem_limit_bytes=60 * 2**20
        ),
        name="layers",
    )(
        seq_lengths, tokens, out_cot, s4_vectors[0], s4_modes[0], glu_loc, glu_bias[0],
        ffn_vectors[0], up_weight[0], up_bias, down_weight[0], angles, table,
    )
    glu_first, glu_second = dglu[:, :chan_width], dglu[:, chan_width:]
    grad_glu = jnp.stack(
        [jnp.where(odd, glu_second, glu_first), jnp.where(odd, glu_first, glu_second)], axis=1
    )
    return (
        hid[None], ig[None], vec[None], modes[None], grad_glu[None], glub[None], ffn[None],
        dup[None], upb, ddown[None],
    )


def solution(mesh):
    placed = (
        P(None, "dp", "chan"),
        P(),
        P(None, "dp", "chan"),
        P("pipe", None, "chan"),
        P("pipe", None, "chan", None),
        P("pipe", None, None, "chan"),
        P("pipe", None, "chan"),
        P("pipe", None, "chan"),
        P("pipe", None, "chan"),
        P("pipe", "chan"),
        P("pipe", "chan", None),
    )
    return jax.shard_map(
        body,
        mesh=mesh,
        in_specs=placed,
        out_specs=(
            P("pipe", None, "dp", "chan"),
            P("pipe", None, "dp", "chan"),
            P("pipe", None, "chan"),
            P("pipe", None, "chan", None),
            P("pipe", None, None, "chan"),
            P("pipe", None, "chan"),
            P("pipe", None, "chan"),
            P("pipe", None, "chan"),
            P("pipe", "chan"),
            P("pipe", "chan", None),
        ),
        check_vma=False,
    )
```

```python
import math

import jax
import jax.numpy as jnp
import ml_dtypes
import numpy as np
from jax import lax
from jax.experimental import pallas as pl
from jax.experimental.pallas import tpu as pltpu
from jax.sharding import PartitionSpec as P

norm_eps = 1e-05
f32 = jnp.float32
bf16 = jnp.bfloat16
LANES = 128


def fourier_table(length, padded):
    half = length // 2
    freq = np.arange(padded, dtype=np.int64)[:, None]
    time = np.arange(length, dtype=np.int64)[None, :]
    angle = (freq * (2 * time + 1) % (2 * length)) * (np.pi / length)
    weight = np.where(freq <= half, np.where((freq == 0) | (freq == half), 1.0, 2.0), 0.0) / length
    table = np.concatenate([np.cos(angle) * weight, -np.sin(angle) * weight], axis=0)
    return table.astype(np.float32)


def half_angles(length, padded):
    angle = np.minimum(np.arange(padded), length // 2) * (np.pi / length)
    rows = np.zeros((8, padded), np.float32)
    rows[0] = np.where(np.arange(padded) < length // 2, np.cos(angle), 0.0)
    rows[1] = np.sin(angle)
    return rows


def shifted(x, by):
    size = x.shape[-1]
    by = by % size
    if by == 0:
        return x
    return pltpu.roll(x, by, x.ndim - 1)


def gelu(x):
    return 0.5 * x * (1.0 + jnp.tanh(math.sqrt(2.0 / math.pi) * (x + 0.044715 * x * x * x)))


def gelu_slope(x):
    scale = math.sqrt(2.0 / math.pi)
    t = jnp.tanh(scale * (x + 0.044715 * x * x * x))
    return 0.5 * (1.0 + t) + 0.5 * x * (1.0 - t * t) * scale * (1.0 + 3.0 * 0.044715 * x * x)


def dot(a, b):
    return lax.dot_general(a, b, (((1,), (0,)), ((), ())), preferred_element_type=f32)


def dot_nt(a, b):
    return lax.dot_general(a, b, (((1,), (1,)), ((), ())), preferred_element_type=f32)


def dot_tn(a, b):
    return lax.dot_general(a, b, (((0,), (0,)), ((), ())), preferred_element_type=f32)


class Sizes:
    def __init__(self, sections, peers, groups, tok_rows, chan_width, model_width, hidden):
        self.sections, self.peers, self.groups = sections, peers, groups
        self.micros = 2
        self.segments = 2
        self.quarters = peers // self.micros
        self.tok = tok_rows // self.quarters
        self.rows = -(-self.tok // 16) * 16
        self.length = tok_rows * groups
        self.blocks = self.length // LANES
        self.width = model_width
        self.cw = chan_width
        self.hid = hidden
        self.members = peers * groups
        self.ch = model_width // self.members
        self.slots = self.quarters * groups
        self.gr = self.micros * self.segments
        self.stack = (2 * self.blocks) * self.gr * self.ch


def main_kernel(z, *refs):
    (
        lengths, tokens, out_cot, vectors, modes, glu_loc, glu_bias, ffn_vec, up_loc, up_bias,
        down_loc, angles, table_in,
    ) = refs[:13]
    (
        hid_out, ig_out, vec_out, modes_out, glu_out, glub_out, ffn_out, dup, upb_out, ddown,
    ) = refs[13:23]
    (
        tok_tx, cot_tx, vec_tx, near, far, skip, masks, hid_rx, ig_rx, xs, gs,
        table, cols, rise_s, sums_s, gsum_s, slope_s, kern_s, lag_s, gcol_s, gstep_s,
        modes_tx, modes_rx, pglu, pup, pdown, kglu, kup, kdown, sglu, sup, sdown,
        lglu, lup, ldown, dglu,
        vec_all, vec_next, glu_all, up_all, down_all, tok_rx, cot_rx, res, gtop,
        tx1, tx1n, rx1, tx2, rx2, tx3, rx3, tx4, rx4, rx4n,
        conv_out, ys, hat1_s, inv1_s, hatn_s, invn_s, hat2_s, inv2_s, val_s, sig_s, hidden_s,
        gated_s, ffn_s, act_s, gh_s, gp_s, lay_s, lay_t, ig_t, ign_t, mid_s, mid_rx,
        vg_s, vgn_s, vg0_s, ga, fi, ac, bg, gh, gp, vrx, vnrx, send, recv,
    ) = refs[23:]
    pipe = lax.axis_index("pipe")
    chan = lax.axis_index("chan")
    data = lax.axis_index("dp")
    last = z.sections - 1
    me = chan * z.groups + data
    slot_me = (chan // z.quarters) * z.slots + data * z.quarters + lax.rem(chan, z.quarters)
    rows, width, tok = z.rows, z.width, z.tok
    spot = lax.broadcasted_iota(jnp.int32, (1, LANES), 1)
    first_half = spot < (LANES // 2)
    row_ok = lax.broadcasted_iota(jnp.int32, (rows, 1), 0) < tok
    odd = lax.rem(chan, 2)
    per = z.hid // LANES

    def slot_of(p):
        c, d = p // z.groups, lax.rem(p, z.groups)
        return (c // z.quarters) * z.slots + d * z.quarters + lax.rem(c, z.quarters)

    def place(c, d, section=None):
        return {"pipe": pipe if section is None else section, "chan": c, "dp": d}

    def member(p, section=None):
        return place(p // z.groups, lax.rem(p, z.groups), section)

    def remote(src, dst, phase, where):
        return pltpu.make_async_remote_copy(
            src_ref=src,
            dst_ref=dst,
            send_sem=send.at[phase],
            recv_sem=recv.at[phase],
            device_id=where,
            device_id_type=pl.DeviceIdType.MESH,
        )

    def wait_bytes(ref, sem):
        pltpu.make_async_copy(ref, ref, sem).wait()

    def to_peers(src_of, dst, phase):
        def step(k, carry):
            c = lax.rem(chan + k, z.peers)
            remote(src_of(c), dst.at[chan], phase, place(c, data)).start()
            return carry

        lax.fori_loop(1, z.peers, step, 0)
        pltpu.make_async_copy(src_of(chan), dst.at[chan], recv.at[phase]).start()

    def to_members(src_of, dst, slot, phase):
        def step(k, carry):
            p = lax.rem(me + k, z.members)
            remote(src_of(p), dst.at[slot], phase, member(p)).start()
            return carry

        lax.fori_loop(1, z.members, step, 0)
        pltpu.make_async_copy(src_of(me), dst.at[slot], recv.at[phase]).start()

    def to_section(src_of, dst, slot, phase, section):
        def step(k, carry):
            p = lax.rem(me + k, z.members)
            remote(src_of(p), dst.at[slot], phase, member(p, section)).start()
            return carry

        lax.fori_loop(0, z.members, step, 0)

    def to_section_peers(src_of, dst, phase, section):
        def step(k, carry):
            c = lax.rem(chan + k, z.peers)
            remote(src_of(c), dst.at[chan], phase, place(c, data, section)).start()
            return carry

        lax.fori_loop(0, z.peers, step, 0)

    (
        VEC, VECN, TOK, COT, A1, A2, A3, A4, A4N, RES, MID, HID, IG, GA, FI, AC, BG, GH, GP, VG,
        VGN, TABLE, MODES,
    ) = range(23)
    GLU, UP, DOWN, GRADS = 23, 29, 35, 41

    high, deep = chan // z.quarters, lax.rem(chan, z.quarters)
    side, core = data // 2, lax.rem(data, 2)
    own_side, far_side = high * z.quarters, (1 - high) * z.quarters
    sibling, across = place(chan, side * 2 + 1 - core), place(chan, (1 - side) * 2 + core)

    def piece_of(t, c, count, part=None):
        if t == GLU:
            if part is None:
                return glu_all.at[core, pl.ds(c, count)]
            fourth = z.cw // 2
            start = pl.multiple_of(part * fourth, fourth)
            return glu_all.at[core, pl.ds(c, count), pl.ds(start, fourth)]
        loc, whole = (up_loc, up_all) if t == UP else (down_loc, down_all)
        half = loc.shape[0] // 2
        fourth = half // 2
        if part is None:
            return whole.at[pl.ds(c, count), pl.ds(pl.multiple_of(core * half, half), half)]
        start = pl.multiple_of(core * half + part * fourth, fourth)
        return whole.at[pl.ds(c, count), pl.ds(start, fourth)]

    def weights_ring(t):
        if t == GLU:
            loc, whole, mine = glu_loc, glu_all.at[:, chan], glu_loc.at[core]
        else:
            loc, whole = (up_loc, up_all) if t == UP else (down_loc, down_all)
            half = loc.shape[0] // 2
            whole, mine = whole.at[chan], loc.at[pl.ds(pl.multiple_of(core * half, half), half)]
        pltpu.make_async_copy(loc, whole, recv.at[t + 5]).start()
        for k in range(1, z.quarters):
            c = own_side + lax.rem(deep + k, z.quarters)
            there = piece_of(t, chan, 1).at[0]
            remote(mine, there, t, place(c, data)).start()

    def weights_across(t):
        loc = {GLU: glu_loc, UP: up_loc, DOWN: down_loc}[t]
        wait_bytes(piece_of(t, 0, z.quarters - 1), recv.at[t])
        wait_bytes(loc, recv.at[t + 5])
        piece = piece_of(t, own_side, z.quarters, side)
        where = place(far_side + deep, (1 - side) * 2 + core)
        remote(piece, piece, t + 1, where).start()
        for k in range(1, z.quarters):
            piece = piece_of(t, own_side + lax.rem(deep + k, z.quarters), 1)
            remote(piece, piece, t + 3, sibling).start()

    def weights_beside(t):
        wait_bytes(piece_of(t, 0, z.quarters, 0), recv.at[t + 1])
        piece = piece_of(t, far_side, z.quarters, 1 - side)
        remote(piece, piece, t + 2, across).start()

    def weights_core(t):
        wait_bytes(piece_of(t, 0, z.quarters, 0), recv.at[t + 2])
        piece = piece_of(t, far_side, z.quarters)
        remote(piece, piece, t + 4, sibling).start()

    def weights_here(t):
        wait_bytes(piece_of(t, 0, z.quarters - 1), recv.at[t + 3])
        wait_bytes(piece_of(t, 0, z.quarters), recv.at[t + 4])

    def weights_sent(t):
        for stage, count, part in (
            (0, z.quarters - 1, None), (1, z.quarters, 0), (2, z.quarters, 0),
            (3, z.quarters - 1, None), (4, z.quarters, None),
        ):
            wait_bytes(piece_of(t, 0, count, part), send.at[t + stage])

    barrier = pltpu.get_barrier_semaphore()

    def greet(p, section):
        pl.semaphore_signal(
            barrier, inc=1, device_id=member(p, section), device_id_type=pl.DeviceIdType.MESH
        )

    def greet_own(k, carry):
        greet(lax.rem(me + k, z.members), None)
        return carry

    def greet_next(k, carry):
        greet(lax.rem(me + k, z.members), pipe + 1)
        return carry

    def greet_before(k, carry):
        greet(lax.rem(me + k, z.members), pipe - 1)
        return carry

    lax.fori_loop(1, z.members, greet_own, 0)

    @pl.when(pipe < last)
    def _():
        lax.fori_loop(0, z.members, greet_next, 0)

    @pl.when(pipe > 0)
    def _():
        lax.fori_loop(0, z.members, greet_before, 0)

    pltpu.make_async_copy(table_in, table, recv.at[TABLE]).start()

    def own_half(x):
        return pltpu.roll(x, odd * (LANES // 2), x.ndim - 1)

    def fill_blocks(source, target):
        count = z.tok * z.quarters
        over = -(-count // LANES) * LANES
        for m in range(z.micros):
            x = source[m].astype(f32)
            x = jnp.concatenate([x, jnp.zeros((z.cw, over - count), f32)], axis=1)
            for q in range(z.quarters):
                target[m * z.quarters + q] = shifted(x, over - q * tok)[:, 0:LANES].astype(bf16)

    vec_rows = [vectors[0:1, :], vectors[1:2, :]] + [ffn_vec[r] for r in range(3)]
    vec_rows += [glu_bias[0:1, :], glu_bias[1:2, :]]
    for r, row in enumerate(vec_rows):
        vec_tx[r : r + 1, :] = jnp.concatenate([row, row], axis=1)
    for r in range(per):
        vec_tx[7 + r : 8 + r, :] = up_bias[:, r * LANES : (r + 1) * LANES].astype(f32)
    pl.when(pipe == 0)(lambda: fill_blocks(tokens, tok_tx))
    pl.when(pipe == last)(lambda: fill_blocks(out_cot, cot_tx))

    ch, nh = z.ch, modes.shape[1]

    def own_lanes(x):
        x = jnp.concatenate([x, jnp.zeros((x.shape[0], LANES - z.cw), f32)], axis=1)
        return pltpu.roll(x, lax.rem(LANES - data * ch, LANES), 1)

    def packed(items):
        total = items[0]
        for i, item in enumerate(items[1:], 1):
            total = jnp.where(spot // ch == i, shifted(item, i * ch), total)
        return total

    decay, rate, rank_r, rank_i, in_r, in_i, out_r, out_i = (own_lanes(modes[p]) for p in range(8))
    pairs = [
        (out_r * in_r - out_i * in_i, out_r * in_i + out_i * in_r),
        (out_r * rank_r - out_i * rank_i, out_r * rank_i + out_i * rank_r),
        (rank_r * in_r + rank_i * in_i, rank_r * in_i - rank_i * in_r),
        (rank_r * rank_r + rank_i * rank_i, None),
    ]
    alphas = [
        decay * v_r if v_i is None else decay * v_r - rate * v_i for v_r, v_i in pairs
    ]
    cols[0] = packed(alphas + [v_r for v_r, v_i in pairs])
    cols[1] = packed([decay * decay + rate * rate, 2.0 * decay])
    own_vectors = own_lanes(vectors[...])
    diagonal = lax.broadcasted_iota(jnp.int32, (ch, LANES), 0) == lax.broadcasted_iota(
        jnp.int32, (ch, LANES), 1
    )

    def upright(row):
        column = jnp.sum(jnp.where(diagonal, row, 0.0), axis=1, keepdims=True)
        return jnp.broadcast_to(column, (ch, LANES))

    rise_s[...] = 2.0 * jnp.exp(-upright(own_vectors[2:3]))
    skip[...] = upright(own_vectors[3:4])
    cosine, sine = angles[0:1, :], angles[1:2, :]
    padded = angles.shape[1]

    def column_of(k, h):
        return pltpu.roll(cols[k], lax.rem(LANES - h, LANES), 1)

    def modes_at(h):
        two = column_of(1, h)
        square, double = two[:, 0:1], two[:, ch : ch + 1]
        y = rise_s[pl.ds(h, 1), 0:1] * sine
        cy = cosine * y
        den_r = square * (cosine * cosine) - y * y
        den_i = double * cy
        inverse = 1.0 / (den_r * den_r + den_i * den_i)
        return double, y, cy, den_r * inverse, den_i * inverse

    def cauchy_one(h):
        _, _, _, u, w = modes_at(h)
        column = column_of(0, h)
        for v in range(4):
            a = column[:, v * ch : v * ch + 1]
            b = column[:, (4 + v) * ch : (4 + v) * ch + 1]
            sums_s[v, pl.ds(h, 1), :] = jnp.sum(a * u, axis=0, keepdims=True)
            sums_s[4 + v, pl.ds(h, 1), :] = jnp.sum(a * w, axis=0, keepdims=True)
            sums_s[8 + v, pl.ds(h, 1), :] = jnp.sum(b * u, axis=0, keepdims=True)
            sums_s[12 + v, pl.ds(h, 1), :] = jnp.sum(b * w, axis=0, keepdims=True)

    def each_channel(one, unroll):
        def step(i, carry):
            for u in range(unroll):
                one(i * unroll + u)
            return carry

        if unroll == ch:
            step(0, 0)
        else:
            lax.fori_loop(0, ch // unroll, step, 0)

    def times(a, b):
        return a[0] * b[0] - a[1] * b[1], a[0] * b[1] + a[1] * b[0]

    def conj(a):
        return a[0], -a[1]

    def moments():
        y_all = rise_s[:, 0:1] * sine
        ms = [
            (
                2.0 * (cosine * sums_s[v] + y_all * sums_s[12 + v]),
                2.0 * (y_all * sums_s[8 + v] - cosine * sums_s[4 + v]),
            )
            for v in range(4)
        ]
        low_r, low_i = 1.0 + cosine * ms[3][0], cosine * ms[3][1]
        size = 1.0 / (low_r * low_r + low_i * low_i)
        return y_all, ms, times(ms[1], ms[2]), (low_r * size, -low_i * size)

    def high_low(x):
        high_part = x.astype(bf16)
        low_part = (x - high_part.astype(f32)).astype(bf16)
        return jnp.concatenate([high_part, low_part], axis=0)

    each_channel(cauchy_one, 4)
    pad_rows = (z.blocks - 1) * z.gr * z.ch
    data_rows = z.blocks * z.gr * z.ch
    xs[0:pad_rows, :] = jnp.zeros((pad_rows, LANES), f32)
    xs[pad_rows + data_rows : z.stack, :] = jnp.zeros(
        (z.stack - pad_rows - data_rows, LANES), f32
    )
    gs[data_rows : z.stack, :] = jnp.zeros((z.stack - data_rows, LANES), f32)
    masks[z.blocks * z.gr :, :] = jnp.zeros((masks.shape[0] - z.blocks * z.gr, LANES), f32)
    for m in range(z.micros):
        first_len, second_len = lengths[m, 0], lengths[m, 1]
        for i in range(z.blocks):
            at = i * z.gr + m * z.segments
            where = spot + i * LANES
            masks[at : at + 1, :] = jnp.where(where < first_len, 1.0, 0.0)
            inside = jnp.where(where < first_len + second_len, 1.0, 0.0)
            masks[at + 1 : at + 2, :] = jnp.where(where >= first_len, inside, 0.0)

    pl.semaphore_wait(
        barrier,
        z.members - 1 + z.members * (jnp.minimum(pipe, 1) + jnp.minimum(last - pipe, 1)),
    )

    @pl.when(pipe == 0)
    def _():
        to_peers(lambda c: tok_tx.at[c], tok_rx, TOK)

    to_peers(lambda c: vec_tx, vec_all, VEC)
    weights_ring(GLU)

    @pl.when(pipe > 0)
    def _():
        to_section_peers(lambda c: vec_tx, vec_next, VECN, pipe - 1)

    @pl.when(pipe == last)
    def _():
        to_peers(lambda c: cot_tx.at[c], cot_rx, COT)

    weights_ring(UP)
    weights_ring(DOWN)

    y_all, ms, cross, over = moments()
    fix = times(cross, over)
    spec = jnp.concatenate([ms[0][0] - cosine * fix[0], ms[0][1] - cosine * fix[1]], axis=1)
    wait_bytes(table, recv.at[TABLE])
    both = dot(high_low(spec), table[...])
    wide = (z.blocks + 1) * LANES
    kern_s[:, 0 : z.length] = both[0:ch] + both[ch : 2 * ch]
    kern_s[:, z.length : wide] = jnp.zeros((ch, wide - z.length), f32)

    def norm_stats(v):
        mean = jnp.sum(v, axis=1, keepdims=True) * (1.0 / width)
        spread = jnp.sum(v * v, axis=1, keepdims=True) * (1.0 / width) - mean * mean
        inv = lax.rsqrt(spread + norm_eps)
        return (v - mean) * inv, inv

    def norm_back(e, hat, inv, gain):
        dh = e * gain
        first = jnp.sum(dh, axis=1, keepdims=True) * (1.0 / width)
        second = jnp.sum(dh * hat, axis=1, keepdims=True) * (1.0 / width)
        return inv * (dh - first - hat * second)

    def turn_out(v, ref):
        tall = jnp.concatenate([v, jnp.zeros((LANES - rows, width), f32)], axis=0)
        ref[...] = tall.T.astype(bf16).reshape(ref.shape)

    def turn_in(ref):
        return ref[...].reshape(width, LANES).astype(f32).T[:rows]

    def full_row(source, r):
        tiles = [
            jnp.where(first_half, source[2 * j, r : r + 1, :], source[2 * j + 1, r : r + 1, :])
            for j in range(z.peers // 2)
        ]
        return jnp.concatenate(tiles, axis=1)

    wait_bytes(vec_all, recv.at[VEC])

    @pl.when(pipe == 0)
    def _():
        wait_bytes(tok_rx, recv.at[TOK])
        x = turn_in(tok_rx)
        res[...] = x.astype(bf16)
        hat1, inv1 = norm_stats(x)
        hat1_s[...] = hat1
        inv1_s[...] = jnp.broadcast_to(inv1, (rows, LANES))
        turn_out(hat1 * full_row(vec_all, 0) + full_row(vec_all, 1), tx1)
        to_members(lambda p: tx1.at[p], rx1, slot_me, A1)

    weights_across(GLU)

    def toeplitz_one(h):
        full = jnp.broadcast_to(kern_s[pl.ds(h, 1), :], (LANES, wide))
        full = pltpu.roll(full, 0, 1, stride=1, stride_axis=0).astype(bf16)
        far[h] = full[:, : z.length]
        for d in range(z.blocks):
            near[h, d * LANES : (d + 1) * LANES, :] = full[:, d * LANES : (d + 1) * LANES]

    each_channel(toeplitz_one, 2)
    weights_across(UP)
    weights_beside(GLU)
    weights_across(DOWN)
    weights_core(GLU)
    weights_beside(UP)

    def lane_tiles(ref, m):
        tiles = []
        for i in range(z.blocks):
            lo, hi = i * LANES, (i + 1) * LANES
            tile = None
            for k in range(lo // tok, -(-hi // tok)):
                piece = shifted(ref[m * z.slots + k].astype(f32), k * tok - lo)
                first = max(0, k * tok - lo)
                if tile is None:
                    tile = piece
                else:
                    tile = jnp.where(spot >= first, piece, tile)
            tiles.append(tile)
        return tiles

    def lane_pieces(tiles, m, ref):
        for k in range(z.slots):
            i, off = divmod(k * tok, LANES)
            piece = shifted(tiles[i], LANES - off)
            if off + tok > LANES:
                piece = jnp.where(spot < LANES - off, piece, shifted(tiles[i + 1], LANES - off))
            ref[m * z.slots + k] = piece.astype(bf16)

    def row_at(i, g):
        return (i * z.gr + g) * z.ch

    def masked_store(ref, base, m, i, tile):
        for q in range(z.segments):
            g = m * z.segments + q
            at = base + row_at(i, g)
            ref[at : at + z.ch, :] = tile * masks[i * z.gr + g : i * z.gr + g + 1, :]

    def masked_sum(m, i):
        total = None
        for q in range(z.segments):
            g = m * z.segments + q
            at = row_at(i, g)
            part = ys[at : at + z.ch, :] * masks[i * z.gr + g : i * z.gr + g + 1, :]
            total = part if total is None else total + part
        return total

    conv_rows = -(-(z.blocks * z.gr) // 8) * 8

    wait_bytes(rx1, recv.at[A1])
    for m in range(z.micros):
        for i, tile in enumerate(lane_tiles(rx1, m)):
            masked_store(xs, pad_rows, m, i, tile)

    def conv_one(h):
        parts = [
            xs[pl.ds((z.blocks - 1 - d) * z.gr * z.ch + h, conv_rows, stride=z.ch), :]
            for d in range(z.blocks)
        ]
        windows = jnp.concatenate(parts, axis=1).astype(bf16)
        ys[pl.ds(h, conv_rows, stride=z.ch), :] = dot(windows, near[h])

    each_channel(conv_one, ch)
    for m in range(z.micros):
        tiles = []
        for i in range(z.blocks):
            own = None
            for q in range(z.segments):
                at = pad_rows + row_at(i, m * z.segments + q)
                own = xs[at : at + z.ch, :] if own is None else own + xs[at : at + z.ch, :]
            tile = masked_sum(m, i) + skip[...] * own
            conv_out[m * z.blocks + i] = tile
            tiles.append(gelu(tile))
        lane_pieces(tiles, m, tx2)
    to_members(lambda p: tx2.at[slot_of(p)], rx2, me, A2)
    weights_beside(DOWN)
    weights_core(UP)
    weights_core(DOWN)
    wait_bytes(rx2, recv.at[A2])
    gated_s[...] = turn_in(rx2).astype(bf16)
    weights_here(GLU)
    gated = gated_s[...]
    value = dot_nt(gated, glu_all[0].reshape(width, width)) + full_row(vec_all, 5)
    sig = jax.nn.sigmoid(
        dot_nt(gated, glu_all[1].reshape(width, width)) + full_row(vec_all, 6)
    )
    val_s[...] = value
    sig_s[...] = sig
    pl.when(pipe > 0)(lambda: wait_bytes(res, recv.at[RES]))
    mid = res[...].astype(f32) + value * sig
    hat2, inv2 = norm_stats(mid)
    hat2_s[...] = hat2
    inv2_s[...] = jnp.broadcast_to(inv2, (rows, LANES))
    ffn_s[...] = (hat2 * full_row(vec_all, 2) + full_row(vec_all, 3)).astype(bf16)
    weights_here(UP)
    weights_here(DOWN)
    ffn_in = ffn_s[...]
    total = mid + full_row(vec_all, 4)
    for c in range(z.peers):
        offset = jnp.concatenate([vec_all[c, 7 + r : 8 + r, :] for r in range(per)], axis=1)
        hidden = dot(ffn_in, up_all[c]) + offset
        hidden_s[c] = hidden
        active = gelu(hidden).astype(bf16)
        act_s[c] = active
        total = total + dot(active, down_all[c])
    layer_out = jnp.where(row_ok, total, 0.0).astype(bf16)
    lay_s[...] = layer_out

    @pl.when(pipe < last)
    def _():
        wait_bytes(vec_next, recv.at[VECN])
        hat, inv = norm_stats(lay_s[...].astype(f32))
        hatn_s[...] = hat
        invn_s[...] = jnp.broadcast_to(inv, (rows, LANES))
        turn_out(hat * full_row(vec_next, 0) + full_row(vec_next, 1), tx1n)
        to_section(lambda p: tx1n.at[p], rx1, slot_me, A1, pipe + 1)
        remote(lay_s, res, RES, place(chan, data, pipe + 1)).start()

    def forward_rows():
        to_peers(lambda c: gated_s, ga, GA)
        to_peers(lambda c: ffn_s, fi, FI)
        to_peers(lambda c: act_s.at[c], ac, AC)

    def backward_rows():
        to_peers(lambda c: gtop, bg, BG)
        to_peers(lambda c: gh_s.at[c], gh, GH)
        to_peers(lambda c: gp_s.at[c], gp, GP)

    turn_out(lay_s[...].astype(f32), lay_t)

    @pl.when(pipe < last)
    def _():
        to_peers(lambda c: lay_t.at[c], hid_rx, HID)
        forward_rows()

    @pl.when(pipe == last)
    def _():
        wait_bytes(cot_rx, recv.at[COT])
        gtop[...] = jnp.where(row_ok, turn_in(cot_rx), 0.0).astype(bf16)

    @pl.when(pipe < last)
    def _():
        wait_bytes(mid_rx, recv.at[MID])
        wait_bytes(rx4n, recv.at[A4N])
        grad_in = jnp.where(row_ok, turn_in(rx4n), 0.0)
        hat = hatn_s[...]
        grad_res = mid_rx[...] + norm_back(
            grad_in, hat, invn_s[:, 0:1], full_row(vec_next, 0)
        )
        gtop[...] = grad_res.astype(bf16)
        pair = (
            jnp.sum(grad_in * hat, axis=0, keepdims=True),
            jnp.sum(grad_in, axis=0, keepdims=True),
        )
        for c in range(z.peers):
            for r, row in enumerate(pair):
                vgn_s[c, r : r + 1, :] = row[:, (c // 2) * LANES : (c // 2 + 1) * LANES]

    grad_low = gtop[...]
    grad_top = grad_low.astype(f32)
    grad_ffn = None
    for c in range(z.peers):
        grad_active = dot_nt(grad_low, down_all[c])
        grad_hidden = (grad_active * gelu_slope(hidden_s[c])).astype(bf16)
        gh_s[c] = grad_hidden
        part = dot_nt(grad_hidden, up_all[c])
        grad_ffn = part if grad_ffn is None else grad_ffn + part
    hat2 = hat2_s[...]
    grad_mid = grad_top + norm_back(grad_ffn, hat2, inv2_s[:, 0:1], full_row(vec_all, 2))
    mid_s[...] = grad_mid
    sig = sig_s[...]
    grad_value = grad_mid * sig
    grad_gate = grad_value * val_s[...] * (1.0 - sig)
    grad_gated = dot(grad_value.astype(bf16), glu_all[0].reshape(width, width)) + dot(
        grad_gate.astype(bf16), glu_all[1].reshape(width, width)
    )
    turn_out(grad_gated, tx3)
    to_members(lambda p: tx3.at[p], rx3, slot_me, A3)
    for j in range(z.peers // 2):
        gv = grad_value[:, j * LANES : (j + 1) * LANES]
        gg = shifted(grad_gate[:, j * LANES : (j + 1) * LANES], LANES // 2)
        gp_s[2 * j] = jnp.where(first_half, gv, gg).astype(bf16)
        gp_s[2 * j + 1] = jnp.where(first_half, gg, gv).astype(bf16)
    pl.when(pipe > 0)(lambda: remote(mid_s, mid_rx, MID, place(chan, data, pipe - 1)).start())
    pl.when(pipe == 0)(backward_rows)

    @pl.when(pipe < last)
    def _():
        turn_out(gtop[...].astype(f32), ign_t)
        to_section_peers(lambda c: ign_t.at[c], ig_rx, IG, pipe + 1)
        to_section(lambda p: vgn_s.at[p // z.groups], vnrx, me, VGN, pipe + 1)

    wait_bytes(rx3, recv.at[A3])
    for m in range(z.micros):
        for i, tile in enumerate(lane_tiles(rx3, m)):
            masked_store(gs, 0, m, i, tile * gelu_slope(conv_out[m * z.blocks + i]))

    def back_one(h):
        parts = [
            gs[pl.ds(d * z.gr * z.ch + h, conv_rows, stride=z.ch), :] for d in range(z.blocks)
        ]
        windows = jnp.concatenate(parts, axis=1).astype(bf16)
        ys[pl.ds(h, conv_rows, stride=z.ch), :] = dot_nt(windows, far[h])

    each_channel(back_one, ch)
    for m in range(z.micros):
        tiles = []
        for i in range(z.blocks):
            own = None
            for q in range(z.segments):
                at = row_at(i, m * z.segments + q)
                own = gs[at : at + z.ch, :] if own is None else own + gs[at : at + z.ch, :]
            tiles.append(masked_sum(m, i) + skip[...] * own)
        lane_pieces(tiles, m, tx4)

    @pl.when(pipe == 0)
    def _():
        to_members(lambda p: tx4.at[slot_of(p)], rx4, me, A4)

    @pl.when(pipe > 0)
    def _():
        to_section(lambda p: tx4.at[slot_of(p)], rx4n, me, A4N, pipe - 1)
        backward_rows()

    @pl.when(pipe == last)
    def _():
        to_peers(lambda c: lay_t.at[c], hid_rx, HID)
        forward_rows()

    def lag_one(h):
        x = xs[pl.ds(pad_rows + h, conv_rows, stride=z.ch), :]
        parts = [
            gs[pl.ds(d * z.gr * z.ch + h, conv_rows, stride=z.ch), :] for d in range(z.blocks)
        ]
        prod = dot_tn(x.astype(bf16), jnp.concatenate(parts, axis=1).astype(bf16))
        prod = jnp.concatenate([prod, jnp.zeros((LANES, LANES), f32)], axis=1)
        size = LANES // 2
        while size >= 8:
            prod = prod[:size] + shifted(prod[size:], wide - size)
            size //= 2
        row = prod[0:1]
        for a in range(1, 8):
            row = row + shifted(prod[a : a + 1], wide - a)
        lag_s[pl.ds(h, 1), :] = row

    each_channel(lag_one, 4)

    @pl.when(pipe == 0)
    def _():
        wait_bytes(rx4, recv.at[A4])
        grad_in = jnp.where(row_ok, turn_in(rx4), 0.0)
        hat = hat1_s[...]
        grad_res = mid_s[...] + norm_back(grad_in, hat, inv1_s[:, 0:1], full_row(vec_all, 0))
        turn_out(grad_res, ig_t)
        to_peers(lambda c: ig_t.at[c], ig_rx, IG)
        pair = (
            jnp.sum(grad_in * hat, axis=0, keepdims=True),
            jnp.sum(grad_in, axis=0, keepdims=True),
        )
        for c in range(z.peers):
            for r, row in enumerate(pair):
                vg0_s[c, r : r + 1, :] = row[:, (c // 2) * LANES : (c // 2 + 1) * LANES]
        to_members(lambda p: vg0_s.at[p // z.groups], vnrx, me, VGN)

    rows_of = [
        jnp.sum(grad_ffn * hat2, axis=0, keepdims=True),
        jnp.sum(grad_ffn, axis=0, keepdims=True),
        jnp.sum(grad_top, axis=0, keepdims=True),
    ]
    for c in range(z.peers):
        j = c // 2
        for r, row in enumerate(rows_of):
            vg_s[c, r : r + 1, :] = row[:, j * LANES : (j + 1) * LANES]
        vg_s[c, 3:4, :] = jnp.sum(gp_s[c].astype(f32), axis=0, keepdims=True)
        up_row = jnp.sum(gh_s[c].astype(f32), axis=0, keepdims=True)
        for r in range(per):
            vg_s[c, 4 + r : 5 + r, :] = up_row[:, r * LANES : (r + 1) * LANES]
    to_members(lambda p: vg_s.at[p // z.groups], vrx, me, VG)
    many = z.peers * rows
    grads = (
        (ac, AC, bg, BG, z.hid, width, pdown, kdown, sdown, ldown, ddown),
        (fi, FI, gh, GH, width, z.hid, pup, kup, sup, lup, dup),
        (gp, GP, ga, GA, 2 * z.cw, width, pglu, kglu, sglu, lglu, dglu),
    )
    for t, (left, lp, right, rp, n_left, n_right, part, krx, *_) in enumerate(grads):
        wait_bytes(left, recv.at[lp])
        wait_bytes(right, recv.at[rp])
        part[...] = dot_tn(left[...].reshape(many, n_left), right[...].reshape(many, n_right))
        half = n_left // 2
        other = pl.ds(pl.multiple_of((1 - core) * half, half), half)
        remote(part.at[other], krx, GRADS + 3 * t, sibling).start()
    for t, (_, _, _, _, n_left, _, part, krx, lsend, lrx, _) in enumerate(grads):
        half = n_left // 2
        own = pl.ds(pl.multiple_of(core * half, half), half)
        wait_bytes(krx, recv.at[GRADS + 3 * t])
        lsend[...] = (part[own, :] + krx[...]).astype(bf16)
        remote(lsend, lrx, GRADS + 3 * t + 1, across).start()

    both = dot_nt(high_low(lag_s[:, 0 : z.length]), table[...])
    grad_spec = both[0:ch] + both[ch : 2 * ch]
    gk = (grad_spec[:, 0:padded], grad_spec[:, padded : 2 * padded])
    y_all, ms, cross, over = moments()
    g_top = times(conj(over), gk)
    g_top = (-cosine * g_top[0], -cosine * g_top[1])
    g_low = times(conj(times(times(cross, over), over)), gk)
    g_three = (cosine * cosine * g_low[0], cosine * cosine * g_low[1])
    g_ms = [gk, times(conj(ms[2]), g_top), times(conj(ms[1]), g_top), g_three]
    g_rise = None
    for v, (g_r, g_i) in enumerate(g_ms):
        gsum_s[v] = 2.0 * cosine * g_r
        gsum_s[4 + v] = -2.0 * cosine * g_i
        gsum_s[8 + v] = 2.0 * y_all * g_i
        gsum_s[12 + v] = 2.0 * y_all * g_r
        part = 2.0 * (sums_s[12 + v] * g_r + sums_s[8 + v] * g_i)
        g_rise = part if g_rise is None else g_rise + part
    slope_s[...] = g_rise
    gcol_s[...] = jnp.zeros(gcol_s.shape, f32)
    gstep_s[...] = jnp.zeros(gstep_s.shape, f32)

    def mode_one(h):
        double, y, cy, u, w = modes_at(h)
        column = column_of(0, h)
        gu, gw = 0.0, 0.0
        acc = gcol_s[0]
        for v in range(4):
            a = column[:, v * ch : v * ch + 1]
            b = column[:, (4 + v) * ch : (4 + v) * ch + 1]
            au, aw = gsum_s[v, pl.ds(h, 1), :], gsum_s[4 + v, pl.ds(h, 1), :]
            bu, bw = gsum_s[8 + v, pl.ds(h, 1), :], gsum_s[12 + v, pl.ds(h, 1), :]
            gu = gu + a * au + b * bu
            gw = gw + a * aw + b * bw
            ga_col = jnp.sum(u * au + w * aw, axis=1, keepdims=True)
            gb_col = jnp.sum(u * bu + w * bw, axis=1, keepdims=True)
            acc = jnp.where(spot == v * ch + h, ga_col, acc)
            acc = jnp.where(spot == (4 + v) * ch + h, gb_col, acc)
        gcol_s[0] = acc
        even, cross_uw = u * u - w * w, 2.0 * u * w
        g_den_r = -(even * gu + cross_uw * gw)
        g_den_i = even * gw - cross_uw * gu
        ge = jnp.sum(cosine * cosine * g_den_r, axis=1, keepdims=True)
        gf = jnp.sum(cy * g_den_i, axis=1, keepdims=True)
        acc = jnp.where(spot == h, ge, gcol_s[1])
        gcol_s[1] = jnp.where(spot == ch + h, gf, acc)
        gy = slope_s[pl.ds(h, 1), :] + jnp.sum(
            double * cosine * g_den_i - 2.0 * y * g_den_r, axis=0, keepdims=True
        )
        total_y = jnp.sum(y * gy, axis=1, keepdims=True)
        gstep_s[0:1, :] = jnp.where(spot == h, -total_y, gstep_s[0:1, :])

    each_channel(mode_one, 2)

    def unpacked(k, i):
        return shifted(gcol_s[k], LANES - i * ch)

    g_square, g_double = unpacked(1, 0), unpacked(1, 1)
    g_decay = 2.0 * decay * g_square + 2.0 * g_double
    g_rate = 2.0 * rate * g_square
    g_pairs = []
    for v, (v_r, v_i) in enumerate(pairs):
        g_alpha, g_beta = unpacked(0, v), unpacked(0, 4 + v)
        g_decay = g_decay + g_alpha * v_r
        if v_i is not None:
            g_rate = g_rate - g_alpha * v_i
        g_pairs.append((decay * g_alpha + g_beta, -rate * g_alpha))
    c_b, c_p, p_b = g_pairs[0], g_pairs[1], g_pairs[2]
    p_p = g_pairs[3][0]
    rank, into, out = (rank_r, rank_i), (in_r, in_i), (out_r, out_i)

    def plus(*terms):
        return sum(t[0] for t in terms), sum(t[1] for t in terms)

    g_out = plus(times(conj(into), c_b), times(conj(rank), c_p))
    g_in = plus(times(conj(out), c_b), times(rank, p_b))
    g_rank = plus(
        times(conj(out), c_p),
        times(into, conj(p_b)),
        (2.0 * rank_r * p_p, 2.0 * rank_i * p_p),
    )
    modes_tx[0:nh, :] = packed([g_decay, g_rate, *g_rank, *g_in, *g_out])
    modes_tx[nh : nh + 8, :] = gstep_s[...]
    skip_row = jnp.sum(jnp.where(diagonal, lag_s[:, 0:1], 0.0), axis=0, keepdims=True)
    modes_tx[nh + 1 : nh + 2, :] = skip_row
    for k in range(1, z.groups):
        remote(modes_tx, modes_rx.at[data], MODES, place(chan, lax.rem(data + k, z.groups))).start()
    pltpu.make_async_copy(modes_tx, modes_rx.at[data], recv.at[MODES]).start()

    for t, (_, _, _, _, n_left, _, _, _, lsend, lrx, final) in enumerate(grads):
        half = n_left // 2
        own = pl.ds(pl.multiple_of(core * half, half), half)
        wait_bytes(lrx, recv.at[GRADS + 3 * t + 1])
        final[own, :] = lsend[...].astype(f32) + lrx[...].astype(f32)
        remote(final.at[own], final.at[own], GRADS + 3 * t + 2, sibling).start()

    def collect(source, target):
        count = tok * z.quarters
        for m in range(z.micros):
            tiles = []
            for i in range(-(-count // LANES)):
                lo, hi = i * LANES, min((i + 1) * LANES, count)
                tile = None
                for q in range(lo // tok, -(-hi // tok)):
                    piece = shifted(source[m * z.quarters + q].astype(f32), q * tok - lo)
                    first = max(0, q * tok - lo)
                    tile = piece if tile is None else jnp.where(spot >= first, piece, tile)
                tiles.append(tile)
            target[m] = jnp.concatenate(tiles, axis=1)[:, 0:count].astype(bf16)

    wait_bytes(hid_rx, recv.at[HID])
    collect(hid_rx, hid_out)
    wait_bytes(ig_rx, recv.at[IG])
    collect(ig_rx, ig_out)
    wait_bytes(vrx, recv.at[VG])
    wait_bytes(vnrx, recv.at[VGN])
    summed, summed_one = vrx[0], vnrx[0]
    for p in range(1, z.members):
        summed = summed + vrx[p]
        summed_one = summed_one + vnrx[p]
    upb_out[...] = jnp.concatenate([summed[4 + r : 5 + r, :] for r in range(per)], axis=1)
    summed, summed_one = own_half(summed), own_half(summed_one)
    for r in range(3):
        ffn_out[r] = summed[r : r + 1, 0 : z.cw]
    glub_out[0:1, :] = summed[3:4, 0 : z.cw]
    glub_out[1:2, :] = shifted(summed[3:4], LANES // 2)[:, 0 : z.cw]
    vec_out[0:2, :] = summed_one[0:2, 0 : z.cw]
    wait_bytes(modes_rx, recv.at[MODES])

    def over_groups(take):
        total = take(0)
        for d in range(1, z.groups):
            total = jnp.where(spot // ch == d, take(d), total)
        return total[:, 0 : z.cw]

    for p in range(8):
        modes_out[p] = over_groups(
            lambda d: shifted(modes_rx[d, 0:nh, :], (d - p) * ch)
        )
    for r in range(2):
        vec_out[2 + r : 3 + r, :] = over_groups(
            lambda d: shifted(modes_rx[d, nh + r : nh + r + 1, :], d * ch)
        )
    for t, (_, _, _, _, n_left, _, _, _, _, _, final) in enumerate(grads):
        half = n_left // 2
        other = pl.ds(pl.multiple_of((1 - core) * half, half), half)
        wait_bytes(final.at[other], recv.at[GRADS + 3 * t + 2])
    glu_out[0] = dglu[pl.ds(pl.multiple_of(odd * z.cw, z.cw), z.cw), :]
    glu_out[1] = dglu[pl.ds(pl.multiple_of((1 - odd) * z.cw, z.cw), z.cw), :]

    for t in (GLU, UP, DOWN):
        weights_sent(t)
    for ref, phase in (
        (vec_all, VEC), (hid_rx, HID), (ga, GA), (fi, FI), (ac, AC), (bg, BG), (gh, GH), (gp, GP),
    ):
        wait_bytes(ref.at[pl.ds(0, z.peers - 1)], send.at[phase])
    for ref, phase in ((rx2, A2), (rx3, A3), (vrx, VG)):
        wait_bytes(ref.at[pl.ds(0, z.members - 1)], send.at[phase])
    wait_bytes(modes_rx.at[pl.ds(0, z.groups - 1)], send.at[MODES])
    for t, (_, _, _, _, n_left, _, _, krx, lsend, _, final) in enumerate(grads):
        wait_bytes(krx, send.at[GRADS + 3 * t])
        wait_bytes(lsend, send.at[GRADS + 3 * t + 1])
        wait_bytes(final.at[pl.ds(0, n_left // 2)], send.at[GRADS + 3 * t + 2])

    @pl.when(pipe == 0)
    def _():
        wait_bytes(tok_rx.at[pl.ds(0, z.peers - 1)], send.at[TOK])
        wait_bytes(ig_rx.at[pl.ds(0, z.peers - 1)], send.at[IG])
        for ref, phase in ((rx1, A1), (rx4, A4), (vnrx, VGN)):
            wait_bytes(ref.at[pl.ds(0, z.members - 1)], send.at[phase])

    @pl.when(pipe == last)
    def _():
        wait_bytes(cot_rx.at[pl.ds(0, z.peers - 1)], send.at[COT])

    @pl.when(pipe < last)
    def _():
        for ref, phase in ((rx1, A1), (lay_s, RES), (ig_rx, IG), (vnrx, VGN)):
            wait_bytes(ref, send.at[phase])

    @pl.when(pipe > 0)
    def _():
        for ref, phase in ((vec_all, VECN), (mid_s, MID), (rx4, A4N)):
            wait_bytes(ref, send.at[phase])


def finish_kernel(*refs):
    count = (len(refs) - 1) // 3
    sems = refs[-1]
    sources, targets, held = refs[:count], refs[count : 2 * count], refs[2 * count : -1]
    loads = [pltpu.make_async_copy(sources[i], held[i], sems.at[i]) for i in range(count)]
    stores = [
        pltpu.make_async_copy(held[i], targets[i], sems.at[count + i]) for i in range(count)
    ]
    for load in loads:
        load.start()
    for load, store in zip(loads, stores):
        load.wait()
        store.start()
    for store in stores:
        store.wait()


def body(
    tokens,
    seq_lengths,
    out_cot,
    s4_vectors,
    s4_modes,
    glu_weight,
    glu_bias,
    ffn_vectors,
    up_weight,
    up_bias,
    down_weight,
):
    micros, tok_rows, chan_width = tokens.shape
    width = glu_weight.shape[1]
    hidden = up_weight.shape[2]
    z = Sizes(
        lax.axis_size("pipe"), lax.axis_size("chan"), lax.axis_size("dp"),
        tok_rows, chan_width, width, hidden,
    )
    length = z.length
    padded = -(-(length // 2 + 1) // LANES) * LANES
    nh = s4_modes.shape[3]
    table = jnp.asarray(fourier_table(length, padded).astype(ml_dtypes.bfloat16))
    angles = jnp.asarray(half_angles(length, padded))

    vmem = pl.BlockSpec(memory_space=pltpu.VMEM)
    smem = pl.BlockSpec(memory_space=pltpu.SMEM)
    anywhere = pl.BlockSpec(memory_space=pl.ANY)
    n, r, w, ch = z.peers, z.rows, width, z.ch

    def s(shape, kind=f32):
        return jax.ShapeDtypeStruct(shape, kind)

    def v(shape, kind=bf16):
        return pltpu.VMEM(shape, kind)

    conv_rows = -(-(z.blocks * z.gr) // 8) * 8
    wide = (z.blocks + 1) * LANES
    rows_full, rows_wide, side = v((r, w)), v((r, w), f32), v((r, LANES), f32)
    peer_tiles, exchange = v((n, chan_width, LANES)), v((z.members, z.ch, LANES))
    small = v((n, 8, LANES), f32)
    results = (
        s((micros, chan_width, tok_rows), bf16), s((micros, chan_width, tok_rows), bf16),
        s((4, chan_width)), s((8, nh, chan_width)), s((2, chan_width, w)),
        s((2, chan_width)), s((3, 1, chan_width)), s((w, hidden)), s((1, hidden)),
        s((hidden, w)),
    )
    raw = pl.pallas_call(
        lambda *refs: main_kernel(z, *refs),
        out_shape=results,
        in_specs=[smem] + [vmem] * 11 + [anywhere],
        out_specs=[vmem] * 10,
        scratch_shapes=[
            peer_tiles, peer_tiles, v((16, LANES), f32), v((ch, length, LANES)),
            v((ch, LANES, length)), v((ch, LANES), f32), v((conv_rows, LANES), f32),
            peer_tiles, peer_tiles, v((z.stack, LANES), f32), v((z.stack, LANES), f32),
            v((2 * padded, length)), v((2, nh, LANES), f32),
            v((ch, LANES), f32), v((16, ch, padded), f32), v((16, ch, padded), f32),
            v((ch, padded), f32), v((ch, wide), f32), v((ch, wide), f32),
            v((2, nh, LANES), f32), v((8, LANES), f32),
            v((nh + 8, LANES), f32), v((z.groups, nh + 8, LANES), f32),
            v((2 * chan_width, w), f32), v((w, hidden), f32), v((hidden, w), f32),
            v((chan_width, w), f32), v((w // 2, hidden), f32), v((hidden // 2, w), f32),
            v((chan_width, w)), v((w // 2, hidden)), v((hidden // 2, w)),
            v((chan_width, w)), v((w // 2, hidden)), v((hidden // 2, w)),
            v((2 * chan_width, w), f32),
            v((n, 16, LANES), f32), v((n, 16, LANES), f32),
            v((2, n, chan_width, w)), v((n, w, hidden)),
            v((n, hidden, w)), peer_tiles, peer_tiles, rows_full, rows_full,
        ]
        + [exchange] * 10
        + [
            v((z.micros * z.blocks, z.ch, LANES), f32), v((conv_rows * z.ch, LANES), f32),
            rows_wide, side, rows_wide, side, rows_wide, side,
            rows_wide, rows_wide, v((n, r, hidden), f32),
            rows_full, rows_full, v((n, r, hidden)), v((n, r, hidden)), v((n, r, LANES)),
            rows_full, peer_tiles, peer_tiles, peer_tiles, rows_wide, rows_wide,
            small, small, small,
            v((n, r, w)), v((n, r, w)), v((n, r, hidden)), v((n, r, w)), v((n, r, hidden)),
            v((n, r, LANES)), v((z.members, 8, LANES), f32), v((z.members, 8, LANES), f32),
            pltpu.SemaphoreType.DMA((50,)), pltpu.SemaphoreType.DMA((50,)),
        ],
        compiler_params=pltpu.CompilerParams(
            collective_id=0, has_side_effects=True, vmem_limit_bytes=60 * 2**20
        ),
        name="layers",
    )(
        seq_lengths, tokens.transpose(0, 2, 1), out_cot.transpose(0, 2, 1), s4_vectors[0],
        s4_modes[0].transpose(0, 2, 1), glu_weight[0].transpose(1, 2, 0), glu_bias[0],
        ffn_vectors.transpose(1, 0, 2), up_weight[0], up_bias, down_weight[0], angles, table,
    )
    hid, ig, vec, modes, dglu, glub, ffn, dup, upb, ddown = pl.pallas_call(
        finish_kernel,
        out_shape=results,
        in_specs=[anywhere] * 10,
        out_specs=[anywhere] * 10,
        scratch_shapes=[pltpu.VMEM(x.shape, x.dtype) for x in results]
        + [pltpu.SemaphoreType.DMA((20,))],
        compiler_params=pltpu.CompilerParams(vmem_limit_bytes=60 * 2**20),
        name="finish",
    )(*raw)
    return (
        hid.transpose(0, 2, 1)[None], ig.transpose(0, 2, 1)[None], vec[None],
        modes.transpose(0, 2, 1)[None], dglu.transpose(2, 0, 1)[None], glub[None],
        ffn.transpose(1, 0, 2), dup[None], upb, ddown[None],
    )


def solution(mesh):
    placed = (
        P(None, "dp", "chan"),
        P(),
        P(None, "dp", "chan"),
        P("pipe", None, "chan"),
        P("pipe", None, "chan", None),
        P("pipe", None, None, "chan"),
        P("pipe", None, "chan"),
        P("pipe", None, "chan"),
        P("pipe", None, "chan"),
        P("pipe", "chan"),
        P("pipe", "chan", None),
    )
    return jax.shard_map(
        body,
        mesh=mesh,
        in_specs=placed,
        out_specs=(
            P("pipe", None, "dp", "chan"),
            P("pipe", None, "dp", "chan"),
            P("pipe", None, "chan"),
            P("pipe", None, "chan", None),
            P("pipe", None, None, "chan"),
            P("pipe", None, "chan"),
            P("pipe", None, "chan"),
            P("pipe", None, "chan"),
            P("pipe", "chan"),
            P("pipe", "chan", None),
        ),
        check_vma=False,
    )
```

```python
import math

import jax
import jax.numpy as jnp
import ml_dtypes
import numpy as np
from jax import lax
from jax.experimental import pallas as pl
from jax.experimental.pallas import tpu as pltpu
from jax.sharding import PartitionSpec as P

norm_eps = 1e-05
f32 = jnp.float32
bf16 = jnp.bfloat16
LANES = 128


def fourier_table(length, padded):
    half = length // 2
    freq = np.arange(padded, dtype=np.int64)[:, None]
    time = np.arange(length, dtype=np.int64)[None, :]
    angle = (freq * (2 * time + 1) % (2 * length)) * (np.pi / length)
    weight = np.where(freq <= half, np.where((freq == 0) | (freq == half), 1.0, 2.0), 0.0) / length
    table = np.concatenate([np.cos(angle) * weight, -np.sin(angle) * weight], axis=0)
    return table.astype(np.float32)


def half_angles(length, padded):
    angle = np.minimum(np.arange(padded), length // 2) * (np.pi / length)
    rows = np.zeros((8, padded), np.float32)
    rows[0] = np.where(np.arange(padded) < length // 2, np.cos(angle), 0.0)
    rows[1] = np.sin(angle)
    return rows


def shifted(x, by):
    size = x.shape[-1]
    by = by % size
    if by == 0:
        return x
    return pltpu.roll(x, by, x.ndim - 1)


def gelu(x):
    return 0.5 * x * (1.0 + jnp.tanh(math.sqrt(2.0 / math.pi) * (x + 0.044715 * x * x * x)))


def gelu_slope(x):
    scale = math.sqrt(2.0 / math.pi)
    t = jnp.tanh(scale * (x + 0.044715 * x * x * x))
    return 0.5 * (1.0 + t) + 0.5 * x * (1.0 - t * t) * scale * (1.0 + 3.0 * 0.044715 * x * x)


def dot(a, b):
    return lax.dot_general(a, b, (((1,), (0,)), ((), ())), preferred_element_type=f32)


def dot_nt(a, b):
    return lax.dot_general(a, b, (((1,), (1,)), ((), ())), preferred_element_type=f32)


def dot_tn(a, b):
    return lax.dot_general(a, b, (((0,), (0,)), ((), ())), preferred_element_type=f32)


class Sizes:
    def __init__(self, sections, peers, groups, tok_rows, chan_width, model_width, hidden):
        self.sections, self.peers, self.groups = sections, peers, groups
        self.micros = 2
        self.segments = 2
        self.quarters = peers // self.micros
        self.tok = tok_rows // self.quarters
        self.rows = -(-self.tok // 16) * 16
        self.length = tok_rows * groups
        self.blocks = self.length // LANES
        self.width = model_width
        self.cw = chan_width
        self.hid = hidden
        self.members = peers * groups
        self.ch = model_width // self.members
        self.slots = self.quarters * groups
        self.conv_rows = -(-(self.blocks * self.segments) // 8) * 8
        spare = -(-(self.conv_rows - self.blocks * self.segments) // self.segments)
        self.stack = (2 * self.blocks - 1 + spare) * self.segments * self.ch


def main_kernel(z, *refs):
    (
        lengths, tokens, out_cot, vectors, modes, glu_loc, glu_bias, ffn_vec, up_loc, up_bias,
        down_loc, angles, table_in,
    ) = refs[:13]
    (
        hid_out, ig_out, vec_out, modes_out, glu_out, glub_out, ffn_out, dup, upb_out, ddown,
    ) = refs[13:23]
    (
        tok_tx, cot_tx, vec_tx, near, far, skip, masks, hid_rx, ig_rx, xs, gs,
        table, cols, rise_s, sums_s, uw_s, guw_s, rest_s, gsum_s, slope_s, kern_s, lag_s, gcol_s, gstep_s,
        modes_tx, modes_rx, pglu, pup, pdown, kglu, kup, kdown, sglu, sup, sdown,
        lglu, lup, ldown, dglu,
        vec_all, vec_next, glu_all, up_all, down_all, tok_rx, cot_rx, res, gtop,
        tx1, tx1n, rx1, tx2, rx2, tx3, rx3, tx4, rx4, rx4n,
        conv_out, ys, hat1_s, inv1_s, hatn_s, invn_s, hat2_s, inv2_s, val_s, sig_s, hidden_s,
        gated_s, ffn_s, act_s, gh_s, gp_s, lay_s, lay_t, ig_t, ign_t, mid_s, mid_rx,
        vg_s, vgn_s, vg0_s, ga, fi, ac, bg, gh, gp, vrx, vnrx, send, recv,
    ) = refs[23:]
    pipe = lax.axis_index("pipe")
    chan = lax.axis_index("chan")
    data = lax.axis_index("dp")
    last = z.sections - 1
    me = chan * z.groups + data
    slot_me = (chan // z.quarters) * z.slots + data * z.quarters + lax.rem(chan, z.quarters)
    rows, width, tok = z.rows, z.width, z.tok
    spot = lax.broadcasted_iota(jnp.int32, (1, LANES), 1)
    first_half = spot < (LANES // 2)
    row_ok = lax.broadcasted_iota(jnp.int32, (rows, 1), 0) < tok
    odd = lax.rem(chan, 2)
    per = z.hid // LANES

    high, deep = chan // z.quarters, lax.rem(chan, z.quarters)
    side, core = data // 2, lax.rem(data, 2)
    height = 2 * high + side

    def slot_of(p):
        c, d = p // z.groups, lax.rem(p, z.groups)
        return (c // z.quarters) * z.slots + d * z.quarters + lax.rem(c, z.quarters)

    def place(c, d, section=None):
        return {"pipe": pipe if section is None else section, "chan": c, "dp": d}

    def member(p, section=None):
        return place(p // z.groups, lax.rem(p, z.groups), section)

    def remote(src, dst, phase, where):
        return pltpu.make_async_remote_copy(
            src_ref=src,
            dst_ref=dst,
            send_sem=send.at[phase],
            recv_sem=recv.at[phase],
            device_id=where,
            device_id_type=pl.DeviceIdType.MESH,
        )

    def wait_bytes(ref, sem):
        pltpu.make_async_copy(ref, ref, sem).wait()

    def to_peers(src_of, dst, phase):
        def step(k, carry):
            c = lax.rem(chan + k, z.peers)
            remote(src_of(c), dst.at[chan], phase, place(c, data)).start()
            return carry

        lax.fori_loop(1, z.peers, step, 0)
        pltpu.make_async_copy(src_of(chan), dst.at[chan], recv.at[phase]).start()

    def far_first(i):
        return lax.rem(2 + i + (i // 2) * (2 * i - 3), 4)

    def number(y, depth, core_there):
        return ((y // 2) * z.quarters + depth) * z.groups + lax.rem(y, 2) * 2 + core_there

    def to_all(src_of, dst, slot, phase, section=None):
        def chip(k):
            y = lax.rem(height + far_first(k // 4), 4)
            return y, lax.rem(deep + far_first(lax.rem(k, 4)), 4)

        def step(k, carry):
            y, depth = chip(k)
            for c in range(2):
                p = number(y, depth, c)
                remote(src_of(p), dst.at[slot], phase, member(p, section)).start()
            return carry

        chips = z.members // 2
        lax.fori_loop(0, chips if section is not None else chips - 1, step, 0)
        if section is None:
            p = number(height, deep, 1 - core)
            remote(src_of(p), dst.at[slot], phase, member(p)).start()
            pltpu.make_async_copy(src_of(me), dst.at[slot], recv.at[phase]).start()

    def to_members(src_of, dst, slot, phase):
        to_all(src_of, dst, slot, phase)

    def to_section(src_of, dst, slot, phase, section):
        to_all(src_of, dst, slot, phase, section)

    def to_micro(m, source, dst, phase, section=None):
        near_by = jnp.where(own_micro == m, 1, 0)

        def send_to(p):
            remote(source.at[slot_of(p)], dst.at[me], phase, member(p, section)).start()

        def chip(k):
            y = 2 * m + lax.rem(side + near_by + k // 4, 2)
            return y, lax.rem(deep + far_first(lax.rem(k, 4)), 4)

        def step(k, carry):
            y, depth = chip(k)
            for c in range(2):
                send_to(number(y, depth, c))
            return carry

        lax.fori_loop(0, z.slots // 2 - 1, step, 0)
        if section is not None:
            step(z.slots // 2 - 1, 0)
            return

        @pl.when(own_micro == m)
        def _():
            send_to(number(height, deep, 1 - core))
            block = source.at[slot_of(me)]
            pltpu.make_async_copy(block, dst.at[me], recv.at[phase]).start()

        @pl.when(own_micro != m)
        def _():
            step(z.slots // 2 - 1, 0)

    def to_section_peers(src_of, dst, phase, section):
        def step(k, carry):
            c = lax.rem(chan + k, z.peers)
            remote(src_of(c), dst.at[chan], phase, place(c, data, section)).start()
            return carry

        lax.fori_loop(0, z.peers, step, 0)

    (
        VEC, VECN, TOK, COT, A2, A4, A4N, RES, MID, HID, IG, GA, FI, AC, BG, GH, GP, VG,
        VGN, TABLE, MODES,
    ) = range(21)
    A1, A3, GLU, UP, DOWN, GRADS = 21, 23, 25, 31, 37, 43
    own_micro = chan // z.quarters

    own_side, far_side = high * z.quarters, (1 - high) * z.quarters
    sibling, across = place(chan, side * 2 + 1 - core), place(chan, (1 - side) * 2 + core)

    def piece_of(t, c, count, part=None):
        if t == GLU:
            if part is None:
                return glu_all.at[core, pl.ds(c, count)]
            fourth = z.cw // 2
            start = pl.multiple_of(part * fourth, fourth)
            return glu_all.at[core, pl.ds(c, count), pl.ds(start, fourth)]
        loc, whole = (up_loc, up_all) if t == UP else (down_loc, down_all)
        half = loc.shape[0] // 2
        fourth = half // 2
        if part is None:
            return whole.at[pl.ds(c, count), pl.ds(pl.multiple_of(core * half, half), half)]
        start = pl.multiple_of(core * half + part * fourth, fourth)
        return whole.at[pl.ds(c, count), pl.ds(start, fourth)]

    def weights_out(t):
        if t == GLU:
            loc, whole, half = glu_loc, glu_all.at[:, chan], glu_loc.at[core]
            fourth = z.cw // 2
            quarter = half.at[pl.ds(pl.multiple_of(side * fourth, fourth), fourth)]
        else:
            loc, whole = (up_loc, up_all) if t == UP else (down_loc, down_all)
            size = loc.shape[0] // 2
            fourth = size // 2
            whole, half = whole.at[chan], loc.at[pl.ds(pl.multiple_of(core * size, size), size)]
            start = pl.multiple_of(core * size + side * fourth, fourth)
            quarter = loc.at[pl.ds(start, fourth)]
        pltpu.make_async_copy(loc, whole, recv.at[t + 5]).start()
        there = piece_of(t, chan, 1, side).at[0]
        for k in range(z.quarters):
            c = far_side + lax.rem(deep + k, z.quarters)
            remote(quarter, there, t + 1, place(c, (1 - side) * 2 + core)).start()
        there = piece_of(t, chan, 1).at[0]
        for k in range(1, z.quarters):
            c = own_side + lax.rem(deep + k, z.quarters)
            remote(half, there, t, place(c, data)).start()

    def weights_beside(t):
        wait_bytes(piece_of(t, 0, z.quarters, 0), recv.at[t + 1])
        piece = piece_of(t, far_side, z.quarters, 1 - side)
        remote(piece, piece, t + 2, across).start()

    def weights_near(t):
        wait_bytes(piece_of(t, 0, z.quarters - 1), recv.at[t])
        for k in range(1, z.quarters):
            piece = piece_of(t, own_side + lax.rem(deep + k, z.quarters), 1)
            remote(piece, piece, t + 3, sibling).start()

    def weights_core(t):
        wait_bytes(piece_of(t, 0, z.quarters, 0), recv.at[t + 2])
        piece = piece_of(t, far_side, z.quarters)
        remote(piece, piece, t + 4, sibling).start()

    def weights_here(t):
        wait_bytes({GLU: glu_loc, UP: up_loc, DOWN: down_loc}[t], recv.at[t + 5])
        wait_bytes(piece_of(t, 0, z.quarters - 1), recv.at[t + 3])
        wait_bytes(piece_of(t, 0, z.quarters), recv.at[t + 4])

    def weights_sent(t):
        for stage, count, part in (
            (0, z.quarters - 1, None), (1, z.quarters, 0), (2, z.quarters, 0),
            (3, z.quarters - 1, None), (4, z.quarters, None),
        ):
            wait_bytes(piece_of(t, 0, count, part), send.at[t + stage])

    barrier = pltpu.get_barrier_semaphore()

    def greet(p, section):
        pl.semaphore_signal(
            barrier, inc=1, device_id=member(p, section), device_id_type=pl.DeviceIdType.MESH
        )

    def greet_own(k, carry):
        greet(lax.rem(me + k, z.members), None)
        return carry

    def greet_next(k, carry):
        greet(lax.rem(me + k, z.members), pipe + 1)
        return carry

    def greet_before(k, carry):
        greet(lax.rem(me + k, z.members), pipe - 1)
        return carry

    lax.fori_loop(1, z.members, greet_own, 0)

    @pl.when(pipe < last)
    def _():
        lax.fori_loop(0, z.members, greet_next, 0)

    @pl.when(pipe > 0)
    def _():
        lax.fori_loop(0, z.members, greet_before, 0)

    pltpu.make_async_copy(table_in, table, recv.at[TABLE]).start()

    def own_half(x):
        return pltpu.roll(x, odd * (LANES // 2), x.ndim - 1)

    def fill_blocks(source, target):
        count = z.tok * z.quarters
        over = -(-count // LANES) * LANES
        for m in range(z.micros):
            x = source[m].astype(f32)
            x = jnp.concatenate([x, jnp.zeros((z.cw, over - count), f32)], axis=1)
            for q in range(z.quarters):
                target[m * z.quarters + q] = shifted(x, over - q * tok)[:, 0:LANES].astype(bf16)

    vec_rows = [vectors[0:1, :], vectors[1:2, :]] + [ffn_vec[r] for r in range(3)]
    vec_rows += [glu_bias[0:1, :], glu_bias[1:2, :]]
    for r, row in enumerate(vec_rows):
        vec_tx[r : r + 1, :] = jnp.concatenate([row, row], axis=1)
    for r in range(per):
        vec_tx[7 + r : 8 + r, :] = up_bias[:, r * LANES : (r + 1) * LANES].astype(f32)
    pl.when(pipe == 0)(lambda: fill_blocks(tokens, tok_tx))
    pl.when(pipe == last)(lambda: fill_blocks(out_cot, cot_tx))

    ch, nh = z.ch, modes.shape[1]

    def own_lanes(x):
        x = jnp.concatenate([x, jnp.zeros((x.shape[0], LANES - z.cw), f32)], axis=1)
        return pltpu.roll(x, lax.rem(LANES - data * ch, LANES), 1)

    def packed(items):
        total = items[0]
        for i, item in enumerate(items[1:], 1):
            total = jnp.where(spot // ch == i, shifted(item, i * ch), total)
        return total

    decay, rate, rank_r, rank_i, in_r, in_i, out_r, out_i = (own_lanes(modes[p]) for p in range(8))
    pairs = [
        (out_r * in_r - out_i * in_i, out_r * in_i + out_i * in_r),
        (out_r * rank_r - out_i * rank_i, out_r * rank_i + out_i * rank_r),
        (rank_r * in_r + rank_i * in_i, rank_r * in_i - rank_i * in_r),
        (rank_r * rank_r + rank_i * rank_i, None),
    ]
    alphas = [
        decay * v_r if v_i is None else decay * v_r - rate * v_i for v_r, v_i in pairs
    ]
    cols[0] = packed(alphas + [v_r for v_r, v_i in pairs])
    cols[1] = packed([decay * decay + rate * rate, 2.0 * decay])
    own_vectors = own_lanes(vectors[...])
    diagonal = lax.broadcasted_iota(jnp.int32, (ch, LANES), 0) == lax.broadcasted_iota(
        jnp.int32, (ch, LANES), 1
    )

    def upright(row):
        column = jnp.sum(jnp.where(diagonal, row, 0.0), axis=1, keepdims=True)
        return jnp.broadcast_to(column, (ch, LANES))

    rise_s[...] = 2.0 * jnp.exp(-upright(own_vectors[2:3]))
    skip[...] = upright(own_vectors[3:4])
    cosine, sine = angles[0:1, :], angles[1:2, :]
    padded = angles.shape[1]

    def column_of(k, h):
        return pltpu.roll(cols[k], lax.rem(LANES - h, LANES), 1)

    def modes_at(h):
        two = column_of(1, h)
        square, double = two[:, 0:1], two[:, ch : ch + 1]
        y = rise_s[pl.ds(h, 1), 0:1] * sine
        cy = cosine * y
        den_r = square * (cosine * cosine) - y * y
        den_i = double * cy
        inverse = 1.0 / (den_r * den_r + den_i * den_i)
        return double, y, cy, den_r * inverse, den_i * inverse

    def cauchy_one(h):
        _, _, _, u, w = modes_at(h)
        at = pl.ds(pl.multiple_of(h * nh, nh), nh)
        uw_s[at, 0:padded] = u
        uw_s[at, padded : 2 * padded] = w
        column = column_of(0, h)
        for v in range(4):
            a = column[:, v * ch : v * ch + 1]
            b = column[:, (4 + v) * ch : (4 + v) * ch + 1]
            sums_s[v, pl.ds(h, 1), :] = jnp.sum(a * u, axis=0, keepdims=True)
            sums_s[4 + v, pl.ds(h, 1), :] = jnp.sum(a * w, axis=0, keepdims=True)
            sums_s[8 + v, pl.ds(h, 1), :] = jnp.sum(b * u, axis=0, keepdims=True)
            sums_s[12 + v, pl.ds(h, 1), :] = jnp.sum(b * w, axis=0, keepdims=True)

    def each_channel(one, unroll):
        def step(i, carry):
            for u in range(unroll):
                one(i * unroll + u)
            return carry

        if unroll == ch:
            step(0, 0)
        else:
            lax.fori_loop(0, ch // unroll, step, 0)

    def times(a, b):
        return a[0] * b[0] - a[1] * b[1], a[0] * b[1] + a[1] * b[0]

    def conj(a):
        return a[0], -a[1]

    def moments():
        y_all = rise_s[:, 0:1] * sine
        ms = [
            (
                2.0 * (cosine * sums_s[v] + y_all * sums_s[12 + v]),
                2.0 * (y_all * sums_s[8 + v] - cosine * sums_s[4 + v]),
            )
            for v in range(4)
        ]
        low_r, low_i = 1.0 + cosine * ms[3][0], cosine * ms[3][1]
        size = 1.0 / (low_r * low_r + low_i * low_i)
        return y_all, ms, times(ms[1], ms[2]), (low_r * size, -low_i * size)

    def high_low(x):
        high_part = x.astype(bf16)
        low_part = (x - high_part.astype(f32)).astype(bf16)
        return jnp.concatenate([high_part, low_part], axis=0)

    each_channel(cauchy_one, 4)
    pad_rows = (z.blocks - 1) * z.segments * z.ch
    data_rows = z.blocks * z.segments * z.ch
    for m in range(z.micros):
        at = m * z.stack
        xs[at : at + pad_rows, :] = jnp.zeros((pad_rows, LANES), f32)
        rest = z.stack - pad_rows - data_rows
        xs[at + z.stack - rest : at + z.stack, :] = jnp.zeros((rest, LANES), f32)
        rest = z.stack - data_rows
        gs[at + data_rows : at + z.stack, :] = jnp.zeros((rest, LANES), f32)
    for m in range(z.micros):
        first_len, second_len = lengths[m, 0], lengths[m, 1]
        for i in range(z.blocks):
            at = (m * z.blocks + i) * z.segments
            where = spot + i * LANES
            masks[at : at + 1, :] = jnp.where(where < first_len, 1.0, 0.0)
            inside = jnp.where(where < first_len + second_len, 1.0, 0.0)
            masks[at + 1 : at + 2, :] = jnp.where(where >= first_len, inside, 0.0)

    pl.semaphore_wait(
        barrier,
        z.members - 1 + z.members * (jnp.minimum(pipe, 1) + jnp.minimum(last - pipe, 1)),
    )

    @pl.when(pipe == 0)
    def _():
        to_peers(lambda c: tok_tx.at[c], tok_rx, TOK)

    to_peers(lambda c: vec_tx, vec_all, VEC)
    weights_out(GLU)

    @pl.when(pipe > 0)
    def _():
        to_section_peers(lambda c: vec_tx, vec_next, VECN, pipe - 1)

    @pl.when(pipe == last)
    def _():
        to_peers(lambda c: cot_tx.at[c], cot_rx, COT)


    y_all, ms, cross, over = moments()
    fix = times(cross, over)
    spec = jnp.concatenate([ms[0][0] - cosine * fix[0], ms[0][1] - cosine * fix[1]], axis=1)
    wait_bytes(table, recv.at[TABLE])
    both = dot(high_low(spec), table[...])
    wide = (z.blocks + 1) * LANES
    kern_s[:, 0 : z.length] = both[0:ch] + both[ch : 2 * ch]
    kern_s[:, z.length : wide] = jnp.zeros((ch, wide - z.length), f32)

    def norm_stats(v):
        mean = jnp.sum(v, axis=1, keepdims=True) * (1.0 / width)
        spread = jnp.sum(v * v, axis=1, keepdims=True) * (1.0 / width) - mean * mean
        inv = lax.rsqrt(spread + norm_eps)
        return (v - mean) * inv, inv

    def norm_back(e, hat, inv, gain):
        dh = e * gain
        first = jnp.sum(dh, axis=1, keepdims=True) * (1.0 / width)
        second = jnp.sum(dh * hat, axis=1, keepdims=True) * (1.0 / width)
        return inv * (dh - first - hat * second)

    def turn_out(v, ref):
        tall = jnp.concatenate([v, jnp.zeros((LANES - rows, width), f32)], axis=0)
        ref[...] = tall.T.astype(bf16).reshape(ref.shape)

    def turn_in(ref):
        return ref[...].reshape(width, LANES).astype(f32).T[:rows]

    def full_row(source, r):
        tiles = [
            jnp.where(first_half, source[2 * j, r : r + 1, :], source[2 * j + 1, r : r + 1, :])
            for j in range(z.peers // 2)
        ]
        return jnp.concatenate(tiles, axis=1)

    wait_bytes(vec_all, recv.at[VEC])

    @pl.when(pipe == 0)
    def _():
        wait_bytes(tok_rx, recv.at[TOK])
        x = turn_in(tok_rx)
        res[...] = x.astype(bf16)
        hat1, inv1 = norm_stats(x)
        hat1_s[...] = hat1
        inv1_s[...] = jnp.broadcast_to(inv1, (rows, LANES))
        turn_out(hat1 * full_row(vec_all, 0) + full_row(vec_all, 1), tx1)
        to_members(lambda p: tx1.at[p], rx1, slot_me, A1 + own_micro)

    weights_out(UP)
    pl.when(pipe > 0)(lambda: weights_out(DOWN))

    def toeplitz_one(h):
        full = jnp.broadcast_to(kern_s[pl.ds(h, 1), :], (LANES, wide))
        full = pltpu.roll(full, 0, 1, stride=1, stride_axis=0).astype(bf16)
        far[h] = full[:, : z.length]
        for d in range(z.blocks):
            near[h, d * LANES : (d + 1) * LANES, :] = full[:, d * LANES : (d + 1) * LANES]

    each_channel(toeplitz_one, 2)
    weights_beside(GLU)
    weights_near(GLU)

    def weights_up():
        weights_beside(UP)
        weights_near(UP)
        weights_core(UP)

    def weights_down():
        weights_beside(DOWN)
        weights_near(DOWN)
        weights_core(DOWN)

    @pl.when(pipe > 0)
    def _():
        weights_up()
        weights_down()

    weights_core(GLU)

    def lane_tiles(ref, m):
        tiles = []
        for i in range(z.blocks):
            lo, hi = i * LANES, (i + 1) * LANES
            tile = None
            for k in range(lo // tok, -(-hi // tok)):
                piece = shifted(ref[m * z.slots + k].astype(f32), k * tok - lo)
                first = max(0, k * tok - lo)
                if tile is None:
                    tile = piece
                else:
                    tile = jnp.where(spot >= first, piece, tile)
            tiles.append(tile)
        return tiles

    def lane_pieces(tiles, m, ref):
        for k in range(z.slots):
            i, off = divmod(k * tok, LANES)
            piece = shifted(tiles[i], LANES - off)
            if off + tok > LANES:
                piece = jnp.where(spot < LANES - off, piece, shifted(tiles[i + 1], LANES - off))
            ref[m * z.slots + k] = piece.astype(bf16)

    def row_at(m, i, q):
        return m * z.stack + (i * z.segments + q) * z.ch

    def mask_of(m, i, q):
        at = (m * z.blocks + i) * z.segments + q
        return masks[at : at + 1, :]

    def masked_store(ref, base, m, i, tile):
        for q in range(z.segments):
            at = base + row_at(m, i, q)
            ref[at : at + z.ch, :] = tile * mask_of(m, i, q)

    def masked_sum(m, i):
        total = None
        for q in range(z.segments):
            at = row_at(0, i, q)
            part = ys[at : at + z.ch, :] * mask_of(m, i, q)
            total = part if total is None else total + part
        return total

    def whole_tile(ref, base, m, i):
        total = None
        for q in range(z.segments):
            at = base + row_at(m, i, q)
            total = ref[at : at + z.ch, :] if total is None else total + ref[at : at + z.ch, :]
        return total

    def windows(ref, m, h, back):
        parts = []
        for d in range(z.blocks):
            first = (z.blocks - 1 - d) if back else d
            start = m * z.stack + first * z.segments * z.ch + h
            parts.append(ref[pl.ds(start, z.conv_rows, stride=z.ch), :])
        return jnp.concatenate(parts, axis=1).astype(bf16)

    for m in range(z.micros):
        wait_bytes(rx1.at[pl.ds(m * z.slots, z.slots)], recv.at[A1 + m])
        for i, tile in enumerate(lane_tiles(rx1, m)):
            masked_store(xs, pad_rows, m, i, tile)

        def conv_one(h):
            ys[pl.ds(h, z.conv_rows, stride=z.ch), :] = dot(windows(xs, m, h, True), near[h])

        each_channel(conv_one, ch)
        tiles = []
        for i in range(z.blocks):
            tile = masked_sum(m, i) + skip[...] * whole_tile(xs, pad_rows, m, i)
            conv_out[m * z.blocks + i] = tile
            tiles.append(gelu(tile))
        lane_pieces(tiles, m, tx2)
        to_micro(m, tx2, rx2, A2)

    @pl.when(pipe == 0)
    def _():
        weights_out(DOWN)
        weights_up()

    wait_bytes(rx2, recv.at[A2])
    gated_s[...] = turn_in(rx2).astype(bf16)
    weights_here(GLU)
    gated = gated_s[...]
    value = dot_nt(gated, glu_all[0].reshape(width, width)) + full_row(vec_all, 5)
    sig = jax.nn.sigmoid(
        dot_nt(gated, glu_all[1].reshape(width, width)) + full_row(vec_all, 6)
    )
    val_s[...] = value
    sig_s[...] = sig
    pl.when(pipe > 0)(lambda: wait_bytes(res, recv.at[RES]))
    mid = res[...].astype(f32) + value * sig
    hat2, inv2 = norm_stats(mid)
    hat2_s[...] = hat2
    inv2_s[...] = jnp.broadcast_to(inv2, (rows, LANES))
    ffn_s[...] = (hat2 * full_row(vec_all, 2) + full_row(vec_all, 3)).astype(bf16)
    weights_here(UP)
    ffn_in = ffn_s[...]
    for c in range(z.peers):
        offset = jnp.concatenate([vec_all[c, 7 + r : 8 + r, :] for r in range(per)], axis=1)
        hidden = dot(ffn_in, up_all[c]) + offset
        hidden_s[c] = hidden
        act_s[c] = gelu(hidden).astype(bf16)
    pl.when(pipe == 0)(weights_down)
    weights_here(DOWN)
    total = mid + full_row(vec_all, 4)
    for c in range(z.peers):
        total = total + dot(act_s[c], down_all[c])
    layer_out = jnp.where(row_ok, total, 0.0).astype(bf16)
    lay_s[...] = layer_out

    @pl.when(pipe < last)
    def _():
        wait_bytes(vec_next, recv.at[VECN])
        hat, inv = norm_stats(lay_s[...].astype(f32))
        hatn_s[...] = hat
        invn_s[...] = jnp.broadcast_to(inv, (rows, LANES))
        turn_out(hat * full_row(vec_next, 0) + full_row(vec_next, 1), tx1n)
        to_section(lambda p: tx1n.at[p], rx1, slot_me, A1 + own_micro, pipe + 1)
        remote(lay_s, res, RES, place(chan, data, pipe + 1)).start()

    def forward_rows():
        to_peers(lambda c: gated_s, ga, GA)
        to_peers(lambda c: ffn_s, fi, FI)
        to_peers(lambda c: act_s.at[c], ac, AC)

    def backward_rows():
        to_peers(lambda c: gtop, bg, BG)
        to_peers(lambda c: gh_s.at[c], gh, GH)
        to_peers(lambda c: gp_s.at[c], gp, GP)

    turn_out(lay_s[...].astype(f32), lay_t)

    @pl.when(pipe < last)
    def _():
        to_peers(lambda c: lay_t.at[c], hid_rx, HID)
        forward_rows()

    @pl.when(pipe == last)
    def _():
        wait_bytes(cot_rx, recv.at[COT])
        gtop[...] = jnp.where(row_ok, turn_in(cot_rx), 0.0).astype(bf16)

    @pl.when(pipe < last)
    def _():
        wait_bytes(mid_rx, recv.at[MID])
        wait_bytes(rx4n, recv.at[A4N])
        grad_in = jnp.where(row_ok, turn_in(rx4n), 0.0)
        hat = hatn_s[...]
        grad_res = mid_rx[...] + norm_back(
            grad_in, hat, invn_s[:, 0:1], full_row(vec_next, 0)
        )
        gtop[...] = grad_res.astype(bf16)
        pair = (
            jnp.sum(grad_in * hat, axis=0, keepdims=True),
            jnp.sum(grad_in, axis=0, keepdims=True),
        )
        for c in range(z.peers):
            for r, row in enumerate(pair):
                vgn_s[c, r : r + 1, :] = row[:, (c // 2) * LANES : (c // 2 + 1) * LANES]

    grad_low = gtop[...]
    grad_top = grad_low.astype(f32)
    grad_ffn = None
    for c in range(z.peers):
        grad_active = dot_nt(grad_low, down_all[c])
        grad_hidden = (grad_active * gelu_slope(hidden_s[c])).astype(bf16)
        gh_s[c] = grad_hidden
        part = dot_nt(grad_hidden, up_all[c])
        grad_ffn = part if grad_ffn is None else grad_ffn + part
    hat2 = hat2_s[...]
    grad_mid = grad_top + norm_back(grad_ffn, hat2, inv2_s[:, 0:1], full_row(vec_all, 2))
    mid_s[...] = grad_mid
    sig = sig_s[...]
    grad_value = grad_mid * sig
    grad_gate = grad_value * val_s[...] * (1.0 - sig)
    grad_gated = dot(grad_value.astype(bf16), glu_all[0].reshape(width, width)) + dot(
        grad_gate.astype(bf16), glu_all[1].reshape(width, width)
    )
    turn_out(grad_gated, tx3)
    to_members(lambda p: tx3.at[p], rx3, slot_me, A3 + own_micro)
    for j in range(z.peers // 2):
        gv = grad_value[:, j * LANES : (j + 1) * LANES]
        gg = shifted(grad_gate[:, j * LANES : (j + 1) * LANES], LANES // 2)
        gp_s[2 * j] = jnp.where(first_half, gv, gg).astype(bf16)
        gp_s[2 * j + 1] = jnp.where(first_half, gg, gv).astype(bf16)
    pl.when(pipe > 0)(lambda: remote(mid_s, mid_rx, MID, place(chan, data, pipe - 1)).start())
    pl.when(pipe == 0)(backward_rows)

    @pl.when(pipe < last)
    def _():
        turn_out(gtop[...].astype(f32), ign_t)
        to_section_peers(lambda c: ign_t.at[c], ig_rx, IG, pipe + 1)
        to_section(lambda p: vgn_s.at[p // z.groups], vnrx, me, VGN, pipe + 1)

    for m in range(z.micros):
        wait_bytes(rx3.at[pl.ds(m * z.slots, z.slots)], recv.at[A3 + m])
        for i, tile in enumerate(lane_tiles(rx3, m)):
            masked_store(gs, 0, m, i, tile * gelu_slope(conv_out[m * z.blocks + i]))

        def back_one(h):
            ys[pl.ds(h, z.conv_rows, stride=z.ch), :] = dot_nt(windows(gs, m, h, False), far[h])

        each_channel(back_one, ch)
        tiles = [
            masked_sum(m, i) + skip[...] * whole_tile(gs, 0, m, i) for i in range(z.blocks)
        ]
        lane_pieces(tiles, m, tx4)
        pl.when(pipe == 0)(lambda: to_micro(m, tx4, rx4, A4))
        pl.when(pipe > 0)(lambda: to_micro(m, tx4, rx4n, A4N, pipe - 1))

    pl.when(pipe > 0)(backward_rows)

    @pl.when(pipe == last)
    def _():
        to_peers(lambda c: lay_t.at[c], hid_rx, HID)
        forward_rows()

    def lag_one(h):
        x = [
            xs[pl.ds(m * z.stack + pad_rows + h, z.conv_rows, stride=z.ch), :]
            for m in range(z.micros)
        ]
        g = jnp.concatenate([windows(gs, m, h, False) for m in range(z.micros)], axis=0)
        prod = dot_tn(jnp.concatenate(x, axis=0).astype(bf16), g)
        prod = jnp.concatenate([prod, jnp.zeros((LANES, LANES), f32)], axis=1)
        size = LANES // 2
        while size >= 8:
            prod = prod[:size] + shifted(prod[size:], wide - size)
            size //= 2
        for t in range(z.blocks + 1):
            rest_s[t, pl.ds(pl.multiple_of(h * 8, 8), 8), :] = prod[:, t * LANES : (t + 1) * LANES]

    def lag_rest():
        total = None
        for a in range(8):
            tiles = [rest_s[t, pl.ds(a, ch, stride=8), :] for t in range(z.blocks + 1)]
            part = shifted(jnp.concatenate(tiles, axis=1), wide - a)
            total = part if total is None else total + part
        lag_s[...] = total

    each_channel(lag_one, 4)
    lag_rest()

    many = z.peers * rows
    grads = (
        (ac, AC, bg, BG, z.hid, width, pdown, kdown, sdown, ldown, ddown),
        (fi, FI, gh, GH, width, z.hid, pup, kup, sup, lup, dup),
        (gp, GP, ga, GA, 2 * z.cw, width, pglu, kglu, sglu, lglu, dglu),
    )
    for t, (left, lp, right, rp, n_left, n_right, part, krx, *_) in enumerate(grads):
        wait_bytes(left, recv.at[lp])
        wait_bytes(right, recv.at[rp])
        part[...] = dot_tn(left[...].reshape(many, n_left), right[...].reshape(many, n_right))
        half = n_left // 2
        other = pl.ds(pl.multiple_of((1 - core) * half, half), half)
        remote(part.at[other], krx, GRADS + 3 * t, sibling).start()
    @pl.when(pipe == 0)
    def _():
        wait_bytes(rx4, recv.at[A4])
        grad_in = jnp.where(row_ok, turn_in(rx4), 0.0)
        hat = hat1_s[...]
        grad_res = mid_s[...] + norm_back(grad_in, hat, inv1_s[:, 0:1], full_row(vec_all, 0))
        turn_out(grad_res, ig_t)
        to_peers(lambda c: ig_t.at[c], ig_rx, IG)
        pair = (
            jnp.sum(grad_in * hat, axis=0, keepdims=True),
            jnp.sum(grad_in, axis=0, keepdims=True),
        )
        for c in range(z.peers):
            for r, row in enumerate(pair):
                vg0_s[c, r : r + 1, :] = row[:, (c // 2) * LANES : (c // 2 + 1) * LANES]
        to_members(lambda p: vg0_s.at[p // z.groups], vnrx, me, VGN)

    for t, (_, _, _, _, n_left, _, part, krx, lsend, lrx, _) in enumerate(grads):
        half = n_left // 2
        own = pl.ds(pl.multiple_of(core * half, half), half)
        wait_bytes(krx, recv.at[GRADS + 3 * t])
        lsend[...] = (part[own, :] + krx[...]).astype(bf16)
        remote(lsend, lrx, GRADS + 3 * t + 1, across).start()

    rows_of = [
        jnp.sum(grad_ffn * hat2, axis=0, keepdims=True),
        jnp.sum(grad_ffn, axis=0, keepdims=True),
        jnp.sum(grad_top, axis=0, keepdims=True),
    ]
    for c in range(z.peers):
        j = c // 2
        for r, row in enumerate(rows_of):
            vg_s[c, r : r + 1, :] = row[:, j * LANES : (j + 1) * LANES]
        vg_s[c, 3:4, :] = jnp.sum(gp_s[c].astype(f32), axis=0, keepdims=True)
        up_row = jnp.sum(gh_s[c].astype(f32), axis=0, keepdims=True)
        for r in range(per):
            vg_s[c, 4 + r : 5 + r, :] = up_row[:, r * LANES : (r + 1) * LANES]
    to_members(lambda p: vg_s.at[p // z.groups], vrx, me, VG)
    both = dot_nt(high_low(lag_s[:, 0 : z.length]), table[...])
    grad_spec = both[0:ch] + both[ch : 2 * ch]
    gk = (grad_spec[:, 0:padded], grad_spec[:, padded : 2 * padded])
    y_all, ms, cross, over = moments()
    g_top = times(conj(over), gk)
    g_top = (-cosine * g_top[0], -cosine * g_top[1])
    g_low = times(conj(times(times(cross, over), over)), gk)
    g_three = (cosine * cosine * g_low[0], cosine * cosine * g_low[1])
    g_ms = [gk, times(conj(ms[2]), g_top), times(conj(ms[1]), g_top), g_three]
    g_rise = None
    for v, (g_r, g_i) in enumerate(g_ms):
        gsum_s[v, :, 0:padded] = 2.0 * cosine * g_r
        gsum_s[v, :, padded : 2 * padded] = -2.0 * cosine * g_i
        gsum_s[4 + v, :, 0:padded] = 2.0 * y_all * g_i
        gsum_s[4 + v, :, padded : 2 * padded] = 2.0 * y_all * g_r
        part = 2.0 * (sums_s[12 + v] * g_r + sums_s[8 + v] * g_i)
        g_rise = part if g_rise is None else g_rise + part
    slope_s[...] = g_rise
    gcol_s[...] = jnp.zeros(gcol_s.shape, f32)
    gstep_s[...] = jnp.zeros(gstep_s.shape, f32)

    def split(x):
        high_part = x.astype(bf16)
        return high_part, (x - high_part.astype(f32)).astype(bf16)

    g_high, g_low = split(gsum_s[...].reshape(8 * ch, 2 * padded))
    own = [jnp.where(lax.rem(spot, ch) == h, cols[0], 0.0) for h in range(ch)]
    c_high, c_low = split(jnp.concatenate(own, axis=0))
    guw_s[...] = dot(c_high, g_high) + dot(c_high, g_low) + dot(c_low, g_high)
    uw_high, uw_low = split(uw_s[...])
    g_cols = dot_nt(uw_high, g_high) + dot_nt(uw_high, g_low) + dot_nt(uw_low, g_high)
    total = g_cols[0:nh]
    for h in range(1, ch):
        total = jnp.where(lax.rem(spot, ch) == h, g_cols[h * nh : (h + 1) * nh], total)
    gcol_s[0] = total

    def mode_one(h):
        at = pl.ds(pl.multiple_of(h * nh, nh), nh)
        u, w = uw_s[at, 0:padded], uw_s[at, padded : 2 * padded]
        gu, gw = guw_s[at, 0:padded], guw_s[at, padded : 2 * padded]
        double = column_of(1, h)[:, ch : ch + 1]
        y = rise_s[pl.ds(h, 1), 0:1] * sine
        even, cross_uw = u * u - w * w, 2.0 * u * w
        g_den_r = -(even * gu + cross_uw * gw)
        g_den_i = even * gw - cross_uw * gu
        ge = jnp.sum(cosine * cosine * g_den_r, axis=1, keepdims=True)
        gf = jnp.sum(cosine * y * g_den_i, axis=1, keepdims=True)
        acc = jnp.where(spot == h, ge, gcol_s[1])
        gcol_s[1] = jnp.where(spot == ch + h, gf, acc)
        gy = slope_s[pl.ds(h, 1), :] + jnp.sum(
            double * cosine * g_den_i - 2.0 * y * g_den_r, axis=0, keepdims=True
        )
        total_y = jnp.sum(y * gy, axis=1, keepdims=True)
        gstep_s[0:1, :] = jnp.where(spot == h, -total_y, gstep_s[0:1, :])

    each_channel(mode_one, 4)

    def unpacked(k, i):
        return shifted(gcol_s[k], LANES - i * ch)

    g_square, g_double = unpacked(1, 0), unpacked(1, 1)
    g_decay = 2.0 * decay * g_square + 2.0 * g_double
    g_rate = 2.0 * rate * g_square
    g_pairs = []
    for v, (v_r, v_i) in enumerate(pairs):
        g_alpha, g_beta = unpacked(0, v), unpacked(0, 4 + v)
        g_decay = g_decay + g_alpha * v_r
        if v_i is not None:
            g_rate = g_rate - g_alpha * v_i
        g_pairs.append((decay * g_alpha + g_beta, -rate * g_alpha))
    c_b, c_p, p_b = g_pairs[0], g_pairs[1], g_pairs[2]
    p_p = g_pairs[3][0]
    rank, into, out = (rank_r, rank_i), (in_r, in_i), (out_r, out_i)

    def plus(*terms):
        return sum(t[0] for t in terms), sum(t[1] for t in terms)

    g_out = plus(times(conj(into), c_b), times(conj(rank), c_p))
    g_in = plus(times(conj(out), c_b), times(rank, p_b))
    g_rank = plus(
        times(conj(out), c_p),
        times(into, conj(p_b)),
        (2.0 * rank_r * p_p, 2.0 * rank_i * p_p),
    )
    modes_tx[0:nh, :] = packed([g_decay, g_rate, *g_rank, *g_in, *g_out])
    modes_tx[nh : nh + 8, :] = gstep_s[...]
    skip_row = jnp.sum(jnp.where(diagonal, lag_s[:, 0:1], 0.0), axis=0, keepdims=True)
    modes_tx[nh + 1 : nh + 2, :] = skip_row
    for k in range(1, z.groups):
        remote(modes_tx, modes_rx.at[data], MODES, place(chan, lax.rem(data + k, z.groups))).start()
    pltpu.make_async_copy(modes_tx, modes_rx.at[data], recv.at[MODES]).start()

    for t, (_, _, _, _, n_left, _, _, _, lsend, lrx, final) in enumerate(grads):
        half = n_left // 2
        own = pl.ds(pl.multiple_of(core * half, half), half)
        wait_bytes(lrx, recv.at[GRADS + 3 * t + 1])
        final[own, :] = lsend[...].astype(f32) + lrx[...].astype(f32)
        remote(final.at[own], final.at[own], GRADS + 3 * t + 2, sibling).start()

    def collect(source, target):
        count = tok * z.quarters
        for m in range(z.micros):
            tiles = []
            for i in range(-(-count // LANES)):
                lo, hi = i * LANES, min((i + 1) * LANES, count)
                tile = None
                for q in range(lo // tok, -(-hi // tok)):
                    piece = shifted(source[m * z.quarters + q].astype(f32), q * tok - lo)
                    first = max(0, q * tok - lo)
                    tile = piece if tile is None else jnp.where(spot >= first, piece, tile)
                tiles.append(tile)
            target[m] = jnp.concatenate(tiles, axis=1)[:, 0:count].astype(bf16)

    wait_bytes(hid_rx, recv.at[HID])
    collect(hid_rx, hid_out)
    wait_bytes(ig_rx, recv.at[IG])
    collect(ig_rx, ig_out)
    wait_bytes(vrx, recv.at[VG])
    wait_bytes(vnrx, recv.at[VGN])
    summed, summed_one = vrx[0], vnrx[0]
    for p in range(1, z.members):
        summed = summed + vrx[p]
        summed_one = summed_one + vnrx[p]
    upb_out[...] = jnp.concatenate([summed[4 + r : 5 + r, :] for r in range(per)], axis=1)
    summed, summed_one = own_half(summed), own_half(summed_one)
    for r in range(3):
        ffn_out[r] = summed[r : r + 1, 0 : z.cw]
    glub_out[0:1, :] = summed[3:4, 0 : z.cw]
    glub_out[1:2, :] = shifted(summed[3:4], LANES // 2)[:, 0 : z.cw]
    vec_out[0:2, :] = summed_one[0:2, 0 : z.cw]
    wait_bytes(modes_rx, recv.at[MODES])

    def over_groups(take):
        total = take(0)
        for d in range(1, z.groups):
            total = jnp.where(spot // ch == d, take(d), total)
        return total[:, 0 : z.cw]

    for p in range(8):
        modes_out[p] = over_groups(
            lambda d: shifted(modes_rx[d, 0:nh, :], (d - p) * ch)
        )
    for r in range(2):
        vec_out[2 + r : 3 + r, :] = over_groups(
            lambda d: shifted(modes_rx[d, nh + r : nh + r + 1, :], d * ch)
        )
    for t, (_, _, _, _, n_left, _, _, _, _, _, final) in enumerate(grads):
        half = n_left // 2
        other = pl.ds(pl.multiple_of((1 - core) * half, half), half)
        wait_bytes(final.at[other], recv.at[GRADS + 3 * t + 2])
    glu_out[0] = dglu[pl.ds(pl.multiple_of(odd * z.cw, z.cw), z.cw), :]
    glu_out[1] = dglu[pl.ds(pl.multiple_of((1 - odd) * z.cw, z.cw), z.cw), :]

    for t in (GLU, UP, DOWN):
        weights_sent(t)
    for ref, phase in (
        (vec_all, VEC), (hid_rx, HID), (ga, GA), (fi, FI), (ac, AC), (bg, BG), (gh, GH), (gp, GP),
    ):
        wait_bytes(ref.at[pl.ds(0, z.peers - 1)], send.at[phase])
    for ref, phase in ((rx2, A2), (rx3, A3 + own_micro), (vrx, VG)):
        wait_bytes(ref.at[pl.ds(0, z.members - 1)], send.at[phase])
    wait_bytes(modes_rx.at[pl.ds(0, z.groups - 1)], send.at[MODES])
    for t, (_, _, _, _, n_left, _, _, krx, lsend, _, final) in enumerate(grads):
        wait_bytes(krx, send.at[GRADS + 3 * t])
        wait_bytes(lsend, send.at[GRADS + 3 * t + 1])
        wait_bytes(final.at[pl.ds(0, n_left // 2)], send.at[GRADS + 3 * t + 2])

    @pl.when(pipe == 0)
    def _():
        wait_bytes(tok_rx.at[pl.ds(0, z.peers - 1)], send.at[TOK])
        wait_bytes(ig_rx.at[pl.ds(0, z.peers - 1)], send.at[IG])
        for ref, phase in ((rx1, A1 + own_micro), (rx4, A4), (vnrx, VGN)):
            wait_bytes(ref.at[pl.ds(0, z.members - 1)], send.at[phase])

    @pl.when(pipe == last)
    def _():
        wait_bytes(cot_rx.at[pl.ds(0, z.peers - 1)], send.at[COT])

    @pl.when(pipe < last)
    def _():
        for ref, phase in ((rx1, A1 + own_micro), (lay_s, RES), (ig_rx, IG), (vnrx, VGN)):
            wait_bytes(ref, send.at[phase])

    @pl.when(pipe > 0)
    def _():
        for ref, phase in ((vec_all, VECN), (mid_s, MID), (rx4, A4N)):
            wait_bytes(ref, send.at[phase])


def finish_kernel(*refs):
    count = (len(refs) - 1) // 3
    sems = refs[-1]
    sources, targets, held = refs[:count], refs[count : 2 * count], refs[2 * count : -1]
    loads = [pltpu.make_async_copy(sources[i], held[i], sems.at[i]) for i in range(count)]
    stores = [
        pltpu.make_async_copy(held[i], targets[i], sems.at[count + i]) for i in range(count)
    ]
    for load in loads:
        load.start()
    for load, store in zip(loads, stores):
        load.wait()
        store.start()
    for store in stores:
        store.wait()


def body(
    tokens,
    seq_lengths,
    out_cot,
    s4_vectors,
    s4_modes,
    glu_weight,
    glu_bias,
    ffn_vectors,
    up_weight,
    up_bias,
    down_weight,
):
    micros, tok_rows, chan_width = tokens.shape
    width = glu_weight.shape[1]
    hidden = up_weight.shape[2]
    z = Sizes(
        lax.axis_size("pipe"), lax.axis_size("chan"), lax.axis_size("dp"),
        tok_rows, chan_width, width, hidden,
    )
    length = z.length
    padded = -(-(length // 2 + 1) // LANES) * LANES
    nh = s4_modes.shape[3]
    table = jnp.asarray(fourier_table(length, padded).astype(ml_dtypes.bfloat16))
    angles = jnp.asarray(half_angles(length, padded))

    vmem = pl.BlockSpec(memory_space=pltpu.VMEM)
    smem = pl.BlockSpec(memory_space=pltpu.SMEM)
    anywhere = pl.BlockSpec(memory_space=pl.ANY)
    n, r, w, ch = z.peers, z.rows, width, z.ch

    def s(shape, kind=f32):
        return jax.ShapeDtypeStruct(shape, kind)

    def v(shape, kind=bf16):
        return pltpu.VMEM(shape, kind)

    wide = (z.blocks + 1) * LANES
    rows_full, rows_wide, side = v((r, w)), v((r, w), f32), v((r, LANES), f32)
    peer_tiles, exchange = v((n, chan_width, LANES)), v((z.members, z.ch, LANES))
    small = v((n, 8, LANES), f32)
    results = (
        s((micros, chan_width, tok_rows), bf16), s((micros, chan_width, tok_rows), bf16),
        s((4, chan_width)), s((8, nh, chan_width)), s((2, chan_width, w)),
        s((2, chan_width)), s((3, 1, chan_width)), s((w, hidden)), s((1, hidden)),
        s((hidden, w)),
    )
    raw = pl.pallas_call(
        lambda *refs: main_kernel(z, *refs),
        out_shape=results,
        in_specs=[smem] + [vmem] * 11 + [anywhere],
        out_specs=[vmem] * 10,
        scratch_shapes=[
            peer_tiles, peer_tiles, v((16, LANES), f32), v((ch, length, LANES)),
            v((ch, LANES, length)), v((ch, LANES), f32), v((40, LANES), f32),
            peer_tiles, peer_tiles, v((micros * z.stack, LANES), f32),
            v((micros * z.stack, LANES), f32),
            v((2 * padded, length)), v((2, nh, LANES), f32),
            v((ch, LANES), f32), v((16, ch, padded), f32), v((ch * nh, 2 * padded), f32),
            v((ch * nh, 2 * padded), f32), v((z.blocks + 1, 8 * ch, LANES), f32),
            v((8, ch, 2 * padded), f32),
            v((ch, padded), f32), v((ch, wide), f32), v((ch, wide), f32),
            v((2, nh, LANES), f32), v((8, LANES), f32),
            v((nh + 8, LANES), f32), v((z.groups, nh + 8, LANES), f32),
            v((2 * chan_width, w), f32), v((w, hidden), f32), v((hidden, w), f32),
            v((chan_width, w), f32), v((w // 2, hidden), f32), v((hidden // 2, w), f32),
            v((chan_width, w)), v((w // 2, hidden)), v((hidden // 2, w)),
            v((chan_width, w)), v((w // 2, hidden)), v((hidden // 2, w)),
            v((2 * chan_width, w), f32),
            v((n, 16, LANES), f32), v((n, 16, LANES), f32),
            v((2, n, chan_width, w)), v((n, w, hidden)),
            v((n, hidden, w)), peer_tiles, peer_tiles, rows_full, rows_full,
        ]
        + [exchange] * 10
        + [
            v((z.micros * z.blocks, z.ch, LANES), f32), v((z.conv_rows * z.ch, LANES), f32),
            rows_wide, side, rows_wide, side, rows_wide, side,
            rows_wide, rows_wide, v((n, r, hidden), f32),
            rows_full, rows_full, v((n, r, hidden)), v((n, r, hidden)), v((n, r, LANES)),
            rows_full, peer_tiles, peer_tiles, peer_tiles, rows_wide, rows_wide,
            small, small, small,
            v((n, r, w)), v((n, r, w)), v((n, r, hidden)), v((n, r, w)), v((n, r, hidden)),
            v((n, r, LANES)), v((z.members, 8, LANES), f32), v((z.members, 8, LANES), f32),
            pltpu.SemaphoreType.DMA((52,)), pltpu.SemaphoreType.DMA((52,)),
        ],
        compiler_params=pltpu.CompilerParams(
            collective_id=0, has_side_effects=True, vmem_limit_bytes=60 * 2**20
        ),
        name="layers",
    )(
        seq_lengths, tokens.transpose(0, 2, 1), out_cot.transpose(0, 2, 1), s4_vectors[0],
        s4_modes[0].transpose(0, 2, 1), glu_weight[0].transpose(1, 2, 0), glu_bias[0],
        ffn_vectors.transpose(1, 0, 2), up_weight[0], up_bias, down_weight[0], angles, table,
    )
    hid, ig, vec, modes, dglu, glub, ffn, dup, upb, ddown = pl.pallas_call(
        finish_kernel,
        out_shape=results,
        in_specs=[anywhere] * 10,
        out_specs=[anywhere] * 10,
        scratch_shapes=[pltpu.VMEM(x.shape, x.dtype) for x in results]
        + [pltpu.SemaphoreType.DMA((20,))],
        compiler_params=pltpu.CompilerParams(vmem_limit_bytes=60 * 2**20),
        name="finish",
    )(*raw)
    return (
        hid.transpose(0, 2, 1)[None], ig.transpose(0, 2, 1)[None], vec[None],
        modes.transpose(0, 2, 1)[None], dglu.transpose(2, 0, 1)[None], glub[None],
        ffn.transpose(1, 0, 2), dup[None], upb, ddown[None],
    )


def solution(mesh):
    placed = (
        P(None, "dp", "chan"),
        P(),
        P(None, "dp", "chan"),
        P("pipe", None, "chan"),
        P("pipe", None, "chan", None),
        P("pipe", None, None, "chan"),
        P("pipe", None, "chan"),
        P("pipe", None, "chan"),
        P("pipe", None, "chan"),
        P("pipe", "chan"),
        P("pipe", "chan", None),
    )
    return jax.shard_map(
        body,
        mesh=mesh,
        in_specs=placed,
        out_specs=(
            P("pipe", None, "dp", "chan"),
            P("pipe", None, "dp", "chan"),
            P("pipe", None, "chan"),
            P("pipe", None, "chan", None),
            P("pipe", None, None, "chan"),
            P("pipe", None, "chan"),
            P("pipe", None, "chan"),
            P("pipe", None, "chan"),
            P("pipe", "chan"),
            P("pipe", "chan", None),
        ),
        check_vma=False,
    )
```

```python
import math

import jax
import jax.numpy as jnp
import ml_dtypes
import numpy as np
from jax import lax
from jax.experimental import pallas as pl
from jax.experimental.pallas import tpu as pltpu
from jax.sharding import PartitionSpec as P

norm_eps = 1e-05
f32 = jnp.float32
bf16 = jnp.bfloat16
LANES = 128


def fourier_table(length, padded):
    half = length // 2
    freq = np.arange(padded, dtype=np.int64)[:, None]
    time = np.arange(length, dtype=np.int64)[None, :]
    angle = (freq * (2 * time + 1) % (2 * length)) * (np.pi / length)
    weight = np.where(freq <= half, np.where((freq == 0) | (freq == half), 1.0, 2.0), 0.0) / length
    table = np.concatenate([np.cos(angle) * weight, -np.sin(angle) * weight], axis=0)
    return table.astype(np.float32)


def half_angles(length, padded):
    angle = np.minimum(np.arange(padded), length // 2) * (np.pi / length)
    rows = np.zeros((8, padded), np.float32)
    rows[0] = np.where(np.arange(padded) < length // 2, np.cos(angle), 0.0)
    rows[1] = np.sin(angle)
    return rows


def shifted(x, by):
    size = x.shape[-1]
    by = by % size
    if by == 0:
        return x
    return pltpu.roll(x, by, x.ndim - 1)


def gelu(x):
    return 0.5 * x * (1.0 + jnp.tanh(math.sqrt(2.0 / math.pi) * (x + 0.044715 * x * x * x)))


def gelu_slope(x):
    scale = math.sqrt(2.0 / math.pi)
    t = jnp.tanh(scale * (x + 0.044715 * x * x * x))
    return 0.5 * (1.0 + t) + 0.5 * x * (1.0 - t * t) * scale * (1.0 + 3.0 * 0.044715 * x * x)


def dot(a, b):
    return lax.dot_general(a, b, (((1,), (0,)), ((), ())), preferred_element_type=f32)


def dot_nt(a, b):
    return lax.dot_general(a, b, (((1,), (1,)), ((), ())), preferred_element_type=f32)


def dot_tn(a, b):
    return lax.dot_general(a, b, (((0,), (0,)), ((), ())), preferred_element_type=f32)


class Sizes:
    def __init__(self, sections, peers, groups, tok_rows, chan_width, model_width, hidden):
        self.sections, self.peers, self.groups = sections, peers, groups
        self.micros = 2
        self.segments = 2
        self.quarters = peers // self.micros
        self.tok = tok_rows // self.quarters
        self.rows = -(-self.tok // 16) * 16
        self.length = tok_rows * groups
        self.blocks = self.length // LANES
        self.width = model_width
        self.cw = chan_width
        self.hid = hidden
        self.members = peers * groups
        self.ch = model_width // self.members
        self.slots = self.quarters * groups
        self.conv_rows = -(-(self.blocks * self.segments) // 8) * 8
        spare = -(-(self.conv_rows - self.blocks * self.segments) // self.segments)
        self.stack = (2 * self.blocks - 1 + spare) * self.segments * self.ch


def main_kernel(z, *refs):
    (
        lengths, tokens, out_cot, vectors, modes, glu_loc, glu_bias, ffn_vec, up_loc, up_bias,
        down_loc, angles, table_in,
    ) = refs[:13]
    (
        hid_out, ig_out, vec_out, modes_out, glu_out, glub_out, ffn_out, dup, upb_out, ddown,
    ) = refs[13:23]
    (
        tok_tx, cot_tx, vec_tx, near, far, skip, masks, hid_rx, ig_rx, xs, gs,
        table, cols, rise_s, sums_s, uw_s, guw_s, rest_s, gsum_s, slope_s, kern_s, lag_s, gcol_s, gstep_s,
        modes_tx, modes_rx, pglu, pup, pdown, kglu, kup, kdown, sglu, sup, sdown,
        lglu, lup, ldown, dglu,
        vec_all, vec_next, glu_all, up_all, down_all, tok_rx, cot_rx, res, gtop,
        tx1, tx1n, rx1, tx2, rx2, tx3, rx3, tx4, rx4, rx4n,
        conv_out, ys, hat1_s, inv1_s, hatn_s, invn_s, hat2_s, inv2_s, val_s, sig_s, hidden_s,
        gated_s, ffn_s, act_s, gh_s, gp_s, lay_s, lay_t, ig_t, ign_t, mid_s, mid_rx,
        vg_s, vgn_s, vg0_s, ga, fi, ac, bg, gh, gp, vrx, vnrx, send, recv,
    ) = refs[23:]
    pipe = lax.axis_index("pipe")
    chan = lax.axis_index("chan")
    data = lax.axis_index("dp")
    last = z.sections - 1
    me = chan * z.groups + data
    slot_me = (chan // z.quarters) * z.slots + data * z.quarters + lax.rem(chan, z.quarters)
    rows, width, tok = z.rows, z.width, z.tok
    spot = lax.broadcasted_iota(jnp.int32, (1, LANES), 1)
    first_half = spot < (LANES // 2)
    row_ok = lax.broadcasted_iota(jnp.int32, (rows, 1), 0) < tok
    odd = lax.rem(chan, 2)
    per = z.hid // LANES

    high, deep = chan // z.quarters, lax.rem(chan, z.quarters)
    side, core = data // 2, lax.rem(data, 2)
    height = 2 * high + side

    def slot_of(p):
        c, d = p // z.groups, lax.rem(p, z.groups)
        return (c // z.quarters) * z.slots + d * z.quarters + lax.rem(c, z.quarters)

    def place(c, d, section=None):
        return {"pipe": pipe if section is None else section, "chan": c, "dp": d}

    def member(p, section=None):
        return place(p // z.groups, lax.rem(p, z.groups), section)

    def remote(src, dst, phase, where):
        return pltpu.make_async_remote_copy(
            src_ref=src,
            dst_ref=dst,
            send_sem=send.at[phase],
            recv_sem=recv.at[phase],
            device_id=where,
            device_id_type=pl.DeviceIdType.MESH,
        )

    def wait_bytes(ref, sem):
        pltpu.make_async_copy(ref, ref, sem).wait()

    def to_peers(src_of, dst, phase):
        def step(k, carry):
            c = lax.rem(chan + k, z.peers)
            remote(src_of(c), dst.at[chan], phase, place(c, data)).start()
            return carry

        lax.fori_loop(1, z.peers, step, 0)
        pltpu.make_async_copy(src_of(chan), dst.at[chan], recv.at[phase]).start()

    def far_first(i):
        return lax.rem(2 + i + (i // 2) * (2 * i - 3), 4)

    def number(y, depth, core_there):
        return ((y // 2) * z.quarters + depth) * z.groups + lax.rem(y, 2) * 2 + core_there

    def to_all(src_of, dst, slot, phase, section=None):
        def chip(k):
            y = lax.rem(height + far_first(k // 4), 4)
            return y, lax.rem(deep + far_first(lax.rem(k, 4)), 4)

        def step(k, carry):
            y, depth = chip(k)
            for c in range(2):
                p = number(y, depth, c)
                remote(src_of(p), dst.at[slot], phase, member(p, section)).start()
            return carry

        chips = z.members // 2
        lax.fori_loop(0, chips if section is not None else chips - 1, step, 0)
        if section is None:
            p = number(height, deep, 1 - core)
            remote(src_of(p), dst.at[slot], phase, member(p)).start()
            pltpu.make_async_copy(src_of(me), dst.at[slot], recv.at[phase]).start()

    def to_members(src_of, dst, slot, phase):
        to_all(src_of, dst, slot, phase)

    def to_section(src_of, dst, slot, phase, section):
        to_all(src_of, dst, slot, phase, section)

    def to_micro(m, source, dst, phase, section=None):
        near_by = jnp.where(own_micro == m, 1, 0)

        def send_to(p):
            remote(source.at[slot_of(p)], dst.at[me], phase, member(p, section)).start()

        def chip(k):
            y = 2 * m + lax.rem(side + near_by + k // 4, 2)
            return y, lax.rem(deep + far_first(lax.rem(k, 4)), 4)

        def step(k, carry):
            y, depth = chip(k)
            for c in range(2):
                send_to(number(y, depth, c))
            return carry

        lax.fori_loop(0, z.slots // 2 - 1, step, 0)
        if section is not None:
            step(z.slots // 2 - 1, 0)
            return

        @pl.when(own_micro == m)
        def _():
            send_to(number(height, deep, 1 - core))
            block = source.at[slot_of(me)]
            pltpu.make_async_copy(block, dst.at[me], recv.at[phase]).start()

        @pl.when(own_micro != m)
        def _():
            step(z.slots // 2 - 1, 0)

    def to_section_peers(src_of, dst, phase, section):
        def step(k, carry):
            c = lax.rem(chan + k, z.peers)
            remote(src_of(c), dst.at[chan], phase, place(c, data, section)).start()
            return carry

        lax.fori_loop(0, z.peers, step, 0)

    (
        VEC, VECN, TOK, COT, A2, A4, A4N, RES, MID, HID, IG, GA, FI, AC, BG, GH, GP, VG,
        VGN, TABLE, MODES,
    ) = range(21)
    A1, A3, GLU, UPA, UPB, DNA, DNB, GRADS = 21, 23, 25, 31, 37, 43, 49, 55
    direct = (DNB,)
    own_micro = chan // z.quarters

    own_side, far_side = high * z.quarters, (1 - high) * z.quarters
    sibling, across = place(chan, side * 2 + 1 - core), place(chan, (1 - side) * 2 + core)

    def columns(t):
        if t == GLU:
            return glu_loc, glu_all
        loc, whole = (up_loc, up_all) if t in (UPA, UPB) else (down_loc, down_all)
        count = loc.shape[1] // 2
        where = pl.ds(count if t in (UPB, DNB) else 0, count)
        return loc.at[:, where], whole.at[:, :, where]

    def own_rows(t, part=None):
        loc, _ = columns(t)
        if t == GLU:
            fourth = z.cw // 2
            half = loc.at[core]
            return half if part is None else half.at[pl.ds(pl.multiple_of(part * fourth, fourth), fourth)]
        half = loc.shape[0] // 2
        if part is None:
            return loc.at[pl.ds(pl.multiple_of(core * half, half), half)]
        fourth = half // 2
        return loc.at[pl.ds(pl.multiple_of(core * half + part * fourth, fourth), fourth)]

    def piece_of(t, c, count, part=None):
        loc, whole = columns(t)
        if t == GLU:
            fourth = z.cw // 2
            if part is None:
                return whole.at[core, pl.ds(c, count)]
            start = pl.multiple_of(part * fourth, fourth)
            return whole.at[core, pl.ds(c, count), pl.ds(start, fourth)]
        half = loc.shape[0] // 2
        fourth = half // 2
        if part is None:
            return whole.at[pl.ds(c, count), pl.ds(pl.multiple_of(core * half, half), half)]
        start = pl.multiple_of(core * half + part * fourth, fourth)
        return whole.at[pl.ds(c, count), pl.ds(start, fourth)]

    def weights_out(t):
        loc, whole = columns(t)
        whole = whole.at[:, chan] if t == GLU else whole.at[chan]
        pltpu.make_async_copy(loc, whole, recv.at[t + 5]).start()
        part = None if t in direct else side
        payload, there = own_rows(t, part), piece_of(t, chan, 1, part).at[0]
        for k in (2, 3, 1, 0):
            c = far_side + lax.rem(deep + k, z.quarters)
            remote(payload, there, t + 1, place(c, (1 - side) * 2 + core)).start()
        payload, there = own_rows(t), piece_of(t, chan, 1).at[0]
        for k in (2, 3, 1):
            c = own_side + lax.rem(deep + k, z.quarters)
            remote(payload, there, t, place(c, data)).start()

    def weights_beside(t):
        if t in direct:
            return
        wait_bytes(piece_of(t, 0, z.quarters, 0), recv.at[t + 1])
        piece = piece_of(t, far_side, z.quarters, 1 - side)
        remote(piece, piece, t + 2, across).start()

    def weights_near(t):
        wait_bytes(piece_of(t, 0, z.quarters - 1), recv.at[t])
        for k in range(1, z.quarters):
            piece = piece_of(t, own_side + lax.rem(deep + k, z.quarters), 1)
            remote(piece, piece, t + 3, sibling).start()

    def weights_core(t):
        if t in direct:
            wait_bytes(piece_of(t, 0, z.quarters), recv.at[t + 1])
        else:
            wait_bytes(piece_of(t, 0, z.quarters, 0), recv.at[t + 2])
        piece = piece_of(t, far_side, z.quarters)
        remote(piece, piece, t + 4, sibling).start()

    def weights_here(t):
        wait_bytes(columns(t)[0], recv.at[t + 5])
        wait_bytes(piece_of(t, 0, z.quarters - 1), recv.at[t + 3])
        wait_bytes(piece_of(t, 0, z.quarters), recv.at[t + 4])

    def weights_sent(t):
        far_part = None if t in direct else 0
        stages = [(0, z.quarters - 1, None), (1, z.quarters, far_part)]
        if t not in direct:
            stages.append((2, z.quarters, 0))
        stages += [(3, z.quarters - 1, None), (4, z.quarters, None)]
        for stage, count, part in stages:
            wait_bytes(piece_of(t, 0, count, part), send.at[t + stage])

    def weights_all(steps, *which):
        for t in which:
            for step in steps:
                step(t)

    forward_steps = (weights_beside, weights_near)

    barrier = pltpu.get_barrier_semaphore()

    def greet(where):
        pl.semaphore_signal(barrier, inc=1, device_id=where, device_id_type=pl.DeviceIdType.MESH)

    def greet_own(k, carry):
        greet(member(lax.rem(me + k, z.members)))
        return carry

    pl.when(pipe < last)(lambda: greet(place(chan, data, pipe + 1)))
    pl.when(pipe > 0)(lambda: greet(place(chan, data, pipe - 1)))
    lax.fori_loop(1, z.members, greet_own, 0)
    pltpu.make_async_copy(table_in, table, recv.at[TABLE]).start()

    def own_half(x):
        return pltpu.roll(x, odd * (LANES // 2), x.ndim - 1)

    def fill_blocks(source, target):
        count = z.tok * z.quarters
        over = -(-count // LANES) * LANES
        for m in range(z.micros):
            x = source[m].astype(f32)
            x = jnp.concatenate([x, jnp.zeros((z.cw, over - count), f32)], axis=1)
            for q in range(z.quarters):
                target[m * z.quarters + q] = shifted(x, over - q * tok)[:, 0:LANES].astype(bf16)

    vec_rows = [vectors[0:1, :], vectors[1:2, :]] + [ffn_vec[r] for r in range(3)]
    vec_rows += [glu_bias[0:1, :], glu_bias[1:2, :]]
    for r, row in enumerate(vec_rows):
        vec_tx[r : r + 1, :] = jnp.concatenate([row, row], axis=1)
    for r in range(per):
        vec_tx[7 + r : 8 + r, :] = up_bias[:, r * LANES : (r + 1) * LANES].astype(f32)
    pl.when(pipe == 0)(lambda: fill_blocks(tokens, tok_tx))
    pl.when(pipe == last)(lambda: fill_blocks(out_cot, cot_tx))

    ch, nh = z.ch, modes.shape[1]

    def own_lanes(x):
        x = jnp.concatenate([x, jnp.zeros((x.shape[0], LANES - z.cw), f32)], axis=1)
        return pltpu.roll(x, lax.rem(LANES - data * ch, LANES), 1)

    def packed(items):
        total = items[0]
        for i, item in enumerate(items[1:], 1):
            total = jnp.where(spot // ch == i, shifted(item, i * ch), total)
        return total

    decay, rate, rank_r, rank_i, in_r, in_i, out_r, out_i = (own_lanes(modes[p]) for p in range(8))
    pairs = [
        (out_r * in_r - out_i * in_i, out_r * in_i + out_i * in_r),
        (out_r * rank_r - out_i * rank_i, out_r * rank_i + out_i * rank_r),
        (rank_r * in_r + rank_i * in_i, rank_r * in_i - rank_i * in_r),
        (rank_r * rank_r + rank_i * rank_i, None),
    ]
    alphas = [
        decay * v_r if v_i is None else decay * v_r - rate * v_i for v_r, v_i in pairs
    ]
    cols[0] = packed(alphas + [v_r for v_r, v_i in pairs])
    cols[1] = packed([decay * decay + rate * rate, 2.0 * decay])
    own_vectors = own_lanes(vectors[...])
    diagonal = lax.broadcasted_iota(jnp.int32, (ch, LANES), 0) == lax.broadcasted_iota(
        jnp.int32, (ch, LANES), 1
    )

    def upright(row):
        column = jnp.sum(jnp.where(diagonal, row, 0.0), axis=1, keepdims=True)
        return jnp.broadcast_to(column, (ch, LANES))

    rise_s[...] = 2.0 * jnp.exp(-upright(own_vectors[2:3]))
    skip[...] = upright(own_vectors[3:4])
    cosine, sine = angles[0:1, :], angles[1:2, :]
    padded = angles.shape[1]

    def column_of(k, h):
        return pltpu.roll(cols[k], lax.rem(LANES - h, LANES), 1)

    def modes_at(h):
        two = column_of(1, h)
        square, double = two[:, 0:1], two[:, ch : ch + 1]
        y = rise_s[pl.ds(h, 1), 0:1] * sine
        cy = cosine * y
        den_r = square * (cosine * cosine) - y * y
        den_i = double * cy
        inverse = 1.0 / (den_r * den_r + den_i * den_i)
        return double, y, cy, den_r * inverse, den_i * inverse

    def cauchy_one(h):
        _, _, _, u, w = modes_at(h)
        at = pl.ds(pl.multiple_of(h * nh, nh), nh)
        uw_s[at, 0:padded] = u
        uw_s[at, padded : 2 * padded] = w
        column = column_of(0, h)
        for v in range(4):
            a = column[:, v * ch : v * ch + 1]
            b = column[:, (4 + v) * ch : (4 + v) * ch + 1]
            sums_s[v, pl.ds(h, 1), :] = jnp.sum(a * u, axis=0, keepdims=True)
            sums_s[4 + v, pl.ds(h, 1), :] = jnp.sum(a * w, axis=0, keepdims=True)
            sums_s[8 + v, pl.ds(h, 1), :] = jnp.sum(b * u, axis=0, keepdims=True)
            sums_s[12 + v, pl.ds(h, 1), :] = jnp.sum(b * w, axis=0, keepdims=True)

    def each_channel(one, unroll, first=0, end=None):
        def step(i, carry):
            for u in range(unroll):
                one(i * unroll + u)
            return carry

        if unroll == ch:
            step(0, 0)
        else:
            lax.fori_loop(first // unroll, (ch if end is None else end) // unroll, step, 0)

    def times(a, b):
        return a[0] * b[0] - a[1] * b[1], a[0] * b[1] + a[1] * b[0]

    def conj(a):
        return a[0], -a[1]

    def moments():
        y_all = rise_s[:, 0:1] * sine
        ms = [
            (
                2.0 * (cosine * sums_s[v] + y_all * sums_s[12 + v]),
                2.0 * (y_all * sums_s[8 + v] - cosine * sums_s[4 + v]),
            )
            for v in range(4)
        ]
        low_r, low_i = 1.0 + cosine * ms[3][0], cosine * ms[3][1]
        size = 1.0 / (low_r * low_r + low_i * low_i)
        return y_all, ms, times(ms[1], ms[2]), (low_r * size, -low_i * size)

    def high_low(x):
        high_part = x.astype(bf16)
        low_part = (x - high_part.astype(f32)).astype(bf16)
        return jnp.concatenate([high_part, low_part], axis=0)

    each_channel(cauchy_one, 4)
    pad_rows = (z.blocks - 1) * z.segments * z.ch
    data_rows = z.blocks * z.segments * z.ch
    for m in range(z.micros):
        at = m * z.stack
        xs[at : at + pad_rows, :] = jnp.zeros((pad_rows, LANES), f32)
        rest = z.stack - pad_rows - data_rows
        xs[at + z.stack - rest : at + z.stack, :] = jnp.zeros((rest, LANES), f32)
        rest = z.stack - data_rows
        gs[at + data_rows : at + z.stack, :] = jnp.zeros((rest, LANES), f32)
    for m in range(z.micros):
        first_len, second_len = lengths[m, 0], lengths[m, 1]
        for i in range(z.blocks):
            at = (m * z.blocks + i) * z.segments
            where = spot + i * LANES
            masks[at : at + 1, :] = jnp.where(where < first_len, 1.0, 0.0)
            inside = jnp.where(where < first_len + second_len, 1.0, 0.0)
            masks[at + 1 : at + 2, :] = jnp.where(where >= first_len, inside, 0.0)

    pl.semaphore_wait(
        barrier,
        z.members - 1 + jnp.minimum(pipe, 1) + jnp.minimum(last - pipe, 1),
    )

    @pl.when(pipe == 0)
    def _():
        to_peers(lambda c: tok_tx.at[c], tok_rx, TOK)

    to_peers(lambda c: vec_tx, vec_all, VEC)
    weights_out(GLU)

    @pl.when(pipe == last)
    def _():
        to_peers(lambda c: cot_tx.at[c], cot_rx, COT)


    y_all, ms, cross, over = moments()
    fix = times(cross, over)
    spec = jnp.concatenate([ms[0][0] - cosine * fix[0], ms[0][1] - cosine * fix[1]], axis=1)
    wait_bytes(table, recv.at[TABLE])
    both = dot(high_low(spec), table[...])
    wide = (z.blocks + 1) * LANES
    kern_s[:, 0 : z.length] = both[0:ch] + both[ch : 2 * ch]
    kern_s[:, z.length : wide] = jnp.zeros((ch, wide - z.length), f32)

    def norm_stats(v):
        mean = jnp.sum(v, axis=1, keepdims=True) * (1.0 / width)
        spread = jnp.sum(v * v, axis=1, keepdims=True) * (1.0 / width) - mean * mean
        inv = lax.rsqrt(spread + norm_eps)
        return (v - mean) * inv, inv

    def norm_back(e, hat, inv, gain):
        dh = e * gain
        first = jnp.sum(dh, axis=1, keepdims=True) * (1.0 / width)
        second = jnp.sum(dh * hat, axis=1, keepdims=True) * (1.0 / width)
        return inv * (dh - first - hat * second)

    def turn_out(v, ref):
        tall = jnp.concatenate([v, jnp.zeros((LANES - rows, width), f32)], axis=0)
        ref[...] = tall.T.astype(bf16).reshape(ref.shape)

    def turn_in(ref):
        return ref[...].reshape(width, LANES).astype(f32).T[:rows]

    def full_row(source, r):
        tiles = [
            jnp.where(first_half, source[2 * j, r : r + 1, :], source[2 * j + 1, r : r + 1, :])
            for j in range(z.peers // 2)
        ]
        return jnp.concatenate(tiles, axis=1)

    wait_bytes(vec_all, recv.at[VEC])

    @pl.when(pipe > 0)
    def _():
        remote(vec_all, vec_next, VECN, place(chan, data, pipe - 1)).start()

    @pl.when(pipe == 0)
    def _():
        wait_bytes(tok_rx, recv.at[TOK])
        x = turn_in(tok_rx)
        res[...] = x.astype(bf16)
        hat1, inv1 = norm_stats(x)
        hat1_s[...] = hat1
        inv1_s[...] = jnp.broadcast_to(inv1, (rows, LANES))
        turn_out(hat1 * full_row(vec_all, 0) + full_row(vec_all, 1), tx1)
        to_members(lambda p: tx1.at[p], rx1, slot_me, A1 + own_micro)

    weights_out(UPA)
    pl.when(pipe == 0)(lambda: weights_out(UPB))

    @pl.when(pipe > 0)
    def _():
        weights_all((weights_out,), UPB, DNA, DNB)

    def toeplitz_one(h):
        full = jnp.broadcast_to(kern_s[pl.ds(h, 1), :], (LANES, wide))
        full = pltpu.roll(full, 0, 1, stride=1, stride_axis=0).astype(bf16)
        far[h] = full[:, : z.length]
        for d in range(z.blocks):
            near[h, d * LANES : (d + 1) * LANES, :] = full[:, d * LANES : (d + 1) * LANES]

    each_channel(toeplitz_one, 2)
    weights_all(forward_steps, GLU)

    @pl.when(pipe > 0)
    def _():
        weights_all(forward_steps, UPA, UPB, DNA, DNB)
        weights_all((weights_core,), UPA, UPB, DNA, DNB)

    weights_core(GLU)

    def lane_tiles(ref, m):
        tiles = []
        for i in range(z.blocks):
            lo, hi = i * LANES, (i + 1) * LANES
            tile = None
            for k in range(lo // tok, -(-hi // tok)):
                piece = shifted(ref[m * z.slots + k].astype(f32), k * tok - lo)
                first = max(0, k * tok - lo)
                if tile is None:
                    tile = piece
                else:
                    tile = jnp.where(spot >= first, piece, tile)
            tiles.append(tile)
        return tiles

    def lane_pieces(tiles, m, ref):
        for k in range(z.slots):
            i, off = divmod(k * tok, LANES)
            piece = shifted(tiles[i], LANES - off)
            if off + tok > LANES:
                piece = jnp.where(spot < LANES - off, piece, shifted(tiles[i + 1], LANES - off))
            ref[m * z.slots + k] = piece.astype(bf16)

    def row_at(m, i, q):
        return m * z.stack + (i * z.segments + q) * z.ch

    def mask_of(m, i, q):
        at = (m * z.blocks + i) * z.segments + q
        return masks[at : at + 1, :]

    def masked_store(ref, base, m, i, tile):
        for q in range(z.segments):
            at = base + row_at(m, i, q)
            ref[at : at + z.ch, :] = tile * mask_of(m, i, q)

    def masked_sum(m, i):
        total = None
        for q in range(z.segments):
            at = row_at(0, i, q)
            part = ys[at : at + z.ch, :] * mask_of(m, i, q)
            total = part if total is None else total + part
        return total

    def whole_tile(ref, base, m, i):
        total = None
        for q in range(z.segments):
            at = base + row_at(m, i, q)
            total = ref[at : at + z.ch, :] if total is None else total + ref[at : at + z.ch, :]
        return total

    def windows(ref, m, h, back):
        parts = []
        for d in range(z.blocks):
            first = (z.blocks - 1 - d) if back else d
            start = m * z.stack + first * z.segments * z.ch + h
            parts.append(ref[pl.ds(start, z.conv_rows, stride=z.ch), :])
        return jnp.concatenate(parts, axis=1).astype(bf16)

    for m in range(z.micros):
        wait_bytes(rx1.at[pl.ds(m * z.slots, z.slots)], recv.at[A1 + m])
        for i, tile in enumerate(lane_tiles(rx1, m)):
            masked_store(xs, pad_rows, m, i, tile)

        def conv_one(h):
            ys[pl.ds(h, z.conv_rows, stride=z.ch), :] = dot(windows(xs, m, h, True), near[h])

        each_channel(conv_one, ch)
        tiles = []
        for i in range(z.blocks):
            tile = masked_sum(m, i) + skip[...] * whole_tile(xs, pad_rows, m, i)
            conv_out[m * z.blocks + i] = tile
            tiles.append(gelu(tile))
        lane_pieces(tiles, m, tx2)
        to_micro(m, tx2, rx2, A2)

    @pl.when(pipe == 0)
    def _():
        weights_out(DNA)
        weights_out(DNB)
        weights_all(forward_steps, UPA, UPB)
        weights_all((weights_core,), UPA)

    wait_bytes(rx2, recv.at[A2])
    gated_s[...] = turn_in(rx2).astype(bf16)
    weights_here(GLU)
    gated = gated_s[...]
    value = dot_nt(gated, glu_all[0].reshape(width, width)) + full_row(vec_all, 5)
    sig = jax.nn.sigmoid(
        dot_nt(gated, glu_all[1].reshape(width, width)) + full_row(vec_all, 6)
    )
    val_s[...] = value
    sig_s[...] = sig
    pl.when(pipe > 0)(lambda: wait_bytes(res, recv.at[RES]))
    mid = res[...].astype(f32) + value * sig
    hat2, inv2 = norm_stats(mid)
    hat2_s[...] = hat2
    inv2_s[...] = jnp.broadcast_to(inv2, (rows, LANES))
    ffn_s[...] = (hat2 * full_row(vec_all, 2) + full_row(vec_all, 3)).astype(bf16)

    @pl.when(pipe == 0)
    def _():
        weights_core(UPB)
        weights_all(forward_steps, DNA)

    weights_all((weights_here,), UPA, UPB)
    ffn_in = ffn_s[...]
    for c in range(z.peers):
        offset = jnp.concatenate([vec_all[c, 7 + r : 8 + r, :] for r in range(per)], axis=1)
        hidden = dot(ffn_in, up_all[c]) + offset
        hidden_s[c] = hidden
        act_s[c] = gelu(hidden).astype(bf16)

    @pl.when(pipe == 0)
    def _():
        weights_core(DNA)
        weights_all(forward_steps, DNB)
        weights_core(DNB)

    weights_all((weights_here,), DNA, DNB)
    total = mid + full_row(vec_all, 4)
    for c in range(z.peers):
        total = total + dot(act_s[c], down_all[c])
    layer_out = jnp.where(row_ok, total, 0.0).astype(bf16)
    lay_s[...] = layer_out

    @pl.when(pipe < last)
    def _():
        wait_bytes(vec_next, recv.at[VECN])
        hat, inv = norm_stats(lay_s[...].astype(f32))
        hatn_s[...] = hat
        invn_s[...] = jnp.broadcast_to(inv, (rows, LANES))
        turn_out(hat * full_row(vec_next, 0) + full_row(vec_next, 1), tx1n)
        to_section(lambda p: tx1n.at[p], rx1, slot_me, A1 + own_micro, pipe + 1)
        remote(lay_s, res, RES, place(chan, data, pipe + 1)).start()

    def forward_rows():
        to_peers(lambda c: gated_s, ga, GA)
        to_peers(lambda c: ffn_s, fi, FI)
        to_peers(lambda c: act_s.at[c], ac, AC)

    def top_rows():
        to_peers(lambda c: gtop, bg, BG)

    def hidden_rows():
        to_peers(lambda c: gh_s.at[c], gh, GH)
        to_peers(lambda c: gp_s.at[c], gp, GP)

    turn_out(lay_s[...].astype(f32), lay_t)

    @pl.when(pipe < last)
    def _():
        to_peers(lambda c: lay_t.at[c], hid_rx, HID)
        forward_rows()

    @pl.when(pipe == last)
    def _():
        wait_bytes(cot_rx, recv.at[COT])
        gtop[...] = jnp.where(row_ok, turn_in(cot_rx), 0.0).astype(bf16)

    @pl.when(pipe < last)
    def _():
        wait_bytes(mid_rx, recv.at[MID])
        wait_bytes(rx4n, recv.at[A4N])
        grad_in = jnp.where(row_ok, turn_in(rx4n), 0.0)
        hat = hatn_s[...]
        grad_res = mid_rx[...] + norm_back(
            grad_in, hat, invn_s[:, 0:1], full_row(vec_next, 0)
        )
        gtop[...] = grad_res.astype(bf16)
        pair = (
            jnp.sum(grad_in * hat, axis=0, keepdims=True),
            jnp.sum(grad_in, axis=0, keepdims=True),
        )
        for c in range(z.peers):
            for r, row in enumerate(pair):
                vgn_s[c, r : r + 1, :] = row[:, (c // 2) * LANES : (c // 2 + 1) * LANES]

    grad_low = gtop[...]
    grad_top = grad_low.astype(f32)
    grad_ffn = None
    for c in range(z.peers):
        grad_active = dot_nt(grad_low, down_all[c])
        grad_hidden = (grad_active * gelu_slope(hidden_s[c])).astype(bf16)
        gh_s[c] = grad_hidden
        part = dot_nt(grad_hidden, up_all[c])
        grad_ffn = part if grad_ffn is None else grad_ffn + part
    hat2 = hat2_s[...]
    grad_mid = grad_top + norm_back(grad_ffn, hat2, inv2_s[:, 0:1], full_row(vec_all, 2))
    mid_s[...] = grad_mid
    sig = sig_s[...]
    grad_value = grad_mid * sig
    grad_gate = grad_value * val_s[...] * (1.0 - sig)
    grad_gated = dot(grad_value.astype(bf16), glu_all[0].reshape(width, width)) + dot(
        grad_gate.astype(bf16), glu_all[1].reshape(width, width)
    )
    turn_out(grad_gated, tx3)
    to_members(lambda p: tx3.at[p], rx3, slot_me, A3 + own_micro)
    for j in range(z.peers // 2):
        gv = grad_value[:, j * LANES : (j + 1) * LANES]
        gg = shifted(grad_gate[:, j * LANES : (j + 1) * LANES], LANES // 2)
        gp_s[2 * j] = jnp.where(first_half, gv, gg).astype(bf16)
        gp_s[2 * j + 1] = jnp.where(first_half, gg, gv).astype(bf16)
    pl.when(pipe > 0)(lambda: remote(mid_s, mid_rx, MID, place(chan, data, pipe - 1)).start())
    pl.when(pipe == 0)(top_rows)

    @pl.when(pipe < last)
    def _():
        turn_out(gtop[...].astype(f32), ign_t)
        to_section_peers(lambda c: ign_t.at[c], ig_rx, IG, pipe + 1)
        to_section(lambda p: vgn_s.at[p // z.groups], vnrx, me, VGN, pipe + 1)

    for m in range(z.micros):
        wait_bytes(rx3.at[pl.ds(m * z.slots, z.slots)], recv.at[A3 + m])
        for i, tile in enumerate(lane_tiles(rx3, m)):
            masked_store(gs, 0, m, i, tile * gelu_slope(conv_out[m * z.blocks + i]))

        def back_one(h):
            ys[pl.ds(h, z.conv_rows, stride=z.ch), :] = dot_nt(windows(gs, m, h, False), far[h])

        each_channel(back_one, ch)
        tiles = [
            masked_sum(m, i) + skip[...] * whole_tile(gs, 0, m, i) for i in range(z.blocks)
        ]
        lane_pieces(tiles, m, tx4)
        pl.when(pipe == 0)(lambda: to_micro(m, tx4, rx4, A4))
        pl.when(pipe > 0)(lambda: to_micro(m, tx4, rx4n, A4N, pipe - 1))

    pl.when(pipe > 0)(top_rows)
    hidden_rows()

    @pl.when(pipe == last)
    def _():
        to_peers(lambda c: lay_t.at[c], hid_rx, HID)
        forward_rows()

    many = z.peers * rows
    grads = (
        (ac, AC, bg, BG, z.hid, width, pdown, kdown, sdown, ldown, ddown),
        (fi, FI, gh, GH, width, z.hid, pup, kup, sup, lup, dup),
        (gp, GP, ga, GA, 2 * z.cw, width, pglu, kglu, sglu, lglu, dglu),
    )

    def product(t):
        left, lp, right, rp, n_left, n_right, part, krx, *_ = grads[t]
        wait_bytes(left, recv.at[lp])
        wait_bytes(right, recv.at[rp])
        part[...] = dot_tn(left[...].reshape(many, n_left), right[...].reshape(many, n_right))
        half = n_left // 2
        other = pl.ds(pl.multiple_of((1 - core) * half, half), half)
        remote(part.at[other], krx, GRADS + 3 * t, sibling).start()

    def chip_sum(t):
        _, _, _, _, n_left, _, part, krx, lsend, lrx, _ = grads[t]
        half = n_left // 2
        own = pl.ds(pl.multiple_of(core * half, half), half)
        wait_bytes(krx, recv.at[GRADS + 3 * t])
        lsend[...] = (part[own, :] + krx[...]).astype(bf16)
        remote(lsend, lrx, GRADS + 3 * t + 1, across).start()

    def both_chips(t):
        _, _, _, _, n_left, _, _, _, lsend, lrx, final = grads[t]
        half = n_left // 2
        own = pl.ds(pl.multiple_of(core * half, half), half)
        wait_bytes(lrx, recv.at[GRADS + 3 * t + 1])
        final[own, :] = lsend[...].astype(f32) + lrx[...].astype(f32)
        remote(final.at[own], final.at[own], GRADS + 3 * t + 2, sibling).start()

    product(0)

    def lag_one(h):
        x = [
            xs[pl.ds(m * z.stack + pad_rows + h, z.conv_rows, stride=z.ch), :]
            for m in range(z.micros)
        ]
        g = jnp.concatenate([windows(gs, m, h, False) for m in range(z.micros)], axis=0)
        prod = dot_tn(jnp.concatenate(x, axis=0).astype(bf16), g)
        prod = jnp.concatenate([prod, jnp.zeros((LANES, LANES), f32)], axis=1)
        size = LANES // 2
        while size >= 8:
            prod = prod[:size] + shifted(prod[size:], wide - size)
            size //= 2
        for t in range(z.blocks + 1):
            rest_s[t, pl.ds(pl.multiple_of(h * 8, 8), 8), :] = prod[:, t * LANES : (t + 1) * LANES]

    def lag_rest():
        total = None
        for a in range(8):
            tiles = [rest_s[t, pl.ds(a, ch, stride=8), :] for t in range(z.blocks + 1)]
            part = shifted(jnp.concatenate(tiles, axis=1), wide - a)
            total = part if total is None else total + part
        lag_s[...] = total

    each_channel(lag_one, 4, 0, ch // 2)
    chip_sum(0)
    each_channel(lag_one, 4, ch // 2, ch)
    lag_rest()
    product(1)
    product(2)


    @pl.when(pipe == 0)
    def _():
        wait_bytes(rx4, recv.at[A4])
        grad_in = jnp.where(row_ok, turn_in(rx4), 0.0)
        hat = hat1_s[...]
        grad_res = mid_s[...] + norm_back(grad_in, hat, inv1_s[:, 0:1], full_row(vec_all, 0))
        turn_out(grad_res, ig_t)
        to_peers(lambda c: ig_t.at[c], ig_rx, IG)
        pair = (
            jnp.sum(grad_in * hat, axis=0, keepdims=True),
            jnp.sum(grad_in, axis=0, keepdims=True),
        )
        for c in range(z.peers):
            for r, row in enumerate(pair):
                vg0_s[c, r : r + 1, :] = row[:, (c // 2) * LANES : (c // 2 + 1) * LANES]
        to_members(lambda p: vg0_s.at[p // z.groups], vnrx, me, VGN)

    chip_sum(1)
    chip_sum(2)

    rows_of = [
        jnp.sum(grad_ffn * hat2, axis=0, keepdims=True),
        jnp.sum(grad_ffn, axis=0, keepdims=True),
        jnp.sum(grad_top, axis=0, keepdims=True),
    ]
    for c in range(z.peers):
        j = c // 2
        for r, row in enumerate(rows_of):
            vg_s[c, r : r + 1, :] = row[:, j * LANES : (j + 1) * LANES]
        vg_s[c, 3:4, :] = jnp.sum(gp_s[c].astype(f32), axis=0, keepdims=True)
        up_row = jnp.sum(gh_s[c].astype(f32), axis=0, keepdims=True)
        for r in range(per):
            vg_s[c, 4 + r : 5 + r, :] = up_row[:, r * LANES : (r + 1) * LANES]
    to_members(lambda p: vg_s.at[p // z.groups], vrx, me, VG)
    both = dot_nt(high_low(lag_s[:, 0 : z.length]), table[...])
    grad_spec = both[0:ch] + both[ch : 2 * ch]
    gk = (grad_spec[:, 0:padded], grad_spec[:, padded : 2 * padded])
    y_all, ms, cross, over = moments()
    g_top = times(conj(over), gk)
    g_top = (-cosine * g_top[0], -cosine * g_top[1])
    g_low = times(conj(times(times(cross, over), over)), gk)
    g_three = (cosine * cosine * g_low[0], cosine * cosine * g_low[1])
    g_ms = [gk, times(conj(ms[2]), g_top), times(conj(ms[1]), g_top), g_three]
    g_rise = None
    for v, (g_r, g_i) in enumerate(g_ms):
        gsum_s[v, :, 0:padded] = 2.0 * cosine * g_r
        gsum_s[v, :, padded : 2 * padded] = -2.0 * cosine * g_i
        gsum_s[4 + v, :, 0:padded] = 2.0 * y_all * g_i
        gsum_s[4 + v, :, padded : 2 * padded] = 2.0 * y_all * g_r
        part = 2.0 * (sums_s[12 + v] * g_r + sums_s[8 + v] * g_i)
        g_rise = part if g_rise is None else g_rise + part
    slope_s[...] = g_rise
    gcol_s[...] = jnp.zeros(gcol_s.shape, f32)
    gstep_s[...] = jnp.zeros(gstep_s.shape, f32)

    def split(x):
        high_part = x.astype(bf16)
        return high_part, (x - high_part.astype(f32)).astype(bf16)

    g_high, g_low = split(gsum_s[...].reshape(8 * ch, 2 * padded))
    own = [jnp.where(lax.rem(spot, ch) == h, cols[0], 0.0) for h in range(ch)]
    c_high, c_low = split(jnp.concatenate(own, axis=0))
    guw_s[...] = dot(c_high, g_high) + dot(c_high, g_low) + dot(c_low, g_high)
    uw_high, uw_low = split(uw_s[...])
    g_cols = dot_nt(uw_high, g_high) + dot_nt(uw_high, g_low) + dot_nt(uw_low, g_high)
    total = g_cols[0:nh]
    for h in range(1, ch):
        total = jnp.where(lax.rem(spot, ch) == h, g_cols[h * nh : (h + 1) * nh], total)
    gcol_s[0] = total

    def mode_one(h):
        at = pl.ds(pl.multiple_of(h * nh, nh), nh)
        u, w = uw_s[at, 0:padded], uw_s[at, padded : 2 * padded]
        gu, gw = guw_s[at, 0:padded], guw_s[at, padded : 2 * padded]
        double = column_of(1, h)[:, ch : ch + 1]
        y = rise_s[pl.ds(h, 1), 0:1] * sine
        even, cross_uw = u * u - w * w, 2.0 * u * w
        g_den_r = -(even * gu + cross_uw * gw)
        g_den_i = even * gw - cross_uw * gu
        ge = jnp.sum(cosine * cosine * g_den_r, axis=1, keepdims=True)
        gf = jnp.sum(cosine * y * g_den_i, axis=1, keepdims=True)
        acc = jnp.where(spot == h, ge, gcol_s[1])
        gcol_s[1] = jnp.where(spot == ch + h, gf, acc)
        gy = slope_s[pl.ds(h, 1), :] + jnp.sum(
            double * cosine * g_den_i - 2.0 * y * g_den_r, axis=0, keepdims=True
        )
        total_y = jnp.sum(y * gy, axis=1, keepdims=True)
        gstep_s[0:1, :] = jnp.where(spot == h, -total_y, gstep_s[0:1, :])

    each_channel(mode_one, 4)

    def unpacked(k, i):
        return shifted(gcol_s[k], LANES - i * ch)

    g_square, g_double = unpacked(1, 0), unpacked(1, 1)
    g_decay = 2.0 * decay * g_square + 2.0 * g_double
    g_rate = 2.0 * rate * g_square
    g_pairs = []
    for v, (v_r, v_i) in enumerate(pairs):
        g_alpha, g_beta = unpacked(0, v), unpacked(0, 4 + v)
        g_decay = g_decay + g_alpha * v_r
        if v_i is not None:
            g_rate = g_rate - g_alpha * v_i
        g_pairs.append((decay * g_alpha + g_beta, -rate * g_alpha))
    c_b, c_p, p_b = g_pairs[0], g_pairs[1], g_pairs[2]
    p_p = g_pairs[3][0]
    rank, into, out = (rank_r, rank_i), (in_r, in_i), (out_r, out_i)

    def plus(*terms):
        return sum(t[0] for t in terms), sum(t[1] for t in terms)

    g_out = plus(times(conj(into), c_b), times(conj(rank), c_p))
    g_in = plus(times(conj(out), c_b), times(rank, p_b))
    g_rank = plus(
        times(conj(out), c_p),
        times(into, conj(p_b)),
        (2.0 * rank_r * p_p, 2.0 * rank_i * p_p),
    )
    modes_tx[0:nh, :] = packed([g_decay, g_rate, *g_rank, *g_in, *g_out])
    modes_tx[nh : nh + 8, :] = gstep_s[...]
    skip_row = jnp.sum(jnp.where(diagonal, lag_s[:, 0:1], 0.0), axis=0, keepdims=True)
    modes_tx[nh + 1 : nh + 2, :] = skip_row
    for k in range(1, z.groups):
        remote(modes_tx, modes_rx.at[data], MODES, place(chan, lax.rem(data + k, z.groups))).start()
    pltpu.make_async_copy(modes_tx, modes_rx.at[data], recv.at[MODES]).start()

    for t in range(3):
        both_chips(t)

    def collect(source, target):
        count = tok * z.quarters
        for m in range(z.micros):
            tiles = []
            for i in range(-(-count // LANES)):
                lo, hi = i * LANES, min((i + 1) * LANES, count)
                tile = None
                for q in range(lo // tok, -(-hi // tok)):
                    piece = shifted(source[m * z.quarters + q].astype(f32), q * tok - lo)
                    first = max(0, q * tok - lo)
                    tile = piece if tile is None else jnp.where(spot >= first, piece, tile)
                tiles.append(tile)
            target[m] = jnp.concatenate(tiles, axis=1)[:, 0:count].astype(bf16)

    wait_bytes(hid_rx, recv.at[HID])
    collect(hid_rx, hid_out)
    wait_bytes(ig_rx, recv.at[IG])
    collect(ig_rx, ig_out)
    wait_bytes(vrx, recv.at[VG])
    wait_bytes(vnrx, recv.at[VGN])
    summed, summed_one = vrx[0], vnrx[0]
    for p in range(1, z.members):
        summed = summed + vrx[p]
        summed_one = summed_one + vnrx[p]
    upb_out[...] = jnp.concatenate([summed[4 + r : 5 + r, :] for r in range(per)], axis=1)
    summed, summed_one = own_half(summed), own_half(summed_one)
    for r in range(3):
        ffn_out[r] = summed[r : r + 1, 0 : z.cw]
    glub_out[0:1, :] = summed[3:4, 0 : z.cw]
    glub_out[1:2, :] = shifted(summed[3:4], LANES // 2)[:, 0 : z.cw]
    vec_out[0:2, :] = summed_one[0:2, 0 : z.cw]
    wait_bytes(modes_rx, recv.at[MODES])

    def over_groups(take):
        total = take(0)
        for d in range(1, z.groups):
            total = jnp.where(spot // ch == d, take(d), total)
        return total[:, 0 : z.cw]

    for p in range(8):
        modes_out[p] = over_groups(
            lambda d: shifted(modes_rx[d, 0:nh, :], (d - p) * ch)
        )
    for r in range(2):
        vec_out[2 + r : 3 + r, :] = over_groups(
            lambda d: shifted(modes_rx[d, nh + r : nh + r + 1, :], d * ch)
        )
    for t, (_, _, _, _, n_left, _, _, _, _, _, final) in enumerate(grads):
        half = n_left // 2
        other = pl.ds(pl.multiple_of((1 - core) * half, half), half)
        wait_bytes(final.at[other], recv.at[GRADS + 3 * t + 2])
    glu_out[0] = dglu[pl.ds(pl.multiple_of(odd * z.cw, z.cw), z.cw), :]
    glu_out[1] = dglu[pl.ds(pl.multiple_of((1 - odd) * z.cw, z.cw), z.cw), :]

    weights_all((weights_sent,), GLU, UPA, UPB, DNA, DNB)
    for ref, phase in (
        (vec_all, VEC), (hid_rx, HID), (ga, GA), (fi, FI), (ac, AC), (bg, BG), (gh, GH), (gp, GP),
    ):
        wait_bytes(ref.at[pl.ds(0, z.peers - 1)], send.at[phase])
    for ref, phase in ((rx2, A2), (rx3, A3 + own_micro), (vrx, VG)):
        wait_bytes(ref.at[pl.ds(0, z.members - 1)], send.at[phase])
    wait_bytes(modes_rx.at[pl.ds(0, z.groups - 1)], send.at[MODES])
    for t, (_, _, _, _, n_left, _, _, krx, lsend, _, final) in enumerate(grads):
        wait_bytes(krx, send.at[GRADS + 3 * t])
        wait_bytes(lsend, send.at[GRADS + 3 * t + 1])
        wait_bytes(final.at[pl.ds(0, n_left // 2)], send.at[GRADS + 3 * t + 2])

    @pl.when(pipe == 0)
    def _():
        wait_bytes(tok_rx.at[pl.ds(0, z.peers - 1)], send.at[TOK])
        wait_bytes(ig_rx.at[pl.ds(0, z.peers - 1)], send.at[IG])
        for ref, phase in ((rx1, A1 + own_micro), (rx4, A4), (vnrx, VGN)):
            wait_bytes(ref.at[pl.ds(0, z.members - 1)], send.at[phase])

    @pl.when(pipe == last)
    def _():
        wait_bytes(cot_rx.at[pl.ds(0, z.peers - 1)], send.at[COT])

    @pl.when(pipe < last)
    def _():
        for ref, phase in ((rx1, A1 + own_micro), (lay_s, RES), (ig_rx, IG), (vnrx, VGN)):
            wait_bytes(ref, send.at[phase])

    @pl.when(pipe > 0)
    def _():
        for ref, phase in ((vec_all, VECN), (mid_s, MID), (rx4, A4N)):
            wait_bytes(ref, send.at[phase])


def finish_kernel(*refs):
    count = (len(refs) - 1) // 3
    sems = refs[-1]
    sources, targets, held = refs[:count], refs[count : 2 * count], refs[2 * count : -1]
    loads = [pltpu.make_async_copy(sources[i], held[i], sems.at[i]) for i in range(count)]
    stores = [
        pltpu.make_async_copy(held[i], targets[i], sems.at[count + i]) for i in range(count)
    ]
    for load in loads:
        load.start()
    for load, store in zip(loads, stores):
        load.wait()
        store.start()
    for store in stores:
        store.wait()


def body(
    tokens,
    seq_lengths,
    out_cot,
    s4_vectors,
    s4_modes,
    glu_weight,
    glu_bias,
    ffn_vectors,
    up_weight,
    up_bias,
    down_weight,
):
    micros, tok_rows, chan_width = tokens.shape
    width = glu_weight.shape[1]
    hidden = up_weight.shape[2]
    z = Sizes(
        lax.axis_size("pipe"), lax.axis_size("chan"), lax.axis_size("dp"),
        tok_rows, chan_width, width, hidden,
    )
    length = z.length
    padded = -(-(length // 2 + 1) // LANES) * LANES
    nh = s4_modes.shape[3]
    table = jnp.asarray(fourier_table(length, padded).astype(ml_dtypes.bfloat16))
    angles = jnp.asarray(half_angles(length, padded))

    vmem = pl.BlockSpec(memory_space=pltpu.VMEM)
    smem = pl.BlockSpec(memory_space=pltpu.SMEM)
    anywhere = pl.BlockSpec(memory_space=pl.ANY)
    n, r, w, ch = z.peers, z.rows, width, z.ch

    def s(shape, kind=f32):
        return jax.ShapeDtypeStruct(shape, kind)

    def v(shape, kind=bf16):
        return pltpu.VMEM(shape, kind)

    wide = (z.blocks + 1) * LANES
    rows_full, rows_wide, side = v((r, w)), v((r, w), f32), v((r, LANES), f32)
    peer_tiles, exchange = v((n, chan_width, LANES)), v((z.members, z.ch, LANES))
    small = v((n, 8, LANES), f32)
    results = (
        s((micros, chan_width, tok_rows), bf16), s((micros, chan_width, tok_rows), bf16),
        s((4, chan_width)), s((8, nh, chan_width)), s((2, chan_width, w)),
        s((2, chan_width)), s((3, 1, chan_width)), s((w, hidden)), s((1, hidden)),
        s((hidden, w)),
    )
    raw = pl.pallas_call(
        lambda *refs: main_kernel(z, *refs),
        out_shape=results,
        in_specs=[smem] + [vmem] * 11 + [anywhere],
        out_specs=[vmem] * 10,
        scratch_shapes=[
            peer_tiles, peer_tiles, v((16, LANES), f32), v((ch, length, LANES)),
            v((ch, LANES, length)), v((ch, LANES), f32), v((40, LANES), f32),
            peer_tiles, peer_tiles, v((micros * z.stack, LANES), f32),
            v((micros * z.stack, LANES), f32),
            v((2 * padded, length)), v((2, nh, LANES), f32),
            v((ch, LANES), f32), v((16, ch, padded), f32), v((ch * nh, 2 * padded), f32),
            v((ch * nh, 2 * padded), f32), v((z.blocks + 1, 8 * ch, LANES), f32),
            v((8, ch, 2 * padded), f32),
            v((ch, padded), f32), v((ch, wide), f32), v((ch, wide), f32),
            v((2, nh, LANES), f32), v((8, LANES), f32),
            v((nh + 8, LANES), f32), v((z.groups, nh + 8, LANES), f32),
            v((2 * chan_width, w), f32), v((w, hidden), f32), v((hidden, w), f32),
            v((chan_width, w), f32), v((w // 2, hidden), f32), v((hidden // 2, w), f32),
            v((chan_width, w)), v((w // 2, hidden)), v((hidden // 2, w)),
            v((chan_width, w)), v((w // 2, hidden)), v((hidden // 2, w)),
            v((2 * chan_width, w), f32),
            v((n, 16, LANES), f32), v((n, 16, LANES), f32),
            v((2, n, chan_width, w)), v((n, w, hidden)),
            v((n, hidden, w)), peer_tiles, peer_tiles, rows_full, rows_full,
        ]
        + [exchange] * 10
        + [
            v((z.micros * z.blocks, z.ch, LANES), f32), v((z.conv_rows * z.ch, LANES), f32),
            rows_wide, side, rows_wide, side, rows_wide, side,
            rows_wide, rows_wide, v((n, r, hidden), f32),
            rows_full, rows_full, v((n, r, hidden)), v((n, r, hidden)), v((n, r, LANES)),
            rows_full, peer_tiles, peer_tiles, peer_tiles, rows_wide, rows_wide,
            small, small, small,
            v((n, r, w)), v((n, r, w)), v((n, r, hidden)), v((n, r, w)), v((n, r, hidden)),
            v((n, r, LANES)), v((z.members, 8, LANES), f32), v((z.members, 8, LANES), f32),
            pltpu.SemaphoreType.DMA((64,)), pltpu.SemaphoreType.DMA((64,)),
        ],
        compiler_params=pltpu.CompilerParams(
            collective_id=0, has_side_effects=True, vmem_limit_bytes=60 * 2**20
        ),
        name="layers",
    )(
        seq_lengths, tokens.transpose(0, 2, 1), out_cot.transpose(0, 2, 1), s4_vectors[0],
        s4_modes[0].transpose(0, 2, 1), glu_weight[0].transpose(1, 2, 0), glu_bias[0],
        ffn_vectors.transpose(1, 0, 2), up_weight[0], up_bias, down_weight[0], angles, table,
    )
    hid, ig, vec, modes, dglu, glub, ffn, dup, upb, ddown = pl.pallas_call(
        finish_kernel,
        out_shape=results,
        in_specs=[anywhere] * 10,
        out_specs=[anywhere] * 10,
        scratch_shapes=[pltpu.VMEM(x.shape, x.dtype) for x in results]
        + [pltpu.SemaphoreType.DMA((20,))],
        compiler_params=pltpu.CompilerParams(vmem_limit_bytes=60 * 2**20),
        name="finish",
    )(*raw)
    return (
        hid.transpose(0, 2, 1)[None], ig.transpose(0, 2, 1)[None], vec[None],
        modes.transpose(0, 2, 1)[None], dglu.transpose(2, 0, 1)[None], glub[None],
        ffn.transpose(1, 0, 2), dup[None], upb, ddown[None],
    )


def solution(mesh):
    placed = (
        P(None, "dp", "chan"),
        P(),
        P(None, "dp", "chan"),
        P("pipe", None, "chan"),
        P("pipe", None, "chan", None),
        P("pipe", None, None, "chan"),
        P("pipe", None, "chan"),
        P("pipe", None, "chan"),
        P("pipe", None, "chan"),
        P("pipe", "chan"),
        P("pipe", "chan", None),
    )
    return jax.shard_map(
        body,
        mesh=mesh,
        in_specs=placed,
        out_specs=(
            P("pipe", None, "dp", "chan"),
            P("pipe", None, "dp", "chan"),
            P("pipe", None, "chan"),
            P("pipe", None, "chan", None),
            P("pipe", None, None, "chan"),
            P("pipe", None, "chan"),
            P("pipe", None, "chan"),
            P("pipe", None, "chan"),
            P("pipe", "chan"),
            P("pipe", "chan", None),
        ),
        check_vma=False,
    )
```

```python
import math

import jax
import jax.numpy as jnp
import ml_dtypes
import numpy as np
from jax import lax
from jax.experimental import pallas as pl
from jax.experimental.pallas import tpu as pltpu
from jax.sharding import PartitionSpec as P

norm_eps = 1e-05
f32 = jnp.float32
bf16 = jnp.bfloat16
LANES = 128


def fourier_table(length, padded):
    half = length // 2
    freq = np.arange(padded, dtype=np.int64)[:, None]
    time = np.arange(length, dtype=np.int64)[None, :]
    angle = (freq * (2 * time + 1) % (2 * length)) * (np.pi / length)
    weight = np.where(freq <= half, np.where((freq == 0) | (freq == half), 1.0, 2.0), 0.0) / length
    table = np.concatenate([np.cos(angle) * weight, -np.sin(angle) * weight], axis=0)
    return table.astype(np.float32)


def half_angles(length, padded):
    angle = np.minimum(np.arange(padded), length // 2) * (np.pi / length)
    rows = np.zeros((8, padded), np.float32)
    rows[0] = np.where(np.arange(padded) < length // 2, np.cos(angle), 0.0)
    rows[1] = np.sin(angle)
    return rows


def shifted(x, by):
    size = x.shape[-1]
    by = by % size
    if by == 0:
        return x
    return pltpu.roll(x, by, x.ndim - 1)


def gelu(x):
    return 0.5 * x * (1.0 + jnp.tanh(math.sqrt(2.0 / math.pi) * (x + 0.044715 * x * x * x)))


def gelu_slope(x):
    scale = math.sqrt(2.0 / math.pi)
    t = jnp.tanh(scale * (x + 0.044715 * x * x * x))
    return 0.5 * (1.0 + t) + 0.5 * x * (1.0 - t * t) * scale * (1.0 + 3.0 * 0.044715 * x * x)


def dot(a, b):
    return lax.dot_general(a, b, (((1,), (0,)), ((), ())), preferred_element_type=f32)


def dot_nt(a, b):
    return lax.dot_general(a, b, (((1,), (1,)), ((), ())), preferred_element_type=f32)


def dot_tn(a, b):
    return lax.dot_general(a, b, (((0,), (0,)), ((), ())), preferred_element_type=f32)


class Sizes:
    def __init__(self, sections, peers, groups, tok_rows, chan_width, model_width, hidden):
        self.sections, self.peers, self.groups = sections, peers, groups
        self.micros = 2
        self.segments = 2
        self.quarters = peers // self.micros
        self.tok = tok_rows // self.quarters
        self.rows = -(-self.tok // 16) * 16
        self.length = tok_rows * groups
        self.blocks = self.length // LANES
        self.local = tok_rows
        self.over = -(-tok_rows // LANES) * LANES
        self.width = model_width
        self.cw = chan_width
        self.hid = hidden
        self.members = peers * groups
        self.ch = model_width // self.members
        self.slots = self.quarters * groups
        self.conv_rows = -(-(self.blocks * self.segments) // 8) * 8
        spare = -(-(self.conv_rows - self.blocks * self.segments) // self.segments)
        self.stack = (2 * self.blocks - 1 + spare) * self.segments * self.ch


def main_kernel(z, *refs):
    (
        lengths, tokens, out_cot, vectors, modes, glu_loc, glu_bias, ffn_vec, up_loc, up_bias,
        down_loc, angles, table_in,
    ) = refs[:13]
    (
        hid_out, ig_out, vec_out, modes_out, glu_out, glub_out, ffn_out, dup, upb_out, ddown,
    ) = refs[13:23]
    (
        tok_tx, cot_tx, vec_tx, near, far, skip, masks, hid_rx, ig_rx, xs, gs,
        table, cols, rise_s, sums_s, uw_s, guw_s, rest_s, gsum_s, slope_s, kern_s, lag_s, gcol_s, gstep_s,
        modes_tx, modes_rx, pglu, pup, pdown, kglu, kup, kdown, sglu, sup, sdown,
        lglu, lup, ldown, dglu,
        vec_all, vec_next, glu_all, up_all, down_all, tok_rx, cot_rx, res, gtop,
        tx1n, rx1, tx2, rx2, tx3, rx3, tx4, rx4, rx4n,
        conv_out, ys, hatn_s, invn_s, hat2_s, inv2_s, val_s, sig_s, hidden_s,
        gated_s, ffn_s, act_s, gh_s, gp_s, lay_s, lay_t, ig_t, ign_t, mid_s, mid_rx,
        stat_tx, stat_rx, entry_tx, entry_rx, vg_s, vgn_s, vg0_s, ga, fi, ac, bg, gh, gp, vrx, vnrx, send, recv,
    ) = refs[23:]
    pipe = lax.axis_index("pipe")
    chan = lax.axis_index("chan")
    data = lax.axis_index("dp")
    last = z.sections - 1
    me = chan * z.groups + data
    slot_me = (chan // z.quarters) * z.slots + data * z.quarters + lax.rem(chan, z.quarters)
    rows, width, tok = z.rows, z.width, z.tok
    spot = lax.broadcasted_iota(jnp.int32, (1, LANES), 1)
    first_half = spot < (LANES // 2)
    row_ok = lax.broadcasted_iota(jnp.int32, (rows, 1), 0) < tok
    odd = lax.rem(chan, 2)
    per = z.hid // LANES

    high, deep = chan // z.quarters, lax.rem(chan, z.quarters)
    side, core = data // 2, lax.rem(data, 2)
    height = 2 * high + side

    def slot_of(p):
        c, d = p // z.groups, lax.rem(p, z.groups)
        return (c // z.quarters) * z.slots + d * z.quarters + lax.rem(c, z.quarters)

    def place(c, d, section=None):
        return {"pipe": pipe if section is None else section, "chan": c, "dp": d}

    def member(p, section=None):
        return place(p // z.groups, lax.rem(p, z.groups), section)

    def remote(src, dst, phase, where):
        return pltpu.make_async_remote_copy(
            src_ref=src,
            dst_ref=dst,
            send_sem=send.at[phase],
            recv_sem=recv.at[phase],
            device_id=where,
            device_id_type=pl.DeviceIdType.MESH,
        )

    def wait_bytes(ref, sem):
        pltpu.make_async_copy(ref, ref, sem).wait()

    def to_peers(src_of, dst, phase):
        def step(k, carry):
            c = lax.rem(chan + k, z.peers)
            remote(src_of(c), dst.at[chan], phase, place(c, data)).start()
            return carry

        lax.fori_loop(1, z.peers, step, 0)
        pltpu.make_async_copy(src_of(chan), dst.at[chan], recv.at[phase]).start()

    def far_first(i):
        return lax.rem(2 + i + (i // 2) * (2 * i - 3), 4)

    def number(y, depth, core_there):
        return ((y // 2) * z.quarters + depth) * z.groups + lax.rem(y, 2) * 2 + core_there

    def to_all(src_of, dst, slot, phase, section=None):
        def chip(k):
            y = lax.rem(height + far_first(k // 4), 4)
            return y, lax.rem(deep + far_first(lax.rem(k, 4)), 4)

        def step(k, carry):
            y, depth = chip(k)
            for c in range(2):
                p = number(y, depth, c)
                remote(src_of(p), dst.at[slot], phase, member(p, section)).start()
            return carry

        chips = z.members // 2
        lax.fori_loop(0, chips if section is not None else chips - 1, step, 0)
        if section is None:
            p = number(height, deep, 1 - core)
            remote(src_of(p), dst.at[slot], phase, member(p)).start()
            pltpu.make_async_copy(src_of(me), dst.at[slot], recv.at[phase]).start()

    def to_members(src_of, dst, slot, phase):
        to_all(src_of, dst, slot, phase)

    def to_section(src_of, dst, slot, phase, section):
        to_all(src_of, dst, slot, phase, section)

    def to_micro(m, source, dst, phase, section=None):
        near_by = jnp.where(own_micro == m, 1, 0)

        def send_to(p):
            remote(source.at[slot_of(p)], dst.at[me], phase, member(p, section)).start()

        def chip(k):
            y = 2 * m + lax.rem(side + near_by + k // 4, 2)
            return y, lax.rem(deep + far_first(lax.rem(k, 4)), 4)

        def step(k, carry):
            y, depth = chip(k)
            for c in range(2):
                send_to(number(y, depth, c))
            return carry

        lax.fori_loop(0, z.slots // 2 - 1, step, 0)
        if section is not None:
            step(z.slots // 2 - 1, 0)
            return

        @pl.when(own_micro == m)
        def _():
            send_to(number(height, deep, 1 - core))
            block = source.at[slot_of(me)]
            pltpu.make_async_copy(block, dst.at[me], recv.at[phase]).start()

        @pl.when(own_micro != m)
        def _():
            step(z.slots // 2 - 1, 0)

    def to_section_peers(src_of, dst, phase, section):
        def step(k, carry):
            c = lax.rem(chan + k, z.peers)
            remote(src_of(c), dst.at[chan], phase, place(c, data, section)).start()
            return carry

        lax.fori_loop(0, z.peers, step, 0)

    (
        VEC, VECN, TOK, COT, A2, A4, A4N, RES, MID, HID, IG, GA, FI, AC, GH, GP, VG,
        VGN, TABLE, MODES,
    ) = range(20)
    STAT, ENTRY = 66, 67
    A1, A3, GLU, UPA, UPB, DNA, DNB, GRADS, BG = 21, 23, 25, 31, 37, 43, 49, 55, 64
    direct = (DNB,)
    own_micro = chan // z.quarters

    own_side, far_side = high * z.quarters, (1 - high) * z.quarters
    sibling, across = place(chan, side * 2 + 1 - core), place(chan, (1 - side) * 2 + core)

    def columns(t):
        if t == GLU:
            return glu_loc, glu_all
        loc, whole = (up_loc, up_all) if t in (UPA, UPB) else (down_loc, down_all)
        count = loc.shape[1] // 2
        where = pl.ds(count if t in (UPB, DNB) else 0, count)
        return loc.at[:, where], whole.at[:, :, where]

    def own_rows(t, part=None):
        loc, _ = columns(t)
        if t == GLU:
            fourth = z.cw // 2
            half = loc.at[core]
            return half if part is None else half.at[pl.ds(pl.multiple_of(part * fourth, fourth), fourth)]
        half = loc.shape[0] // 2
        if part is None:
            return loc.at[pl.ds(pl.multiple_of(core * half, half), half)]
        fourth = half // 2
        return loc.at[pl.ds(pl.multiple_of(core * half + part * fourth, fourth), fourth)]

    def piece_of(t, c, count, part=None):
        loc, whole = columns(t)
        if t == GLU:
            fourth = z.cw // 2
            if part is None:
                return whole.at[core, pl.ds(c, count)]
            start = pl.multiple_of(part * fourth, fourth)
            return whole.at[core, pl.ds(c, count), pl.ds(start, fourth)]
        half = loc.shape[0] // 2
        fourth = half // 2
        if part is None:
            return whole.at[pl.ds(c, count), pl.ds(pl.multiple_of(core * half, half), half)]
        start = pl.multiple_of(core * half + part * fourth, fourth)
        return whole.at[pl.ds(c, count), pl.ds(start, fourth)]

    def weights_out(t):
        loc, whole = columns(t)
        whole = whole.at[:, chan] if t == GLU else whole.at[chan]
        pltpu.make_async_copy(loc, whole, recv.at[t + 5]).start()
        part = None if t in direct else side
        payload, there = own_rows(t, part), piece_of(t, chan, 1, part).at[0]
        for k in (2, 3, 1, 0):
            c = far_side + lax.rem(deep + k, z.quarters)
            remote(payload, there, t + 1, place(c, (1 - side) * 2 + core)).start()
        payload, there = own_rows(t), piece_of(t, chan, 1).at[0]
        for k in (2, 3, 1):
            c = own_side + lax.rem(deep + k, z.quarters)
            remote(payload, there, t, place(c, data)).start()

    def weights_beside(t):
        if t in direct:
            return
        wait_bytes(piece_of(t, 0, z.quarters, 0), recv.at[t + 1])
        piece = piece_of(t, far_side, z.quarters, 1 - side)
        remote(piece, piece, t + 2, across).start()

    def weights_near(t):
        wait_bytes(piece_of(t, 0, z.quarters - 1), recv.at[t])
        for k in range(1, z.quarters):
            piece = piece_of(t, own_side + lax.rem(deep + k, z.quarters), 1)
            remote(piece, piece, t + 3, sibling).start()

    def weights_core(t):
        if t in direct:
            wait_bytes(piece_of(t, 0, z.quarters), recv.at[t + 1])
        else:
            wait_bytes(piece_of(t, 0, z.quarters, 0), recv.at[t + 2])
        piece = piece_of(t, far_side, z.quarters)
        remote(piece, piece, t + 4, sibling).start()

    def weights_here(t):
        wait_bytes(columns(t)[0], recv.at[t + 5])
        wait_bytes(piece_of(t, 0, z.quarters - 1), recv.at[t + 3])
        wait_bytes(piece_of(t, 0, z.quarters), recv.at[t + 4])

    def weights_sent(t):
        far_part = None if t in direct else 0
        stages = [(0, z.quarters - 1, None), (1, z.quarters, far_part)]
        if t not in direct:
            stages.append((2, z.quarters, 0))
        stages += [(3, z.quarters - 1, None), (4, z.quarters, None)]
        for stage, count, part in stages:
            wait_bytes(piece_of(t, 0, count, part), send.at[t + stage])

    def weights_all(steps, *which):
        for t in which:
            for step in steps:
                step(t)

    forward_steps = (weights_beside, weights_near)

    barrier = pltpu.get_barrier_semaphore()

    def greet(where):
        pl.semaphore_signal(barrier, inc=1, device_id=where, device_id_type=pl.DeviceIdType.MESH)

    def greet_own(k, carry):
        greet(member(lax.rem(me + k, z.members)))
        return carry

    pl.when(pipe < last)(lambda: greet(place(chan, data, pipe + 1)))
    pl.when(pipe > 0)(lambda: greet(place(chan, data, pipe - 1)))
    lax.fori_loop(1, z.members, greet_own, 0)
    pltpu.make_async_copy(table_in, table, recv.at[TABLE]).start()

    def own_half(x):
        return pltpu.roll(x, odd * (LANES // 2), x.ndim - 1)

    stat_tx[...] = jnp.zeros(stat_tx.shape, f32)

    def fill_blocks(source, target):
        count = z.tok * z.quarters
        over = -(-count // LANES) * LANES
        for m in range(z.micros):
            x = source[m].astype(f32)
            x = jnp.concatenate([x, jnp.zeros((z.cw, over - count), f32)], axis=1)
            for q in range(z.quarters):
                target[m * z.quarters + q] = shifted(x, over - q * tok)[:, 0:LANES].astype(bf16)

    vec_rows = [vectors[0:1, :], vectors[1:2, :]] + [ffn_vec[r] for r in range(3)]
    vec_rows += [glu_bias[0:1, :], glu_bias[1:2, :]]
    for r, row in enumerate(vec_rows):
        vec_tx[r : r + 1, :] = jnp.concatenate([row, row], axis=1)
    for r in range(per):
        vec_tx[7 + r : 8 + r, :] = up_bias[:, r * LANES : (r + 1) * LANES].astype(f32)
    pl.when(pipe == 0)(lambda: fill_blocks(tokens, tok_tx))
    pl.when(pipe == last)(lambda: fill_blocks(out_cot, cot_tx))

    ch, nh = z.ch, modes.shape[1]

    def own_lanes(x):
        x = jnp.concatenate([x, jnp.zeros((x.shape[0], LANES - z.cw), f32)], axis=1)
        return pltpu.roll(x, lax.rem(LANES - data * ch, LANES), 1)

    def packed(items):
        total = items[0]
        for i, item in enumerate(items[1:], 1):
            total = jnp.where(spot // ch == i, shifted(item, i * ch), total)
        return total

    decay, rate, rank_r, rank_i, in_r, in_i, out_r, out_i = (own_lanes(modes[p]) for p in range(8))
    pairs = [
        (out_r * in_r - out_i * in_i, out_r * in_i + out_i * in_r),
        (out_r * rank_r - out_i * rank_i, out_r * rank_i + out_i * rank_r),
        (rank_r * in_r + rank_i * in_i, rank_r * in_i - rank_i * in_r),
        (rank_r * rank_r + rank_i * rank_i, None),
    ]
    alphas = [
        decay * v_r if v_i is None else decay * v_r - rate * v_i for v_r, v_i in pairs
    ]
    cols[0] = packed(alphas + [v_r for v_r, v_i in pairs])
    cols[1] = packed([decay * decay + rate * rate, 2.0 * decay])
    own_vectors = own_lanes(vectors[...])
    diagonal = lax.broadcasted_iota(jnp.int32, (ch, LANES), 0) == lax.broadcasted_iota(
        jnp.int32, (ch, LANES), 1
    )

    def upright(row):
        column = jnp.sum(jnp.where(diagonal, row, 0.0), axis=1, keepdims=True)
        return jnp.broadcast_to(column, (ch, LANES))

    rise_s[...] = 2.0 * jnp.exp(-upright(own_vectors[2:3]))
    skip[...] = upright(own_vectors[3:4])
    cosine, sine = angles[0:1, :], angles[1:2, :]
    padded = angles.shape[1]

    def column_of(k, h):
        return pltpu.roll(cols[k], lax.rem(LANES - h, LANES), 1)

    def modes_at(h):
        two = column_of(1, h)
        square, double = two[:, 0:1], two[:, ch : ch + 1]
        y = rise_s[pl.ds(h, 1), 0:1] * sine
        cy = cosine * y
        den_r = square * (cosine * cosine) - y * y
        den_i = double * cy
        inverse = 1.0 / (den_r * den_r + den_i * den_i)
        return double, y, cy, den_r * inverse, den_i * inverse

    def cauchy_one(h):
        _, _, _, u, w = modes_at(h)
        at = pl.ds(pl.multiple_of(h * nh, nh), nh)
        uw_s[at, 0:padded] = u
        uw_s[at, padded : 2 * padded] = w
        column = column_of(0, h)
        for v in range(4):
            a = column[:, v * ch : v * ch + 1]
            b = column[:, (4 + v) * ch : (4 + v) * ch + 1]
            sums_s[v, pl.ds(h, 1), :] = jnp.sum(a * u, axis=0, keepdims=True)
            sums_s[4 + v, pl.ds(h, 1), :] = jnp.sum(a * w, axis=0, keepdims=True)
            sums_s[8 + v, pl.ds(h, 1), :] = jnp.sum(b * u, axis=0, keepdims=True)
            sums_s[12 + v, pl.ds(h, 1), :] = jnp.sum(b * w, axis=0, keepdims=True)

    def each_channel(one, unroll, first=0, end=None):
        def step(i, carry):
            for u in range(unroll):
                one(i * unroll + u)
            return carry

        if unroll == ch:
            step(0, 0)
        else:
            lax.fori_loop(first // unroll, (ch if end is None else end) // unroll, step, 0)

    def times(a, b):
        return a[0] * b[0] - a[1] * b[1], a[0] * b[1] + a[1] * b[0]

    def conj(a):
        return a[0], -a[1]

    def moments():
        y_all = rise_s[:, 0:1] * sine
        ms = [
            (
                2.0 * (cosine * sums_s[v] + y_all * sums_s[12 + v]),
                2.0 * (y_all * sums_s[8 + v] - cosine * sums_s[4 + v]),
            )
            for v in range(4)
        ]
        low_r, low_i = 1.0 + cosine * ms[3][0], cosine * ms[3][1]
        size = 1.0 / (low_r * low_r + low_i * low_i)
        return y_all, ms, times(ms[1], ms[2]), (low_r * size, -low_i * size)

    def high_low(x):
        high_part = x.astype(bf16)
        low_part = (x - high_part.astype(f32)).astype(bf16)
        return jnp.concatenate([high_part, low_part], axis=0)

    each_channel(cauchy_one, 4)
    pad_rows = (z.blocks - 1) * z.segments * z.ch
    data_rows = z.blocks * z.segments * z.ch
    for m in range(z.micros):
        at = m * z.stack
        xs[at : at + pad_rows, :] = jnp.zeros((pad_rows, LANES), f32)
        rest = z.stack - pad_rows - data_rows
        xs[at + z.stack - rest : at + z.stack, :] = jnp.zeros((rest, LANES), f32)
        rest = z.stack - data_rows
        gs[at + data_rows : at + z.stack, :] = jnp.zeros((rest, LANES), f32)
    for m in range(z.micros):
        first_len, second_len = lengths[m, 0], lengths[m, 1]
        for i in range(z.blocks):
            at = (m * z.blocks + i) * z.segments
            where = spot + i * LANES
            masks[at : at + 1, :] = jnp.where(where < first_len, 1.0, 0.0)
            inside = jnp.where(where < first_len + second_len, 1.0, 0.0)
            masks[at + 1 : at + 2, :] = jnp.where(where >= first_len, inside, 0.0)

    pl.semaphore_wait(
        barrier,
        z.members - 1 + jnp.minimum(pipe, 1) + jnp.minimum(last - pipe, 1),
    )

    @pl.when(pipe == 0)
    def _():
        for m in range(z.micros):
            x = tokens[m].astype(f32)
            stat_tx[2 * m : 2 * m + 1, 0 : z.local] = jnp.sum(x, axis=0, keepdims=True)
            stat_tx[2 * m + 1 : 2 * m + 2, 0 : z.local] = jnp.sum(x * x, axis=0, keepdims=True)
        to_peers(lambda c: stat_tx, stat_rx, STAT)
        to_peers(lambda c: tok_tx.at[c], tok_rx, TOK)

    to_peers(lambda c: vec_tx, vec_all, VEC)
    weights_out(GLU)
    pl.when(pipe == 0)(lambda: weights_all((weights_out,), UPA, UPB))

    @pl.when(pipe == last)
    def _():
        to_peers(lambda c: cot_tx.at[c], cot_rx, COT)


    y_all, ms, cross, over = moments()
    fix = times(cross, over)
    spec = jnp.concatenate([ms[0][0] - cosine * fix[0], ms[0][1] - cosine * fix[1]], axis=1)
    wait_bytes(table, recv.at[TABLE])
    both = dot(high_low(spec), table[...])
    wide = (z.blocks + 1) * LANES
    kern_s[:, 0 : z.length] = both[0:ch] + both[ch : 2 * ch]
    kern_s[:, z.length : wide] = jnp.zeros((ch, wide - z.length), f32)

    def norm_stats(v):
        mean = jnp.sum(v, axis=1, keepdims=True) * (1.0 / width)
        spread = jnp.sum(v * v, axis=1, keepdims=True) * (1.0 / width) - mean * mean
        inv = lax.rsqrt(spread + norm_eps)
        return (v - mean) * inv, inv

    def norm_back(e, hat, inv, gain):
        dh = e * gain
        first = jnp.sum(dh, axis=1, keepdims=True) * (1.0 / width)
        second = jnp.sum(dh * hat, axis=1, keepdims=True) * (1.0 / width)
        return inv * (dh - first - hat * second)

    def turn_out(v, ref):
        tall = jnp.concatenate([v, jnp.zeros((LANES - rows, width), f32)], axis=0)
        ref[...] = tall.T.astype(bf16).reshape(ref.shape)

    def turn_in(ref):
        return ref[...].reshape(width, LANES).astype(f32).T[:rows]

    def full_row(source, r):
        tiles = [
            jnp.where(first_half, source[2 * j, r : r + 1, :], source[2 * j + 1, r : r + 1, :])
            for j in range(z.peers // 2)
        ]
        return jnp.concatenate(tiles, axis=1)

    @pl.when(pipe == 0)
    def _():
        tall = lax.broadcasted_iota(jnp.int32, (z.cw, LANES), 0) == spot

        def upright_all(r):
            row = jnp.concatenate([vectors[r : r + 1, :], jnp.zeros((1, LANES - z.cw), f32)], axis=1)
            return jnp.sum(jnp.where(tall, row, 0.0), axis=1, keepdims=True)

        gain, bias = upright_all(0), upright_all(1)
        wait_bytes(stat_rx, recv.at[STAT])
        total = stat_rx[0]
        for c in range(1, z.peers):
            total = total + stat_rx[c]
        total = total * (1.0 / width)
        for m in range(z.micros):
            mean = total[2 * m : 2 * m + 1, 0 : z.local]
            spread = total[2 * m + 1 : 2 * m + 2, 0 : z.local] - mean * mean
            hat = (tokens[m].astype(f32) - mean) * lax.rsqrt(spread + norm_eps)
            normed = (hat * gain + bias).astype(bf16)
            for d in range(z.groups):
                entry_tx[d, m, :, 0 : z.local] = normed[d * ch : (d + 1) * ch, :]
        for k in range(1, z.groups):
            d = lax.rem(data + k, z.groups)
            remote(entry_tx.at[d], entry_rx.at[data], ENTRY, place(chan, d)).start()
        pltpu.make_async_copy(entry_tx.at[data], entry_rx.at[data], recv.at[ENTRY]).start()

    pl.when(pipe == 0)(lambda: weights_out(DNA))
    wait_bytes(vec_all, recv.at[VEC])

    @pl.when(pipe > 0)
    def _():
        remote(vec_all, vec_next, VECN, place(chan, data, pipe - 1)).start()


    @pl.when(pipe > 0)
    def _():
        weights_all((weights_out,), UPA, UPB, DNA, DNB)

    def toeplitz_one(h):
        full = jnp.broadcast_to(kern_s[pl.ds(h, 1), :], (LANES, wide))
        full = pltpu.roll(full, 0, 1, stride=1, stride_axis=0).astype(bf16)
        for d in range(z.blocks):
            near[h, d * LANES : (d + 1) * LANES, :] = full[:, d * LANES : (d + 1) * LANES]

    each_channel(toeplitz_one, 2)

    def reversed_one(h):
        full = jnp.broadcast_to(lag_s[pl.ds(h, 1), :], (LANES, wide))
        full = pltpu.roll(full, 0, 1, stride=1, stride_axis=0).astype(bf16)
        for d in range(z.blocks):
            at = (z.blocks - 1 - d) * LANES
            far[h, d * LANES : (d + 1) * LANES, :] = full[:, at : at + LANES]

    def reversed_kernel():
        down = lax.broadcasted_iota(jnp.int32, (LANES, LANES), 0)
        along = lax.broadcasted_iota(jnp.int32, (LANES, LANES), 1)
        flip = jnp.where(down + along == LANES - 1, 1.0, 0.0).astype(bf16)
        tiles = [
            dot(kern_s[:, t * LANES : (t + 1) * LANES].astype(bf16), flip)
            for t in reversed(range(z.blocks + 1))
        ]
        lag_s[...] = shifted(jnp.concatenate(tiles, axis=1), wide - (2 * LANES - 1))
        each_channel(reversed_one, 2)

    weights_all(forward_steps, GLU)

    @pl.when(pipe > 0)
    def _():
        weights_all(forward_steps, UPA, UPB, DNA, DNB)
        weights_all((weights_core,), UPA, UPB, DNA, DNB)

    weights_core(GLU)

    def lane_tiles(pieces, size):
        tiles = []
        for i in range(z.blocks):
            lo, hi = i * LANES, (i + 1) * LANES
            tile = None
            for k in range(lo // size, -(-hi // size)):
                piece = shifted(pieces(k).astype(f32), k * size - lo)[:, 0:LANES]
                first = max(0, k * size - lo)
                if tile is None:
                    tile = piece
                else:
                    tile = jnp.where(spot >= first, piece, tile)
            tiles.append(tile)
        return tiles

    def lane_pieces(tiles, m, ref):
        for k in range(z.slots):
            i, off = divmod(k * tok, LANES)
            piece = shifted(tiles[i], LANES - off)
            if off + tok > LANES:
                piece = jnp.where(spot < LANES - off, piece, shifted(tiles[i + 1], LANES - off))
            ref[m * z.slots + k] = piece.astype(bf16)

    def row_at(m, i, q):
        return m * z.stack + (i * z.segments + q) * z.ch

    def mask_of(m, i, q):
        at = (m * z.blocks + i) * z.segments + q
        return masks[at : at + 1, :]

    def masked_store(ref, base, m, i, tile):
        for q in range(z.segments):
            at = base + row_at(m, i, q)
            ref[at : at + z.ch, :] = tile * mask_of(m, i, q)

    def masked_sum(m, i):
        total = None
        for q in range(z.segments):
            at = row_at(0, i, q)
            part = ys[at : at + z.ch, :] * mask_of(m, i, q)
            total = part if total is None else total + part
        return total

    def whole_tile(ref, base, m, i):
        total = None
        for q in range(z.segments):
            at = base + row_at(m, i, q)
            total = ref[at : at + z.ch, :] if total is None else total + ref[at : at + z.ch, :]
        return total

    def windows(ref, m, h, back):
        parts = []
        for d in range(z.blocks):
            first = (z.blocks - 1 - d) if back else d
            start = m * z.stack + first * z.segments * z.ch + h
            parts.append(ref[pl.ds(start, z.conv_rows, stride=z.ch), :])
        return jnp.concatenate(parts, axis=1).astype(bf16)

    for m in range(z.micros):
        @pl.when(pipe == 0)
        def _():
            if m == 0:
                wait_bytes(entry_rx, recv.at[ENTRY])
            for i, tile in enumerate(lane_tiles(lambda k: entry_rx[k, m], z.local)):
                masked_store(xs, pad_rows, m, i, tile)

        @pl.when(pipe > 0)
        def _():
            wait_bytes(rx1.at[pl.ds(m * z.slots, z.slots)], recv.at[A1 + m])
            for i, tile in enumerate(lane_tiles(lambda k: rx1[m * z.slots + k], tok)):
                masked_store(xs, pad_rows, m, i, tile)

        def conv_one(h):
            ys[pl.ds(h, z.conv_rows, stride=z.ch), :] = dot(windows(xs, m, h, True), near[h])

        each_channel(conv_one, ch)
        tiles = []
        for i in range(z.blocks):
            tile = masked_sum(m, i) + skip[...] * whole_tile(xs, pad_rows, m, i)
            conv_out[m * z.blocks + i] = tile
            tiles.append(gelu(tile))
        lane_pieces(tiles, m, tx2)
        to_micro(m, tx2, rx2, A2)

    pl.when(pipe == last)(reversed_kernel)

    @pl.when(pipe == 0)
    def _():
        wait_bytes(tok_rx, recv.at[TOK])
        res[...] = turn_in(tok_rx).astype(bf16)
        weights_out(DNB)
        weights_all(forward_steps, UPA, UPB)
        weights_all((weights_core,), UPA)
        weights_all(forward_steps, DNA)
        weights_all((weights_core,), UPB)

    wait_bytes(rx2, recv.at[A2])
    gated_s[...] = turn_in(rx2).astype(bf16)
    weights_here(GLU)
    gated = gated_s[...]
    value = dot_nt(gated, glu_all[0].reshape(width, width)) + full_row(vec_all, 5)
    sig = jax.nn.sigmoid(
        dot_nt(gated, glu_all[1].reshape(width, width)) + full_row(vec_all, 6)
    )
    val_s[...] = value
    sig_s[...] = sig

    @pl.when(pipe > 0)
    def _():
        wait_bytes(res, recv.at[RES])

    mid = res[...].astype(f32) + value * sig
    hat2, inv2 = norm_stats(mid)
    hat2_s[...] = hat2
    inv2_s[...] = jnp.broadcast_to(inv2, (rows, LANES))
    ffn_s[...] = (hat2 * full_row(vec_all, 2) + full_row(vec_all, 3)).astype(bf16)
    weights_all((weights_here,), UPA, UPB)
    ffn_in = ffn_s[...]
    for c in range(z.peers):
        offset = jnp.concatenate([vec_all[c, 7 + r : 8 + r, :] for r in range(per)], axis=1)
        hidden = dot(ffn_in, up_all[c]) + offset
        hidden_s[c] = hidden
        act_s[c] = gelu(hidden).astype(bf16)

    @pl.when(pipe == 0)
    def _():
        weights_all(forward_steps, DNB)
        weights_core(DNA)
        weights_core(DNB)

    weights_all((weights_here,), DNA, DNB)
    total = mid + full_row(vec_all, 4)
    for c in range(z.peers):
        total = total + dot(act_s[c], down_all[c])
    layer_out = jnp.where(row_ok, total, 0.0).astype(bf16)
    lay_s[...] = layer_out

    @pl.when(pipe < last)
    def _():
        wait_bytes(vec_next, recv.at[VECN])
        hat, inv = norm_stats(lay_s[...].astype(f32))
        hatn_s[...] = hat
        invn_s[...] = jnp.broadcast_to(inv, (rows, LANES))
        turn_out(hat * full_row(vec_next, 0) + full_row(vec_next, 1), tx1n)
        to_section(lambda p: tx1n.at[p], rx1, slot_me, A1 + own_micro, pipe + 1)
        remote(lay_s, res, RES, place(chan, data, pipe + 1)).start()

    def forward_rows():
        to_peers(lambda c: gated_s, ga, GA)
        to_peers(lambda c: ffn_s, fi, FI)
        to_peers(lambda c: act_s.at[c], ac, AC)

    def top_rows(part):
        count = width // 2
        where = pl.ds(part * count, count)
        to_peers(lambda c: gtop.at[:, where], bg.at[:, :, where], BG + part)

    def hidden_rows():
        to_peers(lambda c: gh_s.at[c], gh, GH)
        to_peers(lambda c: gp_s.at[c], gp, GP)

    turn_out(lay_s[...].astype(f32), lay_t)

    @pl.when(pipe < last)
    def _():
        to_peers(lambda c: lay_t.at[c], hid_rx, HID)
        reversed_kernel()
        wait_bytes(hid_rx, recv.at[HID])
        forward_rows()

    @pl.when(pipe == last)
    def _():
        wait_bytes(cot_rx, recv.at[COT])
        gtop[...] = jnp.where(row_ok, turn_in(cot_rx), 0.0).astype(bf16)

    @pl.when(pipe < last)
    def _():
        wait_bytes(mid_rx, recv.at[MID])
        wait_bytes(rx4n, recv.at[A4N])
        grad_in = jnp.where(row_ok, turn_in(rx4n), 0.0)
        hat = hatn_s[...]
        grad_res = mid_rx[...] + norm_back(
            grad_in, hat, invn_s[:, 0:1], full_row(vec_next, 0)
        )
        gtop[...] = grad_res.astype(bf16)
        pair = (
            jnp.sum(grad_in * hat, axis=0, keepdims=True),
            jnp.sum(grad_in, axis=0, keepdims=True),
        )
        for c in range(z.peers):
            for r, row in enumerate(pair):
                vgn_s[c, r : r + 1, :] = row[:, (c // 2) * LANES : (c // 2 + 1) * LANES]

    pl.when(pipe == 0)(lambda: top_rows(0))
    grad_low = gtop[...]
    grad_top = grad_low.astype(f32)
    grad_ffn = None
    for c in range(z.peers):
        grad_active = dot_nt(grad_low, down_all[c])
        grad_hidden = (grad_active * gelu_slope(hidden_s[c])).astype(bf16)
        gh_s[c] = grad_hidden
        part = dot_nt(grad_hidden, up_all[c])
        grad_ffn = part if grad_ffn is None else grad_ffn + part
    hat2 = hat2_s[...]
    grad_mid = grad_top + norm_back(grad_ffn, hat2, inv2_s[:, 0:1], full_row(vec_all, 2))
    mid_s[...] = grad_mid
    sig = sig_s[...]
    grad_value = grad_mid * sig
    grad_gate = grad_value * val_s[...] * (1.0 - sig)
    grad_gated = dot(grad_value.astype(bf16), glu_all[0].reshape(width, width)) + dot(
        grad_gate.astype(bf16), glu_all[1].reshape(width, width)
    )
    turn_out(grad_gated, tx3)
    to_members(lambda p: tx3.at[p], rx3, slot_me, A3 + own_micro)
    for j in range(z.peers // 2):
        gv = grad_value[:, j * LANES : (j + 1) * LANES]
        gg = shifted(grad_gate[:, j * LANES : (j + 1) * LANES], LANES // 2)
        gp_s[2 * j] = jnp.where(first_half, gv, gg).astype(bf16)
        gp_s[2 * j + 1] = jnp.where(first_half, gg, gv).astype(bf16)
    pl.when(pipe > 0)(lambda: remote(mid_s, mid_rx, MID, place(chan, data, pipe - 1)).start())
    pl.when(pipe == 0)(lambda: top_rows(1))

    @pl.when(pipe < last)
    def _():
        turn_out(gtop[...].astype(f32), ign_t)
        to_section_peers(lambda c: ign_t.at[c], ig_rx, IG, pipe + 1)
        to_section(lambda p: vgn_s.at[p // z.groups], vnrx, me, VGN, pipe + 1)

    for m in range(z.micros):
        wait_bytes(rx3.at[pl.ds(m * z.slots, z.slots)], recv.at[A3 + m])
        if m == 0:
            pl.when(pipe == 0)(hidden_rows)
        for i, tile in enumerate(lane_tiles(lambda k: rx3[m * z.slots + k], tok)):
            masked_store(gs, 0, m, i, tile * gelu_slope(conv_out[m * z.blocks + i]))

        def back_one(h):
            ys[pl.ds(h, z.conv_rows, stride=z.ch), :] = dot(windows(gs, m, h, False), far[h])

        each_channel(back_one, ch)
        tiles = [
            masked_sum(m, i) + skip[...] * whole_tile(gs, 0, m, i) for i in range(z.blocks)
        ]
        lane_pieces(tiles, m, tx4)
        pl.when(pipe == 0)(lambda: to_micro(m, tx4, rx4, A4))
        pl.when(pipe > 0)(lambda: to_micro(m, tx4, rx4n, A4N, pipe - 1))


    @pl.when(pipe > 0)
    def _():
        top_rows(0)
        top_rows(1)
        hidden_rows()


    @pl.when(pipe == last)
    def _():
        to_peers(lambda c: lay_t.at[c], hid_rx, HID)
        forward_rows()

    many = z.peers * rows
    grads = (
        (ac, AC, bg, BG, z.hid, width, pdown, kdown, sdown, ldown, ddown),
        (fi, FI, gh, GH, width, z.hid, pup, kup, sup, lup, dup),
        (gp, GP, ga, GA, 2 * z.cw, width, pglu, kglu, sglu, lglu, dglu),
    )

    def product(t):
        left, lp, right, rp, n_left, n_right, local, krx, *_ = grads[t]
        wait_bytes(left, recv.at[lp])
        if rp == BG:
            for part in range(2):
                wait_bytes(bg.at[:, :, pl.ds(0, width // 2)], recv.at[BG + part])
        else:
            wait_bytes(right, recv.at[rp])
        local[...] = dot_tn(left[...].reshape(many, n_left), right[...].reshape(many, n_right))
        half = n_left // 2
        other = pl.ds(pl.multiple_of((1 - core) * half, half), half)
        remote(local.at[other], krx, GRADS + 3 * t, sibling).start()

    def chip_sum(t):
        _, _, _, _, n_left, _, part, krx, lsend, lrx, _ = grads[t]
        half = n_left // 2
        own = pl.ds(pl.multiple_of(core * half, half), half)
        wait_bytes(krx, recv.at[GRADS + 3 * t])
        lsend[...] = (part[own, :] + krx[...]).astype(bf16)
        remote(lsend, lrx, GRADS + 3 * t + 1, across).start()

    def both_chips(t):
        _, _, _, _, n_left, _, _, _, lsend, lrx, final = grads[t]
        half = n_left // 2
        own = pl.ds(pl.multiple_of(core * half, half), half)
        wait_bytes(lrx, recv.at[GRADS + 3 * t + 1])
        final[own, :] = lsend[...].astype(f32) + lrx[...].astype(f32)
        remote(final.at[own], final.at[own], GRADS + 3 * t + 2, sibling).start()

    product(0)

    def lag_one(h):
        x = [
            xs[pl.ds(m * z.stack + pad_rows + h, z.conv_rows, stride=z.ch), :]
            for m in range(z.micros)
        ]
        g = jnp.concatenate([windows(gs, m, h, False) for m in range(z.micros)], axis=0)
        prod = dot_tn(jnp.concatenate(x, axis=0).astype(bf16), g)
        prod = jnp.concatenate([prod, jnp.zeros((LANES, LANES), f32)], axis=1)
        size = LANES // 2
        while size >= 8:
            prod = prod[:size] + shifted(prod[size:], wide - size)
            size //= 2
        for t in range(z.blocks + 1):
            rest_s[t, pl.ds(pl.multiple_of(h * 8, 8), 8), :] = prod[:, t * LANES : (t + 1) * LANES]

    def lag_rest():
        total = None
        for a in range(8):
            tiles = [rest_s[t, pl.ds(a, ch, stride=8), :] for t in range(z.blocks + 1)]
            part = shifted(jnp.concatenate(tiles, axis=1), wide - a)
            total = part if total is None else total + part
        lag_s[...] = total

    each_channel(lag_one, 4, 0, ch // 2)
    chip_sum(0)
    each_channel(lag_one, 4, ch // 2, ch)
    lag_rest()
    product(1)
    product(2)


    @pl.when(pipe == 0)
    def _():
        hat, inv = norm_stats(res[...].astype(f32))
        wait_bytes(rx4, recv.at[A4])
        grad_in = jnp.where(row_ok, turn_in(rx4), 0.0)
        grad_res = mid_s[...] + norm_back(grad_in, hat, inv, full_row(vec_all, 0))
        turn_out(grad_res, ig_t)
        to_peers(lambda c: ig_t.at[c], ig_rx, IG)
        pair = (
            jnp.sum(grad_in * hat, axis=0, keepdims=True),
            jnp.sum(grad_in, axis=0, keepdims=True),
        )
        for c in range(z.peers):
            for r, row in enumerate(pair):
                vg0_s[c, r : r + 1, :] = row[:, (c // 2) * LANES : (c // 2 + 1) * LANES]
        to_members(lambda p: vg0_s.at[p // z.groups], vnrx, me, VGN)

    chip_sum(1)
    chip_sum(2)

    rows_of = [
        jnp.sum(grad_ffn * hat2, axis=0, keepdims=True),
        jnp.sum(grad_ffn, axis=0, keepdims=True),
        jnp.sum(grad_top, axis=0, keepdims=True),
    ]
    for c in range(z.peers):
        j = c // 2
        for r, row in enumerate(rows_of):
            vg_s[c, r : r + 1, :] = row[:, j * LANES : (j + 1) * LANES]
        vg_s[c, 3:4, :] = jnp.sum(gp_s[c].astype(f32), axis=0, keepdims=True)
        up_row = jnp.sum(gh_s[c].astype(f32), axis=0, keepdims=True)
        for r in range(per):
            vg_s[c, 4 + r : 5 + r, :] = up_row[:, r * LANES : (r + 1) * LANES]
    to_members(lambda p: vg_s.at[p // z.groups], vrx, me, VG)
    both = dot_nt(high_low(lag_s[:, 0 : z.length]), table[...])
    grad_spec = both[0:ch] + both[ch : 2 * ch]
    gk = (grad_spec[:, 0:padded], grad_spec[:, padded : 2 * padded])
    y_all, ms, cross, over = moments()
    g_top = times(conj(over), gk)
    g_top = (-cosine * g_top[0], -cosine * g_top[1])
    g_low = times(conj(times(times(cross, over), over)), gk)
    g_three = (cosine * cosine * g_low[0], cosine * cosine * g_low[1])
    g_ms = [gk, times(conj(ms[2]), g_top), times(conj(ms[1]), g_top), g_three]
    g_rise = None
    for v, (g_r, g_i) in enumerate(g_ms):
        gsum_s[v, :, 0:padded] = 2.0 * cosine * g_r
        gsum_s[v, :, padded : 2 * padded] = -2.0 * cosine * g_i
        gsum_s[4 + v, :, 0:padded] = 2.0 * y_all * g_i
        gsum_s[4 + v, :, padded : 2 * padded] = 2.0 * y_all * g_r
        part = 2.0 * (sums_s[12 + v] * g_r + sums_s[8 + v] * g_i)
        g_rise = part if g_rise is None else g_rise + part
    slope_s[...] = g_rise
    gcol_s[...] = jnp.zeros(gcol_s.shape, f32)
    gstep_s[...] = jnp.zeros(gstep_s.shape, f32)

    def split(x):
        high_part = x.astype(bf16)
        return high_part, (x - high_part.astype(f32)).astype(bf16)

    g_high, g_low = split(gsum_s[...].reshape(8 * ch, 2 * padded))
    own = [jnp.where(lax.rem(spot, ch) == h, cols[0], 0.0) for h in range(ch)]
    c_high, c_low = split(jnp.concatenate(own, axis=0))
    guw_s[...] = dot(c_high, g_high) + dot(c_high, g_low) + dot(c_low, g_high)
    uw_high, uw_low = split(uw_s[...])
    g_cols = dot_nt(uw_high, g_high) + dot_nt(uw_high, g_low) + dot_nt(uw_low, g_high)
    total = g_cols[0:nh]
    for h in range(1, ch):
        total = jnp.where(lax.rem(spot, ch) == h, g_cols[h * nh : (h + 1) * nh], total)
    gcol_s[0] = total

    def mode_one(h):
        at = pl.ds(pl.multiple_of(h * nh, nh), nh)
        u, w = uw_s[at, 0:padded], uw_s[at, padded : 2 * padded]
        gu, gw = guw_s[at, 0:padded], guw_s[at, padded : 2 * padded]
        double = column_of(1, h)[:, ch : ch + 1]
        y = rise_s[pl.ds(h, 1), 0:1] * sine
        even, cross_uw = u * u - w * w, 2.0 * u * w
        g_den_r = -(even * gu + cross_uw * gw)
        g_den_i = even * gw - cross_uw * gu
        ge = jnp.sum(cosine * cosine * g_den_r, axis=1, keepdims=True)
        gf = jnp.sum(cosine * y * g_den_i, axis=1, keepdims=True)
        acc = jnp.where(spot == h, ge, gcol_s[1])
        gcol_s[1] = jnp.where(spot == ch + h, gf, acc)
        gy = slope_s[pl.ds(h, 1), :] + jnp.sum(
            double * cosine * g_den_i - 2.0 * y * g_den_r, axis=0, keepdims=True
        )
        total_y = jnp.sum(y * gy, axis=1, keepdims=True)
        gstep_s[0:1, :] = jnp.where(spot == h, -total_y, gstep_s[0:1, :])

    each_channel(mode_one, 4)

    def unpacked(k, i):
        return shifted(gcol_s[k], LANES - i * ch)

    g_square, g_double = unpacked(1, 0), unpacked(1, 1)
    g_decay = 2.0 * decay * g_square + 2.0 * g_double
    g_rate = 2.0 * rate * g_square
    g_pairs = []
    for v, (v_r, v_i) in enumerate(pairs):
        g_alpha, g_beta = unpacked(0, v), unpacked(0, 4 + v)
        g_decay = g_decay + g_alpha * v_r
        if v_i is not None:
            g_rate = g_rate - g_alpha * v_i
        g_pairs.append((decay * g_alpha + g_beta, -rate * g_alpha))
    c_b, c_p, p_b = g_pairs[0], g_pairs[1], g_pairs[2]
    p_p = g_pairs[3][0]
    rank, into, out = (rank_r, rank_i), (in_r, in_i), (out_r, out_i)

    def plus(*terms):
        return sum(t[0] for t in terms), sum(t[1] for t in terms)

    g_out = plus(times(conj(into), c_b), times(conj(rank), c_p))
    g_in = plus(times(conj(out), c_b), times(rank, p_b))
    g_rank = plus(
        times(conj(out), c_p),
        times(into, conj(p_b)),
        (2.0 * rank_r * p_p, 2.0 * rank_i * p_p),
    )
    modes_tx[0:nh, :] = packed([g_decay, g_rate, *g_rank, *g_in, *g_out])
    modes_tx[nh : nh + 8, :] = gstep_s[...]
    skip_row = jnp.sum(jnp.where(diagonal, lag_s[:, 0:1], 0.0), axis=0, keepdims=True)
    modes_tx[nh + 1 : nh + 2, :] = skip_row
    for k in range(1, z.groups):
        remote(modes_tx, modes_rx.at[data], MODES, place(chan, lax.rem(data + k, z.groups))).start()
    pltpu.make_async_copy(modes_tx, modes_rx.at[data], recv.at[MODES]).start()

    for t in range(3):
        both_chips(t)

    def collect(source, target):
        count = tok * z.quarters
        for m in range(z.micros):
            tiles = []
            for i in range(-(-count // LANES)):
                lo, hi = i * LANES, min((i + 1) * LANES, count)
                tile = None
                for q in range(lo // tok, -(-hi // tok)):
                    piece = shifted(source[m * z.quarters + q].astype(f32), q * tok - lo)
                    first = max(0, q * tok - lo)
                    tile = piece if tile is None else jnp.where(spot >= first, piece, tile)
                tiles.append(tile)
            target[m] = jnp.concatenate(tiles, axis=1)[:, 0:count].astype(bf16)

    pl.when(pipe == last)(lambda: wait_bytes(hid_rx, recv.at[HID]))
    collect(hid_rx, hid_out)
    wait_bytes(ig_rx, recv.at[IG])
    collect(ig_rx, ig_out)
    wait_bytes(vrx, recv.at[VG])
    wait_bytes(vnrx, recv.at[VGN])
    summed, summed_one = vrx[0], vnrx[0]
    for p in range(1, z.members):
        summed = summed + vrx[p]
        summed_one = summed_one + vnrx[p]
    upb_out[...] = jnp.concatenate([summed[4 + r : 5 + r, :] for r in range(per)], axis=1)
    summed, summed_one = own_half(summed), own_half(summed_one)
    for r in range(3):
        ffn_out[r] = summed[r : r + 1, 0 : z.cw]
    glub_out[0:1, :] = summed[3:4, 0 : z.cw]
    glub_out[1:2, :] = shifted(summed[3:4], LANES // 2)[:, 0 : z.cw]
    vec_out[0:2, :] = summed_one[0:2, 0 : z.cw]
    wait_bytes(modes_rx, recv.at[MODES])

    def over_groups(take):
        total = take(0)
        for d in range(1, z.groups):
            total = jnp.where(spot // ch == d, take(d), total)
        return total[:, 0 : z.cw]

    for p in range(8):
        modes_out[p] = over_groups(
            lambda d: shifted(modes_rx[d, 0:nh, :], (d - p) * ch)
        )
    for r in range(2):
        vec_out[2 + r : 3 + r, :] = over_groups(
            lambda d: shifted(modes_rx[d, nh + r : nh + r + 1, :], d * ch)
        )
    for t, (_, _, _, _, n_left, _, _, _, _, _, final) in enumerate(grads):
        half = n_left // 2
        other = pl.ds(pl.multiple_of((1 - core) * half, half), half)
        wait_bytes(final.at[other], recv.at[GRADS + 3 * t + 2])
    glu_out[0] = dglu[pl.ds(pl.multiple_of(odd * z.cw, z.cw), z.cw), :]
    glu_out[1] = dglu[pl.ds(pl.multiple_of((1 - odd) * z.cw, z.cw), z.cw), :]

    weights_all((weights_sent,), GLU, UPA, UPB, DNA, DNB)
    for ref, phase in (
        (vec_all, VEC), (hid_rx, HID), (ga, GA), (fi, FI), (ac, AC), (gh, GH), (gp, GP),
    ):
        wait_bytes(ref.at[pl.ds(0, z.peers - 1)], send.at[phase])
    for part in range(2):
        sent = bg.at[pl.ds(0, z.peers - 1), :, pl.ds(0, width // 2)]
        wait_bytes(sent, send.at[BG + part])
    for ref, phase in ((rx2, A2), (rx3, A3 + own_micro), (vrx, VG)):
        wait_bytes(ref.at[pl.ds(0, z.members - 1)], send.at[phase])
    wait_bytes(modes_rx.at[pl.ds(0, z.groups - 1)], send.at[MODES])
    for t, (_, _, _, _, n_left, _, _, krx, lsend, _, final) in enumerate(grads):
        wait_bytes(krx, send.at[GRADS + 3 * t])
        wait_bytes(lsend, send.at[GRADS + 3 * t + 1])
        wait_bytes(final.at[pl.ds(0, n_left // 2)], send.at[GRADS + 3 * t + 2])

    @pl.when(pipe == 0)
    def _():
        wait_bytes(tok_rx.at[pl.ds(0, z.peers - 1)], send.at[TOK])
        wait_bytes(ig_rx.at[pl.ds(0, z.peers - 1)], send.at[IG])
        wait_bytes(stat_rx.at[pl.ds(0, z.peers - 1)], send.at[STAT])
        wait_bytes(entry_rx.at[pl.ds(0, z.groups - 1)], send.at[ENTRY])
        for ref, phase in ((rx4, A4), (vnrx, VGN)):
            wait_bytes(ref.at[pl.ds(0, z.members - 1)], send.at[phase])

    @pl.when(pipe == last)
    def _():
        wait_bytes(cot_rx.at[pl.ds(0, z.peers - 1)], send.at[COT])

    @pl.when(pipe < last)
    def _():
        for ref, phase in ((rx1, A1 + own_micro), (lay_s, RES), (ig_rx, IG), (vnrx, VGN)):
            wait_bytes(ref, send.at[phase])

    @pl.when(pipe > 0)
    def _():
        for ref, phase in ((vec_all, VECN), (mid_s, MID), (rx4, A4N)):
            wait_bytes(ref, send.at[phase])


def finish_kernel(*refs):
    count = (len(refs) - 1) // 3
    sems = refs[-1]
    sources, targets, held = refs[:count], refs[count : 2 * count], refs[2 * count : -1]
    loads = [pltpu.make_async_copy(sources[i], held[i], sems.at[i]) for i in range(count)]
    stores = [
        pltpu.make_async_copy(held[i], targets[i], sems.at[count + i]) for i in range(count)
    ]
    for load in loads:
        load.start()
    for load, store in zip(loads, stores):
        load.wait()
        store.start()
    for store in stores:
        store.wait()


def body(
    tokens,
    seq_lengths,
    out_cot,
    s4_vectors,
    s4_modes,
    glu_weight,
    glu_bias,
    ffn_vectors,
    up_weight,
    up_bias,
    down_weight,
):
    micros, tok_rows, chan_width = tokens.shape
    width = glu_weight.shape[1]
    hidden = up_weight.shape[2]
    z = Sizes(
        lax.axis_size("pipe"), lax.axis_size("chan"), lax.axis_size("dp"),
        tok_rows, chan_width, width, hidden,
    )
    length = z.length
    padded = -(-(length // 2 + 1) // LANES) * LANES
    nh = s4_modes.shape[3]
    table = jnp.asarray(fourier_table(length, padded).astype(ml_dtypes.bfloat16))
    angles = jnp.asarray(half_angles(length, padded))

    vmem = pl.BlockSpec(memory_space=pltpu.VMEM)
    smem = pl.BlockSpec(memory_space=pltpu.SMEM)
    anywhere = pl.BlockSpec(memory_space=pl.ANY)
    n, r, w, ch = z.peers, z.rows, width, z.ch

    def s(shape, kind=f32):
        return jax.ShapeDtypeStruct(shape, kind)

    def v(shape, kind=bf16):
        return pltpu.VMEM(shape, kind)

    wide = (z.blocks + 1) * LANES
    rows_full, rows_wide, side = v((r, w)), v((r, w), f32), v((r, LANES), f32)
    peer_tiles, exchange = v((n, chan_width, LANES)), v((z.members, z.ch, LANES))
    small = v((n, 8, LANES), f32)
    results = (
        s((micros, chan_width, tok_rows), bf16), s((micros, chan_width, tok_rows), bf16),
        s((4, chan_width)), s((8, nh, chan_width)), s((2, chan_width, w)),
        s((2, chan_width)), s((3, 1, chan_width)), s((w, hidden)), s((1, hidden)),
        s((hidden, w)),
    )
    raw = pl.pallas_call(
        lambda *refs: main_kernel(z, *refs),
        out_shape=results,
        in_specs=[smem] + [vmem] * 11 + [anywhere],
        out_specs=[vmem] * 10,
        scratch_shapes=[
            peer_tiles, peer_tiles, v((16, LANES), f32), v((ch, length, LANES)),
            v((ch, length, LANES)), v((ch, LANES), f32), v((40, LANES), f32),
            peer_tiles, peer_tiles, v((micros * z.stack, LANES), f32),
            v((micros * z.stack, LANES), f32),
            v((2 * padded, length)), v((2, nh, LANES), f32),
            v((ch, LANES), f32), v((16, ch, padded), f32), v((ch * nh, 2 * padded), f32),
            v((ch * nh, 2 * padded), f32), v((z.blocks + 1, 8 * ch, LANES), f32),
            v((8, ch, 2 * padded), f32),
            v((ch, padded), f32), v((ch, wide), f32), v((ch, wide), f32),
            v((2, nh, LANES), f32), v((8, LANES), f32),
            v((nh + 8, LANES), f32), v((z.groups, nh + 8, LANES), f32),
            v((2 * chan_width, w), f32), v((w, hidden), f32), v((hidden, w), f32),
            v((chan_width, w), f32), v((w // 2, hidden), f32), v((hidden // 2, w), f32),
            v((chan_width, w)), v((w // 2, hidden)), v((hidden // 2, w)),
            v((chan_width, w)), v((w // 2, hidden)), v((hidden // 2, w)),
            v((2 * chan_width, w), f32),
            v((n, 16, LANES), f32), v((n, 16, LANES), f32),
            v((2, n, chan_width, w)), v((n, w, hidden)),
            v((n, hidden, w)), peer_tiles, peer_tiles, rows_full, rows_full,
        ]
        + [exchange] * 9
        + [
            v((z.micros * z.blocks, z.ch, LANES), f32), v((z.conv_rows * z.ch, LANES), f32),
            rows_wide, side, rows_wide, side,
            rows_wide, rows_wide, v((n, r, hidden), f32),
            rows_full, rows_full, v((n, r, hidden)), v((n, r, hidden)), v((n, r, LANES)),
            rows_full, peer_tiles, peer_tiles, peer_tiles, rows_wide, rows_wide,
            v((8, z.over), f32), v((n, 8, z.over), f32),
            v((z.groups, micros, ch, z.over)), v((z.groups, micros, ch, z.over)),
            small, small, small,
            v((n, r, w)), v((n, r, w)), v((n, r, hidden)), v((n, r, w)), v((n, r, hidden)),
            v((n, r, LANES)), v((z.members, 8, LANES), f32), v((z.members, 8, LANES), f32),
            pltpu.SemaphoreType.DMA((68,)), pltpu.SemaphoreType.DMA((68,)),
        ],
        compiler_params=pltpu.CompilerParams(
            collective_id=0, has_side_effects=True, vmem_limit_bytes=60 * 2**20
        ),
        name="layers",
    )(
        seq_lengths, tokens.transpose(0, 2, 1), out_cot.transpose(0, 2, 1), s4_vectors[0],
        s4_modes[0].transpose(0, 2, 1), glu_weight[0].transpose(1, 2, 0), glu_bias[0],
        ffn_vectors.transpose(1, 0, 2), up_weight[0], up_bias, down_weight[0], angles, table,
    )
    hid, ig, vec, modes, dglu, glub, ffn, dup, upb, ddown = pl.pallas_call(
        finish_kernel,
        out_shape=results,
        in_specs=[anywhere] * 10,
        out_specs=[anywhere] * 10,
        scratch_shapes=[pltpu.VMEM(x.shape, x.dtype) for x in results]
        + [pltpu.SemaphoreType.DMA((20,))],
        compiler_params=pltpu.CompilerParams(vmem_limit_bytes=60 * 2**20),
        name="finish",
    )(*raw)
    return (
        hid.transpose(0, 2, 1)[None], ig.transpose(0, 2, 1)[None], vec[None],
        modes.transpose(0, 2, 1)[None], dglu.transpose(2, 0, 1)[None], glub[None],
        ffn.transpose(1, 0, 2), dup[None], upb, ddown[None],
    )


def solution(mesh):
    placed = (
        P(None, "dp", "chan"),
        P(),
        P(None, "dp", "chan"),
        P("pipe", None, "chan"),
        P("pipe", None, "chan", None),
        P("pipe", None, None, "chan"),
        P("pipe", None, "chan"),
        P("pipe", None, "chan"),
        P("pipe", None, "chan"),
        P("pipe", "chan"),
        P("pipe", "chan", None),
    )
    return jax.shard_map(
        body,
        mesh=mesh,
        in_specs=placed,
        out_specs=(
            P("pipe", None, "dp", "chan"),
            P("pipe", None, "dp", "chan"),
            P("pipe", None, "chan"),
            P("pipe", None, "chan", None),
            P("pipe", None, None, "chan"),
            P("pipe", None, "chan"),
            P("pipe", None, "chan"),
            P("pipe", None, "chan"),
            P("pipe", "chan"),
            P("pipe", "chan", None),
        ),
        check_vma=False,
    )
```

```python
import math

import jax
import jax.numpy as jnp
import ml_dtypes
import numpy as np
from jax import lax
from jax.experimental import pallas as pl
from jax.experimental.pallas import tpu as pltpu
from jax.sharding import PartitionSpec as P

norm_eps = 1e-05
f32 = jnp.float32
bf16 = jnp.bfloat16
LANES = 128


def fourier_table(length, padded):
    half = length // 2
    freq = np.arange(padded, dtype=np.int64)[:, None]
    time = np.arange(length, dtype=np.int64)[None, :]
    angle = (freq * (2 * time + 1) % (2 * length)) * (np.pi / length)
    weight = np.where(freq <= half, np.where((freq == 0) | (freq == half), 1.0, 2.0), 0.0) / length
    table = np.concatenate([np.cos(angle) * weight, -np.sin(angle) * weight], axis=0)
    return table.astype(np.float32)


def half_angles(length, padded):
    angle = np.minimum(np.arange(padded), length // 2) * (np.pi / length)
    rows = np.zeros((8, padded), np.float32)
    rows[0] = np.where(np.arange(padded) < length // 2, np.cos(angle), 0.0)
    rows[1] = np.sin(angle)
    return rows


def shifted(x, by):
    size = x.shape[-1]
    by = by % size
    if by == 0:
        return x
    return pltpu.roll(x, by, x.ndim - 1)


def gelu(x):
    return 0.5 * x * (1.0 + jnp.tanh(math.sqrt(2.0 / math.pi) * (x + 0.044715 * x * x * x)))


def gelu_slope(x):
    scale = math.sqrt(2.0 / math.pi)
    t = jnp.tanh(scale * (x + 0.044715 * x * x * x))
    return 0.5 * (1.0 + t) + 0.5 * x * (1.0 - t * t) * scale * (1.0 + 3.0 * 0.044715 * x * x)


def dot(a, b):
    return lax.dot_general(a, b, (((1,), (0,)), ((), ())), preferred_element_type=f32)


def dot_nt(a, b):
    return lax.dot_general(a, b, (((1,), (1,)), ((), ())), preferred_element_type=f32)


def dot_tn(a, b):
    return lax.dot_general(a, b, (((0,), (0,)), ((), ())), preferred_element_type=f32)


class Sizes:
    def __init__(self, sections, peers, groups, tok_rows, chan_width, model_width, hidden):
        self.sections, self.peers, self.groups = sections, peers, groups
        self.micros = 2
        self.segments = 2
        self.quarters = peers // self.micros
        self.tok = tok_rows // self.quarters
        self.rows = -(-self.tok // 16) * 16
        self.length = tok_rows * groups
        self.blocks = self.length // LANES
        self.local = tok_rows
        self.over = -(-tok_rows // LANES) * LANES
        self.width = model_width
        self.cw = chan_width
        self.hid = hidden
        self.members = peers * groups
        self.ch = model_width // self.members
        self.slots = self.quarters * groups
        self.conv_rows = -(-(self.blocks * self.segments) // 8) * 8
        spare = -(-(self.conv_rows - self.blocks * self.segments) // self.segments)
        self.stack = (2 * self.blocks - 1 + spare) * self.segments * self.ch


def main_kernel(z, *refs):
    (
        lengths, tokens, out_cot, vectors, modes, glu_loc, glu_bias, ffn_vec, up_loc, up_bias,
        down_loc, angles, table_in,
    ) = refs[:13]
    (
        hid_out, ig_out, vec_out, modes_out, glu_out, glub_out, ffn_out, dup, upb_out, ddown,
    ) = refs[13:23]
    (
        tok_tx, cot_tx, vec_tx, near, far, skip, masks, hid_rx, ig_rx, xs, gs,
        table, cols, rise_s, sums_s, uw_s, guw_s, rest_s, gsum_s, slope_s, kern_s, lag_s, gcol_s, gstep_s,
        modes_tx, modes_rx, pglu, pup, pdown, kglu, kup, kdown, sglu, sup, sdown,
        lglu, lup, ldown, dglu,
        vec_all, vec_next, glu_all, up_all, down_all, tok_rx, cot_rx, res, gtop,
        tx1n, rx1, tx2, rx2, tx3, rx3, tx4, rx4, rx4n,
        conv_out, ys, hatn_s, invn_s, hat2_s, inv2_s, val_s, sig_s, hidden_s,
        gated_s, ffn_s, act_s, gh_s, gp_s, lay_s, lay_t, ig_t, ign_t, mid_s, mid_rx,
        stat_tx, stat_rx, entry_tx, entry_rx, vg_s, vgn_s, vg0_s, ga, fi, ac, bg, gh, gp, vrx, vnrx, send, recv,
    ) = refs[23:]
    pipe = lax.axis_index("pipe")
    chan = lax.axis_index("chan")
    data = lax.axis_index("dp")
    last = z.sections - 1
    me = chan * z.groups + data
    slot_me = (chan // z.quarters) * z.slots + data * z.quarters + lax.rem(chan, z.quarters)
    rows, width, tok = z.rows, z.width, z.tok
    spot = lax.broadcasted_iota(jnp.int32, (1, LANES), 1)
    first_half = spot < (LANES // 2)
    row_ok = lax.broadcasted_iota(jnp.int32, (rows, 1), 0) < tok
    odd = lax.rem(chan, 2)
    per = z.hid // LANES

    high, deep = chan // z.quarters, lax.rem(chan, z.quarters)
    side, core = data // 2, lax.rem(data, 2)
    height = 2 * high + side

    def slot_of(p):
        c, d = p // z.groups, lax.rem(p, z.groups)
        return (c // z.quarters) * z.slots + d * z.quarters + lax.rem(c, z.quarters)

    def place(c, d, section=None):
        return {"pipe": pipe if section is None else section, "chan": c, "dp": d}

    def member(p, section=None):
        return place(p // z.groups, lax.rem(p, z.groups), section)

    def remote(src, dst, phase, where):
        return pltpu.make_async_remote_copy(
            src_ref=src,
            dst_ref=dst,
            send_sem=send.at[phase],
            recv_sem=recv.at[phase],
            device_id=where,
            device_id_type=pl.DeviceIdType.MESH,
        )

    def wait_bytes(ref, sem):
        pltpu.make_async_copy(ref, ref, sem).wait()

    def to_peers(src_of, dst, phase):
        def step(k, carry):
            c = lax.rem(chan + k, z.peers)
            remote(src_of(c), dst.at[chan], phase, place(c, data)).start()
            return carry

        lax.fori_loop(1, z.peers, step, 0)
        pltpu.make_async_copy(src_of(chan), dst.at[chan], recv.at[phase]).start()

    def far_first(i):
        return lax.rem(2 + i + (i // 2) * (2 * i - 3), 4)

    def number(y, depth, core_there):
        return ((y // 2) * z.quarters + depth) * z.groups + lax.rem(y, 2) * 2 + core_there

    def to_all(src_of, dst, slot, phase, section=None):
        def chip(k):
            y = lax.rem(height + far_first(k // 4), 4)
            return y, lax.rem(deep + far_first(lax.rem(k, 4)), 4)

        def step(k, carry):
            y, depth = chip(k)
            for c in range(2):
                p = number(y, depth, c)
                remote(src_of(p), dst.at[slot], phase, member(p, section)).start()
            return carry

        chips = z.members // 2
        lax.fori_loop(0, chips if section is not None else chips - 1, step, 0)
        if section is None:
            p = number(height, deep, 1 - core)
            remote(src_of(p), dst.at[slot], phase, member(p)).start()
            pltpu.make_async_copy(src_of(me), dst.at[slot], recv.at[phase]).start()

    def to_members(src_of, dst, slot, phase):
        to_all(src_of, dst, slot, phase)

    def to_section(src_of, dst, slot, phase, section):
        to_all(src_of, dst, slot, phase, section)

    def to_micro(m, source, dst, phase, section=None):
        near_by = jnp.where(own_micro == m, 1, 0)

        def send_to(p):
            remote(source.at[slot_of(p)], dst.at[me], phase, member(p, section)).start()

        def chip(k):
            y = 2 * m + lax.rem(side + near_by + k // 4, 2)
            return y, lax.rem(deep + far_first(lax.rem(k, 4)), 4)

        def step(k, carry):
            y, depth = chip(k)
            for c in range(2):
                send_to(number(y, depth, c))
            return carry

        lax.fori_loop(0, z.slots // 2 - 1, step, 0)
        if section is not None:
            step(z.slots // 2 - 1, 0)
            return

        @pl.when(own_micro == m)
        def _():
            send_to(number(height, deep, 1 - core))
            block = source.at[slot_of(me)]
            pltpu.make_async_copy(block, dst.at[me], recv.at[phase]).start()

        @pl.when(own_micro != m)
        def _():
            step(z.slots // 2 - 1, 0)

    def to_section_peers(src_of, dst, phase, section):
        def step(k, carry):
            c = lax.rem(chan + k, z.peers)
            remote(src_of(c), dst.at[chan], phase, place(c, data, section)).start()
            return carry

        lax.fori_loop(0, z.peers, step, 0)

    (
        VEC, VECN, TOK, COT, A2, A4, A4N, RES, MID, HID, IG, GA, FI, AC, GH, GP, VG,
        VGN, TABLE, MODES,
    ) = range(20)
    STAT, ENTRY = 66, 67
    A1, A3, GLU, UPA, UPB, DNA, DNB, GRADS, BG = 21, 23, 25, 31, 37, 43, 49, 55, 64
    direct = (DNB,)
    own_micro = chan // z.quarters

    own_side, far_side = high * z.quarters, (1 - high) * z.quarters
    sibling, across = place(chan, side * 2 + 1 - core), place(chan, (1 - side) * 2 + core)

    def columns(t):
        if t == GLU:
            return glu_loc, glu_all
        loc, whole = (up_loc, up_all) if t in (UPA, UPB) else (down_loc, down_all)
        count = loc.shape[1] // 2
        where = pl.ds(count if t in (UPB, DNB) else 0, count)
        return loc.at[:, where], whole.at[:, :, where]

    def own_rows(t, part=None):
        loc, _ = columns(t)
        if t == GLU:
            fourth = z.cw // 2
            half = loc.at[core]
            return half if part is None else half.at[pl.ds(pl.multiple_of(part * fourth, fourth), fourth)]
        half = loc.shape[0] // 2
        if part is None:
            return loc.at[pl.ds(pl.multiple_of(core * half, half), half)]
        fourth = half // 2
        return loc.at[pl.ds(pl.multiple_of(core * half + part * fourth, fourth), fourth)]

    def piece_of(t, c, count, part=None):
        loc, whole = columns(t)
        if t == GLU:
            fourth = z.cw // 2
            if part is None:
                return whole.at[core, pl.ds(c, count)]
            start = pl.multiple_of(part * fourth, fourth)
            return whole.at[core, pl.ds(c, count), pl.ds(start, fourth)]
        half = loc.shape[0] // 2
        fourth = half // 2
        if part is None:
            return whole.at[pl.ds(c, count), pl.ds(pl.multiple_of(core * half, half), half)]
        start = pl.multiple_of(core * half + part * fourth, fourth)
        return whole.at[pl.ds(c, count), pl.ds(start, fourth)]

    def weights_out(t):
        loc, whole = columns(t)
        whole = whole.at[:, chan] if t == GLU else whole.at[chan]
        pltpu.make_async_copy(loc, whole, recv.at[t + 5]).start()
        part = None if t in direct else side
        payload, there = own_rows(t, part), piece_of(t, chan, 1, part).at[0]
        for k in (2, 3, 1, 0):
            c = far_side + lax.rem(deep + k, z.quarters)
            remote(payload, there, t + 1, place(c, (1 - side) * 2 + core)).start()
        payload, there = own_rows(t), piece_of(t, chan, 1).at[0]
        for k in (2, 3, 1):
            c = own_side + lax.rem(deep + k, z.quarters)
            remote(payload, there, t, place(c, data)).start()

    def weights_beside(t):
        if t in direct:
            return
        wait_bytes(piece_of(t, 0, z.quarters, 0), recv.at[t + 1])
        piece = piece_of(t, far_side, z.quarters, 1 - side)
        remote(piece, piece, t + 2, across).start()

    def weights_near(t):
        wait_bytes(piece_of(t, 0, z.quarters - 1), recv.at[t])
        for k in range(1, z.quarters):
            piece = piece_of(t, own_side + lax.rem(deep + k, z.quarters), 1)
            remote(piece, piece, t + 3, sibling).start()

    def weights_core(t):
        if t in direct:
            wait_bytes(piece_of(t, 0, z.quarters), recv.at[t + 1])
        else:
            wait_bytes(piece_of(t, 0, z.quarters, 0), recv.at[t + 2])
        piece = piece_of(t, far_side, z.quarters)
        remote(piece, piece, t + 4, sibling).start()

    def weights_here(t):
        wait_bytes(columns(t)[0], recv.at[t + 5])
        wait_bytes(piece_of(t, 0, z.quarters - 1), recv.at[t + 3])
        wait_bytes(piece_of(t, 0, z.quarters), recv.at[t + 4])

    def weights_sent(t):
        far_part = None if t in direct else 0
        stages = [(0, z.quarters - 1, None), (1, z.quarters, far_part)]
        if t not in direct:
            stages.append((2, z.quarters, 0))
        stages += [(3, z.quarters - 1, None), (4, z.quarters, None)]
        for stage, count, part in stages:
            wait_bytes(piece_of(t, 0, count, part), send.at[t + stage])

    def weights_all(steps, *which):
        for t in which:
            for step in steps:
                step(t)

    forward_steps = (weights_beside, weights_near)

    barrier = pltpu.get_barrier_semaphore()

    def greet(where):
        pl.semaphore_signal(barrier, inc=1, device_id=where, device_id_type=pl.DeviceIdType.MESH)

    def greet_own(k, carry):
        greet(member(lax.rem(me + k, z.members)))
        return carry

    pl.when(pipe < last)(lambda: greet(place(chan, data, pipe + 1)))
    pl.when(pipe > 0)(lambda: greet(place(chan, data, pipe - 1)))
    lax.fori_loop(1, z.members, greet_own, 0)
    pltpu.make_async_copy(table_in, table, recv.at[TABLE]).start()

    def own_half(x):
        return pltpu.roll(x, odd * (LANES // 2), x.ndim - 1)

    stat_tx[...] = jnp.zeros(stat_tx.shape, f32)

    def fill_blocks(source, target):
        count = z.tok * z.quarters
        over = -(-count // LANES) * LANES
        for m in range(z.micros):
            x = source[m].astype(f32)
            x = jnp.concatenate([x, jnp.zeros((z.cw, over - count), f32)], axis=1)
            for q in range(z.quarters):
                target[m * z.quarters + q] = shifted(x, over - q * tok)[:, 0:LANES].astype(bf16)

    vec_rows = [vectors[0:1, :], vectors[1:2, :]] + [ffn_vec[r] for r in range(3)]
    vec_rows += [glu_bias[0:1, :], glu_bias[1:2, :]]
    for r, row in enumerate(vec_rows):
        vec_tx[r : r + 1, :] = jnp.concatenate([row, row], axis=1)
    for r in range(per):
        vec_tx[7 + r : 8 + r, :] = up_bias[:, r * LANES : (r + 1) * LANES].astype(f32)
    pl.when(pipe == 0)(lambda: fill_blocks(tokens, tok_tx))
    pl.when(pipe == last)(lambda: fill_blocks(out_cot, cot_tx))

    ch, nh = z.ch, modes.shape[1]

    def own_lanes(x):
        x = jnp.concatenate([x, jnp.zeros((x.shape[0], LANES - z.cw), f32)], axis=1)
        return pltpu.roll(x, lax.rem(LANES - data * ch, LANES), 1)

    def packed(items):
        total = items[0]
        for i, item in enumerate(items[1:], 1):
            total = jnp.where(spot // ch == i, shifted(item, i * ch), total)
        return total

    decay, rate, rank_r, rank_i, in_r, in_i, out_r, out_i = (own_lanes(modes[p]) for p in range(8))
    pairs = [
        (out_r * in_r - out_i * in_i, out_r * in_i + out_i * in_r),
        (out_r * rank_r - out_i * rank_i, out_r * rank_i + out_i * rank_r),
        (rank_r * in_r + rank_i * in_i, rank_r * in_i - rank_i * in_r),
        (rank_r * rank_r + rank_i * rank_i, None),
    ]
    alphas = [
        decay * v_r if v_i is None else decay * v_r - rate * v_i for v_r, v_i in pairs
    ]
    cols[0] = packed(alphas + [v_r for v_r, v_i in pairs])
    cols[1] = packed([decay * decay + rate * rate, 2.0 * decay])
    own_vectors = own_lanes(vectors[...])
    diagonal = lax.broadcasted_iota(jnp.int32, (ch, LANES), 0) == lax.broadcasted_iota(
        jnp.int32, (ch, LANES), 1
    )

    def upright(row):
        column = jnp.sum(jnp.where(diagonal, row, 0.0), axis=1, keepdims=True)
        return jnp.broadcast_to(column, (ch, LANES))

    rise_s[...] = 2.0 * jnp.exp(-upright(own_vectors[2:3]))
    skip[...] = upright(own_vectors[3:4])
    cosine, sine = angles[0:1, :], angles[1:2, :]
    padded = angles.shape[1]

    def column_of(k, h):
        return pltpu.roll(cols[k], lax.rem(LANES - h, LANES), 1)

    def modes_at(h):
        two = column_of(1, h)
        square, double = two[:, 0:1], two[:, ch : ch + 1]
        y = rise_s[pl.ds(h, 1), 0:1] * sine
        cy = cosine * y
        den_r = square * (cosine * cosine) - y * y
        den_i = double * cy
        inverse = 1.0 / (den_r * den_r + den_i * den_i)
        return double, y, cy, den_r * inverse, den_i * inverse

    def cauchy_one(h):
        _, _, _, u, w = modes_at(h)
        at = pl.ds(pl.multiple_of(h * nh, nh), nh)
        uw_s[at, 0:padded] = u
        uw_s[at, padded : 2 * padded] = w
        column = column_of(0, h)
        for v in range(4):
            a = column[:, v * ch : v * ch + 1]
            b = column[:, (4 + v) * ch : (4 + v) * ch + 1]
            sums_s[v, pl.ds(h, 1), :] = jnp.sum(a * u, axis=0, keepdims=True)
            sums_s[4 + v, pl.ds(h, 1), :] = jnp.sum(a * w, axis=0, keepdims=True)
            sums_s[8 + v, pl.ds(h, 1), :] = jnp.sum(b * u, axis=0, keepdims=True)
            sums_s[12 + v, pl.ds(h, 1), :] = jnp.sum(b * w, axis=0, keepdims=True)

    def each_channel(one, unroll, first=0, end=None):
        def step(i, carry):
            for u in range(unroll):
                one(i * unroll + u)
            return carry

        if unroll == ch:
            step(0, 0)
        else:
            lax.fori_loop(first // unroll, (ch if end is None else end) // unroll, step, 0)

    def times(a, b):
        return a[0] * b[0] - a[1] * b[1], a[0] * b[1] + a[1] * b[0]

    def conj(a):
        return a[0], -a[1]

    def moments():
        y_all = rise_s[:, 0:1] * sine
        ms = [
            (
                2.0 * (cosine * sums_s[v] + y_all * sums_s[12 + v]),
                2.0 * (y_all * sums_s[8 + v] - cosine * sums_s[4 + v]),
            )
            for v in range(4)
        ]
        low_r, low_i = 1.0 + cosine * ms[3][0], cosine * ms[3][1]
        size = 1.0 / (low_r * low_r + low_i * low_i)
        return y_all, ms, times(ms[1], ms[2]), (low_r * size, -low_i * size)

    def high_low(x):
        high_part = x.astype(bf16)
        low_part = (x - high_part.astype(f32)).astype(bf16)
        return jnp.concatenate([high_part, low_part], axis=0)

    each_channel(cauchy_one, 4)
    pad_rows = (z.blocks - 1) * z.segments * z.ch
    data_rows = z.blocks * z.segments * z.ch
    for m in range(z.micros):
        at = m * z.stack
        xs[at : at + pad_rows, :] = jnp.zeros((pad_rows, LANES), f32)
        rest = z.stack - pad_rows - data_rows
        xs[at + z.stack - rest : at + z.stack, :] = jnp.zeros((rest, LANES), f32)
        rest = z.stack - data_rows
        gs[at + data_rows : at + z.stack, :] = jnp.zeros((rest, LANES), f32)
    for m in range(z.micros):
        first_len, second_len = lengths[m, 0], lengths[m, 1]
        for i in range(z.blocks):
            at = (m * z.blocks + i) * z.segments
            where = spot + i * LANES
            masks[at : at + 1, :] = jnp.where(where < first_len, 1.0, 0.0)
            inside = jnp.where(where < first_len + second_len, 1.0, 0.0)
            masks[at + 1 : at + 2, :] = jnp.where(where >= first_len, inside, 0.0)

    pl.semaphore_wait(
        barrier,
        z.members - 1 + jnp.minimum(pipe, 1) + jnp.minimum(last - pipe, 1),
    )

    @pl.when(pipe == 0)
    def _():
        for m in range(z.micros):
            x = tokens[m].astype(f32)
            stat_tx[2 * m : 2 * m + 1, 0 : z.local] = jnp.sum(x, axis=0, keepdims=True)
            stat_tx[2 * m + 1 : 2 * m + 2, 0 : z.local] = jnp.sum(x * x, axis=0, keepdims=True)
        to_peers(lambda c: stat_tx, stat_rx, STAT)
        to_peers(lambda c: tok_tx.at[c], tok_rx, TOK)

    to_peers(lambda c: vec_tx, vec_all, VEC)
    weights_out(GLU)
    pl.when(pipe == 0)(lambda: weights_all((weights_out,), UPA, UPB))

    @pl.when(pipe == last)
    def _():
        to_peers(lambda c: cot_tx.at[c], cot_rx, COT)


    y_all, ms, cross, over = moments()
    fix = times(cross, over)
    spec = jnp.concatenate([ms[0][0] - cosine * fix[0], ms[0][1] - cosine * fix[1]], axis=1)
    wait_bytes(table, recv.at[TABLE])
    both = dot(high_low(spec), table[...])
    wide = (z.blocks + 1) * LANES
    kern_s[:, 0 : z.length] = both[0:ch] + both[ch : 2 * ch]
    kern_s[:, z.length : wide] = jnp.zeros((ch, wide - z.length), f32)

    def norm_stats(v):
        mean = jnp.sum(v, axis=1, keepdims=True) * (1.0 / width)
        spread = jnp.sum(v * v, axis=1, keepdims=True) * (1.0 / width) - mean * mean
        inv = lax.rsqrt(spread + norm_eps)
        return (v - mean) * inv, inv

    def norm_back(e, hat, inv, gain):
        dh = e * gain
        first = jnp.sum(dh, axis=1, keepdims=True) * (1.0 / width)
        second = jnp.sum(dh * hat, axis=1, keepdims=True) * (1.0 / width)
        return inv * (dh - first - hat * second)

    def turn_out(v, ref):
        tall = jnp.concatenate([v, jnp.zeros((LANES - rows, width), f32)], axis=0)
        ref[...] = tall.T.astype(bf16).reshape(ref.shape)

    def turn_in(ref):
        return ref[...].reshape(width, LANES).astype(f32).T[:rows]

    def full_row(source, r):
        tiles = [
            jnp.where(first_half, source[2 * j, r : r + 1, :], source[2 * j + 1, r : r + 1, :])
            for j in range(z.peers // 2)
        ]
        return jnp.concatenate(tiles, axis=1)

    @pl.when(pipe == 0)
    def _():
        tall = lax.broadcasted_iota(jnp.int32, (z.cw, LANES), 0) == spot

        def upright_all(r):
            row = jnp.concatenate([vectors[r : r + 1, :], jnp.zeros((1, LANES - z.cw), f32)], axis=1)
            return jnp.sum(jnp.where(tall, row, 0.0), axis=1, keepdims=True)

        gain, bias = upright_all(0), upright_all(1)
        wait_bytes(stat_rx, recv.at[STAT])
        total = stat_rx[0]
        for c in range(1, z.peers):
            total = total + stat_rx[c]
        total = total * (1.0 / width)
        for m in range(z.micros):
            mean = total[2 * m : 2 * m + 1, 0 : z.local]
            spread = total[2 * m + 1 : 2 * m + 2, 0 : z.local] - mean * mean
            hat = (tokens[m].astype(f32) - mean) * lax.rsqrt(spread + norm_eps)
            normed = (hat * gain + bias).astype(bf16)
            for d in range(z.groups):
                entry_tx[d, m, :, 0 : z.local] = normed[d * ch : (d + 1) * ch, :]
        for k in range(1, z.groups):
            d = lax.rem(data + k, z.groups)
            remote(entry_tx.at[d], entry_rx.at[data], ENTRY, place(chan, d)).start()
        pltpu.make_async_copy(entry_tx.at[data], entry_rx.at[data], recv.at[ENTRY]).start()

    pl.when(pipe == 0)(lambda: weights_out(DNA))
    wait_bytes(vec_all, recv.at[VEC])

    @pl.when(pipe > 0)
    def _():
        remote(vec_all, vec_next, VECN, place(chan, data, pipe - 1)).start()


    @pl.when(pipe > 0)
    def _():
        weights_all((weights_out,), UPA, UPB, DNA, DNB)

    def toeplitz_one(h):
        full = jnp.broadcast_to(kern_s[pl.ds(h, 1), :], (LANES, wide))
        full = pltpu.roll(full, 0, 1, stride=1, stride_axis=0).astype(bf16)
        for d in range(z.blocks):
            near[h, d * LANES : (d + 1) * LANES, :] = full[:, d * LANES : (d + 1) * LANES]

    each_channel(toeplitz_one, 2)

    def reversed_one(h):
        full = jnp.broadcast_to(lag_s[pl.ds(h, 1), :], (LANES, wide))
        full = pltpu.roll(full, 0, 1, stride=1, stride_axis=0).astype(bf16)
        for d in range(z.blocks):
            at = (z.blocks - 1 - d) * LANES
            far[h, d * LANES : (d + 1) * LANES, :] = full[:, at : at + LANES]

    def reversed_kernel():
        down = lax.broadcasted_iota(jnp.int32, (LANES, LANES), 0)
        along = lax.broadcasted_iota(jnp.int32, (LANES, LANES), 1)
        flip = jnp.where(down + along == LANES - 1, 1.0, 0.0).astype(bf16)
        tiles = [
            dot(kern_s[:, t * LANES : (t + 1) * LANES].astype(bf16), flip)
            for t in reversed(range(z.blocks + 1))
        ]
        lag_s[...] = shifted(jnp.concatenate(tiles, axis=1), wide - (2 * LANES - 1))
        each_channel(reversed_one, 2)

    weights_all(forward_steps, GLU)

    @pl.when(pipe > 0)
    def _():
        weights_all(forward_steps, UPA, UPB, DNA, DNB)
        weights_all((weights_core,), UPA, UPB, DNA, DNB)

    weights_core(GLU)

    def lane_tiles(pieces, size):
        tiles = []
        for i in range(z.blocks):
            lo, hi = i * LANES, (i + 1) * LANES
            tile = None
            for k in range(lo // size, -(-hi // size)):
                piece = shifted(pieces(k).astype(f32), k * size - lo)[:, 0:LANES]
                first = max(0, k * size - lo)
                if tile is None:
                    tile = piece
                else:
                    tile = jnp.where(spot >= first, piece, tile)
            tiles.append(tile)
        return tiles

    def lane_pieces(tiles, m, ref):
        for k in range(z.slots):
            i, off = divmod(k * tok, LANES)
            piece = shifted(tiles[i], LANES - off)
            if off + tok > LANES:
                piece = jnp.where(spot < LANES - off, piece, shifted(tiles[i + 1], LANES - off))
            ref[m * z.slots + k] = piece.astype(bf16)

    def row_at(m, i, q):
        return m * z.stack + (i * z.segments + q) * z.ch

    def mask_of(m, i, q):
        at = (m * z.blocks + i) * z.segments + q
        return masks[at : at + 1, :]

    def masked_store(ref, base, m, i, tile):
        for q in range(z.segments):
            at = base + row_at(m, i, q)
            ref[at : at + z.ch, :] = tile * mask_of(m, i, q)

    def masked_sum(m, i):
        total = None
        for q in range(z.segments):
            at = row_at(0, i, q)
            part = ys[at : at + z.ch, :] * mask_of(m, i, q)
            total = part if total is None else total + part
        return total

    def whole_tile(ref, base, m, i):
        total = None
        for q in range(z.segments):
            at = base + row_at(m, i, q)
            total = ref[at : at + z.ch, :] if total is None else total + ref[at : at + z.ch, :]
        return total

    def windows(ref, m, h, back):
        parts = []
        for d in range(z.blocks):
            first = (z.blocks - 1 - d) if back else d
            start = m * z.stack + first * z.segments * z.ch + h
            parts.append(ref[pl.ds(start, z.conv_rows, stride=z.ch), :])
        return jnp.concatenate(parts, axis=1).astype(bf16)

    for m in range(z.micros):
        @pl.when(pipe == 0)
        def _():
            if m == 0:
                wait_bytes(entry_rx, recv.at[ENTRY])
            for i, tile in enumerate(lane_tiles(lambda k: entry_rx[k, m], z.local)):
                masked_store(xs, pad_rows, m, i, tile)

        @pl.when(pipe > 0)
        def _():
            wait_bytes(rx1.at[pl.ds(m * z.slots, z.slots)], recv.at[A1 + m])
            for i, tile in enumerate(lane_tiles(lambda k: rx1[m * z.slots + k], tok)):
                masked_store(xs, pad_rows, m, i, tile)

        def conv_one(h):
            ys[pl.ds(h, z.conv_rows, stride=z.ch), :] = dot(windows(xs, m, h, True), near[h])

        each_channel(conv_one, ch)
        tiles = []
        for i in range(z.blocks):
            tile = masked_sum(m, i) + skip[...] * whole_tile(xs, pad_rows, m, i)
            conv_out[m * z.blocks + i] = tile
            tiles.append(gelu(tile))
        lane_pieces(tiles, m, tx2)
        to_micro(m, tx2, rx2, A2)

    pl.when(pipe == last)(reversed_kernel)

    @pl.when(pipe == 0)
    def _():
        wait_bytes(tok_rx, recv.at[TOK])
        res[...] = turn_in(tok_rx).astype(bf16)
        weights_out(DNB)
        weights_all(forward_steps, UPA, UPB)
        weights_all((weights_core,), UPA)
        weights_all(forward_steps, DNA)
        weights_all((weights_core,), UPB)

    wait_bytes(rx2, recv.at[A2])
    gated_s[...] = turn_in(rx2).astype(bf16)
    weights_here(GLU)
    gated = gated_s[...]
    value = dot_nt(gated, glu_all[0].reshape(width, width)) + full_row(vec_all, 5)
    sig = jax.nn.sigmoid(
        dot_nt(gated, glu_all[1].reshape(width, width)) + full_row(vec_all, 6)
    )
    val_s[...] = value
    sig_s[...] = sig

    @pl.when(pipe > 0)
    def _():
        wait_bytes(res, recv.at[RES])

    mid = res[...].astype(f32) + value * sig
    hat2, inv2 = norm_stats(mid)
    hat2_s[...] = hat2
    inv2_s[...] = jnp.broadcast_to(inv2, (rows, LANES))
    ffn_s[...] = (hat2 * full_row(vec_all, 2) + full_row(vec_all, 3)).astype(bf16)
    weights_all((weights_here,), UPA, UPB)
    ffn_in = ffn_s[...]
    for c in range(z.peers):
        offset = jnp.concatenate([vec_all[c, 7 + r : 8 + r, :] for r in range(per)], axis=1)
        hidden = dot(ffn_in, up_all[c]) + offset
        hidden_s[c] = hidden
        act_s[c] = gelu(hidden).astype(bf16)

    @pl.when(pipe == 0)
    def _():
        weights_all(forward_steps, DNB)
        weights_core(DNA)
        weights_core(DNB)

    weights_all((weights_here,), DNA, DNB)
    total = mid + full_row(vec_all, 4)
    for c in range(z.peers):
        total = total + dot(act_s[c], down_all[c])
    layer_out = jnp.where(row_ok, total, 0.0).astype(bf16)
    lay_s[...] = layer_out

    @pl.when(pipe < last)
    def _():
        wait_bytes(vec_next, recv.at[VECN])
        hat, inv = norm_stats(lay_s[...].astype(f32))
        hatn_s[...] = hat
        invn_s[...] = jnp.broadcast_to(inv, (rows, LANES))
        turn_out(hat * full_row(vec_next, 0) + full_row(vec_next, 1), tx1n)
        to_section(lambda p: tx1n.at[p], rx1, slot_me, A1 + own_micro, pipe + 1)
        remote(lay_s, res, RES, place(chan, data, pipe + 1)).start()

    def collect(source, target):
        count = tok * z.quarters
        for m in range(z.micros):
            tiles = []
            for i in range(-(-count // LANES)):
                lo, hi = i * LANES, min((i + 1) * LANES, count)
                tile = None
                for q in range(lo // tok, -(-hi // tok)):
                    piece = shifted(source[m * z.quarters + q].astype(f32), q * tok - lo)
                    first = max(0, q * tok - lo)
                    tile = piece if tile is None else jnp.where(spot >= first, piece, tile)
                tiles.append(tile)
            target[m] = jnp.concatenate(tiles, axis=1)[:, 0:count].astype(bf16)

    def forward_rows():
        to_peers(lambda c: gated_s, ga, GA)
        to_peers(lambda c: ffn_s, fi, FI)
        to_peers(lambda c: act_s.at[c], ac, AC)

    def top_rows(part):
        count = width // 2
        where = pl.ds(part * count, count)
        to_peers(lambda c: gtop.at[:, where], bg.at[:, :, where], BG + part)

    def hidden_rows():
        to_peers(lambda c: gh_s.at[c], gh, GH)
        to_peers(lambda c: gp_s.at[c], gp, GP)

    turn_out(lay_s[...].astype(f32), lay_t)

    @pl.when(pipe < last)
    def _():
        to_peers(lambda c: lay_t.at[c], hid_rx, HID)
        reversed_kernel()
        wait_bytes(hid_rx, recv.at[HID])
        forward_rows()
        collect(hid_rx, hid_out)

    @pl.when(pipe == last)
    def _():
        wait_bytes(cot_rx, recv.at[COT])
        gtop[...] = jnp.where(row_ok, turn_in(cot_rx), 0.0).astype(bf16)

    @pl.when(pipe < last)
    def _():
        wait_bytes(mid_rx, recv.at[MID])
        wait_bytes(rx4n, recv.at[A4N])
        grad_in = jnp.where(row_ok, turn_in(rx4n), 0.0)
        hat = hatn_s[...]
        grad_res = mid_rx[...] + norm_back(
            grad_in, hat, invn_s[:, 0:1], full_row(vec_next, 0)
        )
        gtop[...] = grad_res.astype(bf16)
        pair = (
            jnp.sum(grad_in * hat, axis=0, keepdims=True),
            jnp.sum(grad_in, axis=0, keepdims=True),
        )
        for c in range(z.peers):
            for r, row in enumerate(pair):
                vgn_s[c, r : r + 1, :] = row[:, (c // 2) * LANES : (c // 2 + 1) * LANES]

    pl.when(pipe == 0)(lambda: top_rows(0))
    grad_low = gtop[...]
    grad_top = grad_low.astype(f32)
    grad_ffn = None
    for c in range(z.peers):
        grad_active = dot_nt(grad_low, down_all[c])
        grad_hidden = (grad_active * gelu_slope(hidden_s[c])).astype(bf16)
        gh_s[c] = grad_hidden
        part = dot_nt(grad_hidden, up_all[c])
        grad_ffn = part if grad_ffn is None else grad_ffn + part
    hat2 = hat2_s[...]
    grad_mid = grad_top + norm_back(grad_ffn, hat2, inv2_s[:, 0:1], full_row(vec_all, 2))
    mid_s[...] = grad_mid
    sig = sig_s[...]
    grad_value = grad_mid * sig
    grad_gate = grad_value * val_s[...] * (1.0 - sig)
    grad_gated = dot(grad_value.astype(bf16), glu_all[0].reshape(width, width)) + dot(
        grad_gate.astype(bf16), glu_all[1].reshape(width, width)
    )
    turn_out(grad_gated, tx3)
    to_members(lambda p: tx3.at[p], rx3, slot_me, A3 + own_micro)
    for j in range(z.peers // 2):
        gv = grad_value[:, j * LANES : (j + 1) * LANES]
        gg = shifted(grad_gate[:, j * LANES : (j + 1) * LANES], LANES // 2)
        gp_s[2 * j] = jnp.where(first_half, gv, gg).astype(bf16)
        gp_s[2 * j + 1] = jnp.where(first_half, gg, gv).astype(bf16)
    pl.when(pipe > 0)(lambda: remote(mid_s, mid_rx, MID, place(chan, data, pipe - 1)).start())
    pl.when(pipe == 0)(lambda: top_rows(1))

    @pl.when(pipe < last)
    def _():
        turn_out(gtop[...].astype(f32), ign_t)
        to_section_peers(lambda c: ign_t.at[c], ig_rx, IG, pipe + 1)
        to_section(lambda p: vgn_s.at[p // z.groups], vnrx, me, VGN, pipe + 1)

    rows_of = [
        jnp.sum(grad_ffn * hat2, axis=0, keepdims=True),
        jnp.sum(grad_ffn, axis=0, keepdims=True),
        jnp.sum(grad_top, axis=0, keepdims=True),
    ]
    for c in range(z.peers):
        j = c // 2
        for r, row in enumerate(rows_of):
            vg_s[c, r : r + 1, :] = row[:, j * LANES : (j + 1) * LANES]
        vg_s[c, 3:4, :] = jnp.sum(gp_s[c].astype(f32), axis=0, keepdims=True)
        up_row = jnp.sum(gh_s[c].astype(f32), axis=0, keepdims=True)
        for r in range(per):
            vg_s[c, 4 + r : 5 + r, :] = up_row[:, r * LANES : (r + 1) * LANES]
    for m in range(z.micros):
        wait_bytes(rx3.at[pl.ds(m * z.slots, z.slots)], recv.at[A3 + m])
        if m == 0:
            pl.when(pipe == 0)(hidden_rows)
        for i, tile in enumerate(lane_tiles(lambda k: rx3[m * z.slots + k], tok)):
            masked_store(gs, 0, m, i, tile * gelu_slope(conv_out[m * z.blocks + i]))

        def back_one(h):
            ys[pl.ds(h, z.conv_rows, stride=z.ch), :] = dot(windows(gs, m, h, False), far[h])

        each_channel(back_one, ch)
        tiles = [
            masked_sum(m, i) + skip[...] * whole_tile(gs, 0, m, i) for i in range(z.blocks)
        ]
        lane_pieces(tiles, m, tx4)
        pl.when(pipe == 0)(lambda: to_micro(m, tx4, rx4, A4))
        pl.when(pipe > 0)(lambda: to_micro(m, tx4, rx4n, A4N, pipe - 1))


    @pl.when(pipe > 0)
    def _():
        top_rows(0)
        top_rows(1)
        hidden_rows()


    @pl.when(pipe == last)
    def _():
        to_peers(lambda c: lay_t.at[c], hid_rx, HID)
        forward_rows()

    many = z.peers * rows
    grads = (
        (ac, AC, bg, BG, z.hid, width, pdown, kdown, sdown, ldown, ddown),
        (fi, FI, gh, GH, width, z.hid, pup, kup, sup, lup, dup),
        (gp, GP, ga, GA, 2 * z.cw, width, pglu, kglu, sglu, lglu, dglu),
    )

    def product(t):
        left, lp, right, rp, n_left, n_right, local, krx, *_ = grads[t]
        wait_bytes(left, recv.at[lp])
        if rp == BG:
            for part in range(2):
                wait_bytes(bg.at[:, :, pl.ds(0, width // 2)], recv.at[BG + part])
        else:
            wait_bytes(right, recv.at[rp])
        local[...] = dot_tn(left[...].reshape(many, n_left), right[...].reshape(many, n_right))
        half = n_left // 2
        other = pl.ds(pl.multiple_of((1 - core) * half, half), half)
        remote(local.at[other], krx, GRADS + 3 * t, sibling).start()

    def chip_sum(t):
        _, _, _, _, n_left, _, part, krx, lsend, lrx, _ = grads[t]
        half = n_left // 2
        own = pl.ds(pl.multiple_of(core * half, half), half)
        wait_bytes(krx, recv.at[GRADS + 3 * t])
        lsend[...] = (part[own, :] + krx[...]).astype(bf16)
        remote(lsend, lrx, GRADS + 3 * t + 1, across).start()

    def both_chips(t):
        _, _, _, _, n_left, _, _, _, lsend, lrx, final = grads[t]
        half = n_left // 2
        own = pl.ds(pl.multiple_of(core * half, half), half)
        wait_bytes(lrx, recv.at[GRADS + 3 * t + 1])
        final[own, :] = lsend[...].astype(f32) + lrx[...].astype(f32)
        remote(final.at[own], final.at[own], GRADS + 3 * t + 2, sibling).start()

    to_members(lambda p: vg_s.at[p // z.groups], vrx, me, VG)
    product(0)

    def lag_one(h):
        x = [
            xs[pl.ds(m * z.stack + pad_rows + h, z.conv_rows, stride=z.ch), :]
            for m in range(z.micros)
        ]
        g = jnp.concatenate([windows(gs, m, h, False) for m in range(z.micros)], axis=0)
        prod = dot_tn(jnp.concatenate(x, axis=0).astype(bf16), g)
        prod = jnp.concatenate([prod, jnp.zeros((LANES, LANES), f32)], axis=1)
        size = LANES // 2
        while size >= 8:
            prod = prod[:size] + shifted(prod[size:], wide - size)
            size //= 2
        for t in range(z.blocks + 1):
            rest_s[t, pl.ds(pl.multiple_of(h * 8, 8), 8), :] = prod[:, t * LANES : (t + 1) * LANES]

    def lag_rest():
        total = None
        for a in range(8):
            tiles = [rest_s[t, pl.ds(a, ch, stride=8), :] for t in range(z.blocks + 1)]
            part = shifted(jnp.concatenate(tiles, axis=1), wide - a)
            total = part if total is None else total + part
        lag_s[...] = total

    each_channel(lag_one, 4, 0, ch // 2)
    chip_sum(0)
    each_channel(lag_one, 4, ch // 2, ch)
    lag_rest()
    product(1)
    product(2)


    @pl.when(pipe == 0)
    def _():
        hat, inv = norm_stats(res[...].astype(f32))
        wait_bytes(rx4, recv.at[A4])
        grad_in = jnp.where(row_ok, turn_in(rx4), 0.0)
        grad_res = mid_s[...] + norm_back(grad_in, hat, inv, full_row(vec_all, 0))
        turn_out(grad_res, ig_t)
        to_peers(lambda c: ig_t.at[c], ig_rx, IG)
        pair = (
            jnp.sum(grad_in * hat, axis=0, keepdims=True),
            jnp.sum(grad_in, axis=0, keepdims=True),
        )
        for c in range(z.peers):
            for r, row in enumerate(pair):
                vg0_s[c, r : r + 1, :] = row[:, (c // 2) * LANES : (c // 2 + 1) * LANES]
        to_members(lambda p: vg0_s.at[p // z.groups], vnrx, me, VGN)

    chip_sum(1)
    chip_sum(2)

    both = dot_nt(high_low(lag_s[:, 0 : z.length]), table[...])
    grad_spec = both[0:ch] + both[ch : 2 * ch]
    gk = (grad_spec[:, 0:padded], grad_spec[:, padded : 2 * padded])
    y_all, ms, cross, over = moments()
    g_top = times(conj(over), gk)
    g_top = (-cosine * g_top[0], -cosine * g_top[1])
    g_low = times(conj(times(times(cross, over), over)), gk)
    g_three = (cosine * cosine * g_low[0], cosine * cosine * g_low[1])
    g_ms = [gk, times(conj(ms[2]), g_top), times(conj(ms[1]), g_top), g_three]
    g_rise = None
    for v, (g_r, g_i) in enumerate(g_ms):
        gsum_s[v, :, 0:padded] = 2.0 * cosine * g_r
        gsum_s[v, :, padded : 2 * padded] = -2.0 * cosine * g_i
        gsum_s[4 + v, :, 0:padded] = 2.0 * y_all * g_i
        gsum_s[4 + v, :, padded : 2 * padded] = 2.0 * y_all * g_r
        part = 2.0 * (sums_s[12 + v] * g_r + sums_s[8 + v] * g_i)
        g_rise = part if g_rise is None else g_rise + part
    slope_s[...] = g_rise
    gcol_s[...] = jnp.zeros(gcol_s.shape, f32)
    gstep_s[...] = jnp.zeros(gstep_s.shape, f32)

    def split(x):
        high_part = x.astype(bf16)
        return high_part, (x - high_part.astype(f32)).astype(bf16)

    g_high, g_low = split(gsum_s[...].reshape(8 * ch, 2 * padded))
    own = [jnp.where(lax.rem(spot, ch) == h, cols[0], 0.0) for h in range(ch)]
    c_high, c_low = split(jnp.concatenate(own, axis=0))
    guw_s[...] = dot(c_high, g_high) + dot(c_high, g_low) + dot(c_low, g_high)
    uw_high, uw_low = split(uw_s[...])
    g_cols = dot_nt(uw_high, g_high) + dot_nt(uw_high, g_low) + dot_nt(uw_low, g_high)
    total = g_cols[0:nh]
    for h in range(1, ch):
        total = jnp.where(lax.rem(spot, ch) == h, g_cols[h * nh : (h + 1) * nh], total)
    gcol_s[0] = total

    def mode_one(h):
        at = pl.ds(pl.multiple_of(h * nh, nh), nh)
        u, w = uw_s[at, 0:padded], uw_s[at, padded : 2 * padded]
        gu, gw = guw_s[at, 0:padded], guw_s[at, padded : 2 * padded]
        double = column_of(1, h)[:, ch : ch + 1]
        y = rise_s[pl.ds(h, 1), 0:1] * sine
        even, cross_uw = u * u - w * w, 2.0 * u * w
        g_den_r = -(even * gu + cross_uw * gw)
        g_den_i = even * gw - cross_uw * gu
        ge = jnp.sum(cosine * cosine * g_den_r, axis=1, keepdims=True)
        gf = jnp.sum(cosine * y * g_den_i, axis=1, keepdims=True)
        acc = jnp.where(spot == h, ge, gcol_s[1])
        gcol_s[1] = jnp.where(spot == ch + h, gf, acc)
        gy = slope_s[pl.ds(h, 1), :] + jnp.sum(
            double * cosine * g_den_i - 2.0 * y * g_den_r, axis=0, keepdims=True
        )
        total_y = jnp.sum(y * gy, axis=1, keepdims=True)
        gstep_s[0:1, :] = jnp.where(spot == h, -total_y, gstep_s[0:1, :])

    each_channel(mode_one, 4)

    def unpacked(k, i):
        return shifted(gcol_s[k], LANES - i * ch)

    g_square, g_double = unpacked(1, 0), unpacked(1, 1)
    g_decay = 2.0 * decay * g_square + 2.0 * g_double
    g_rate = 2.0 * rate * g_square
    g_pairs = []
    for v, (v_r, v_i) in enumerate(pairs):
        g_alpha, g_beta = unpacked(0, v), unpacked(0, 4 + v)
        g_decay = g_decay + g_alpha * v_r
        if v_i is not None:
            g_rate = g_rate - g_alpha * v_i
        g_pairs.append((decay * g_alpha + g_beta, -rate * g_alpha))
    c_b, c_p, p_b = g_pairs[0], g_pairs[1], g_pairs[2]
    p_p = g_pairs[3][0]
    rank, into, out = (rank_r, rank_i), (in_r, in_i), (out_r, out_i)

    def plus(*terms):
        return sum(t[0] for t in terms), sum(t[1] for t in terms)

    g_out = plus(times(conj(into), c_b), times(conj(rank), c_p))
    g_in = plus(times(conj(out), c_b), times(rank, p_b))
    g_rank = plus(
        times(conj(out), c_p),
        times(into, conj(p_b)),
        (2.0 * rank_r * p_p, 2.0 * rank_i * p_p),
    )
    modes_tx[0:nh, :] = packed([g_decay, g_rate, *g_rank, *g_in, *g_out])
    modes_tx[nh : nh + 8, :] = gstep_s[...]
    skip_row = jnp.sum(jnp.where(diagonal, lag_s[:, 0:1], 0.0), axis=0, keepdims=True)
    modes_tx[nh + 1 : nh + 2, :] = skip_row
    for k in range(1, z.groups):
        remote(modes_tx, modes_rx.at[data], MODES, place(chan, lax.rem(data + k, z.groups))).start()
    pltpu.make_async_copy(modes_tx, modes_rx.at[data], recv.at[MODES]).start()

    for t in range(3):
        both_chips(t)


    @pl.when(pipe == last)
    def _():
        wait_bytes(hid_rx, recv.at[HID])
        collect(hid_rx, hid_out)

    wait_bytes(ig_rx, recv.at[IG])
    collect(ig_rx, ig_out)
    wait_bytes(vrx, recv.at[VG])
    wait_bytes(vnrx, recv.at[VGN])
    summed, summed_one = vrx[0], vnrx[0]
    for p in range(1, z.members):
        summed = summed + vrx[p]
        summed_one = summed_one + vnrx[p]
    upb_out[...] = jnp.concatenate([summed[4 + r : 5 + r, :] for r in range(per)], axis=1)
    summed, summed_one = own_half(summed), own_half(summed_one)
    for r in range(3):
        ffn_out[r] = summed[r : r + 1, 0 : z.cw]
    glub_out[0:1, :] = summed[3:4, 0 : z.cw]
    glub_out[1:2, :] = shifted(summed[3:4], LANES // 2)[:, 0 : z.cw]
    vec_out[0:2, :] = summed_one[0:2, 0 : z.cw]
    wait_bytes(modes_rx, recv.at[MODES])

    def over_groups(take):
        total = take(0)
        for d in range(1, z.groups):
            total = jnp.where(spot // ch == d, take(d), total)
        return total[:, 0 : z.cw]

    for p in range(8):
        modes_out[p] = over_groups(
            lambda d: shifted(modes_rx[d, 0:nh, :], (d - p) * ch)
        )
    for r in range(2):
        vec_out[2 + r : 3 + r, :] = over_groups(
            lambda d: shifted(modes_rx[d, nh + r : nh + r + 1, :], d * ch)
        )
    for t, (_, _, _, _, n_left, _, _, _, _, _, final) in enumerate(grads):
        half = n_left // 2
        other = pl.ds(pl.multiple_of((1 - core) * half, half), half)
        wait_bytes(final.at[other], recv.at[GRADS + 3 * t + 2])
    glu_out[0] = dglu[pl.ds(pl.multiple_of(odd * z.cw, z.cw), z.cw), :]
    glu_out[1] = dglu[pl.ds(pl.multiple_of((1 - odd) * z.cw, z.cw), z.cw), :]

    weights_all((weights_sent,), GLU, UPA, UPB, DNA, DNB)
    for ref, phase in (
        (vec_all, VEC), (hid_rx, HID), (ga, GA), (fi, FI), (ac, AC), (gh, GH), (gp, GP),
    ):
        wait_bytes(ref.at[pl.ds(0, z.peers - 1)], send.at[phase])
    for part in range(2):
        sent = bg.at[pl.ds(0, z.peers - 1), :, pl.ds(0, width // 2)]
        wait_bytes(sent, send.at[BG + part])
    for ref, phase in ((rx2, A2), (rx3, A3 + own_micro), (vrx, VG)):
        wait_bytes(ref.at[pl.ds(0, z.members - 1)], send.at[phase])
    wait_bytes(modes_rx.at[pl.ds(0, z.groups - 1)], send.at[MODES])
    for t, (_, _, _, _, n_left, _, _, krx, lsend, _, final) in enumerate(grads):
        wait_bytes(krx, send.at[GRADS + 3 * t])
        wait_bytes(lsend, send.at[GRADS + 3 * t + 1])
        wait_bytes(final.at[pl.ds(0, n_left // 2)], send.at[GRADS + 3 * t + 2])

    @pl.when(pipe == 0)
    def _():
        wait_bytes(tok_rx.at[pl.ds(0, z.peers - 1)], send.at[TOK])
        wait_bytes(ig_rx.at[pl.ds(0, z.peers - 1)], send.at[IG])
        wait_bytes(stat_rx.at[pl.ds(0, z.peers - 1)], send.at[STAT])
        wait_bytes(entry_rx.at[pl.ds(0, z.groups - 1)], send.at[ENTRY])
        for ref, phase in ((rx4, A4), (vnrx, VGN)):
            wait_bytes(ref.at[pl.ds(0, z.members - 1)], send.at[phase])

    @pl.when(pipe == last)
    def _():
        wait_bytes(cot_rx.at[pl.ds(0, z.peers - 1)], send.at[COT])

    @pl.when(pipe < last)
    def _():
        for ref, phase in ((rx1, A1 + own_micro), (lay_s, RES), (ig_rx, IG), (vnrx, VGN)):
            wait_bytes(ref, send.at[phase])

    @pl.when(pipe > 0)
    def _():
        for ref, phase in ((vec_all, VECN), (mid_s, MID), (rx4, A4N)):
            wait_bytes(ref, send.at[phase])


def finish_kernel(*refs):
    count = (len(refs) - 1) // 3
    sems = refs[-1]
    sources, targets, held = refs[:count], refs[count : 2 * count], refs[2 * count : -1]
    loads = [pltpu.make_async_copy(sources[i], held[i], sems.at[i]) for i in range(count)]
    stores = [
        pltpu.make_async_copy(held[i], targets[i], sems.at[count + i]) for i in range(count)
    ]
    for load in loads:
        load.start()
    for load, store in zip(loads, stores):
        load.wait()
        store.start()
    for store in stores:
        store.wait()


def body(
    tokens,
    seq_lengths,
    out_cot,
    s4_vectors,
    s4_modes,
    glu_weight,
    glu_bias,
    ffn_vectors,
    up_weight,
    up_bias,
    down_weight,
):
    micros, tok_rows, chan_width = tokens.shape
    width = glu_weight.shape[1]
    hidden = up_weight.shape[2]
    z = Sizes(
        lax.axis_size("pipe"), lax.axis_size("chan"), lax.axis_size("dp"),
        tok_rows, chan_width, width, hidden,
    )
    length = z.length
    padded = -(-(length // 2 + 1) // LANES) * LANES
    nh = s4_modes.shape[3]
    table = jnp.asarray(fourier_table(length, padded).astype(ml_dtypes.bfloat16))
    angles = jnp.asarray(half_angles(length, padded))

    vmem = pl.BlockSpec(memory_space=pltpu.VMEM)
    smem = pl.BlockSpec(memory_space=pltpu.SMEM)
    anywhere = pl.BlockSpec(memory_space=pl.ANY)
    n, r, w, ch = z.peers, z.rows, width, z.ch

    def s(shape, kind=f32):
        return jax.ShapeDtypeStruct(shape, kind)

    def v(shape, kind=bf16):
        return pltpu.VMEM(shape, kind)

    wide = (z.blocks + 1) * LANES
    rows_full, rows_wide, side = v((r, w)), v((r, w), f32), v((r, LANES), f32)
    peer_tiles, exchange = v((n, chan_width, LANES)), v((z.members, z.ch, LANES))
    small = v((n, 8, LANES), f32)
    results = (
        s((micros, chan_width, tok_rows), bf16), s((micros, chan_width, tok_rows), bf16),
        s((4, chan_width)), s((8, nh, chan_width)), s((2, chan_width, w)),
        s((2, chan_width)), s((3, 1, chan_width)), s((w, hidden)), s((1, hidden)),
        s((hidden, w)),
    )
    raw = pl.pallas_call(
        lambda *refs: main_kernel(z, *refs),
        out_shape=results,
        in_specs=[smem] + [vmem] * 11 + [anywhere],
        out_specs=[vmem] * 10,
        scratch_shapes=[
            peer_tiles, peer_tiles, v((16, LANES), f32), v((ch, length, LANES)),
            v((ch, length, LANES)), v((ch, LANES), f32), v((40, LANES), f32),
            peer_tiles, peer_tiles, v((micros * z.stack, LANES), f32),
            v((micros * z.stack, LANES), f32),
            v((2 * padded, length)), v((2, nh, LANES), f32),
            v((ch, LANES), f32), v((16, ch, padded), f32), v((ch * nh, 2 * padded), f32),
            v((ch * nh, 2 * padded), f32), v((z.blocks + 1, 8 * ch, LANES), f32),
            v((8, ch, 2 * padded), f32),
            v((ch, padded), f32), v((ch, wide), f32), v((ch, wide), f32),
            v((2, nh, LANES), f32), v((8, LANES), f32),
            v((nh + 8, LANES), f32), v((z.groups, nh + 8, LANES), f32),
            v((2 * chan_width, w), f32), v((w, hidden), f32), v((hidden, w), f32),
            v((chan_width, w), f32), v((w // 2, hidden), f32), v((hidden // 2, w), f32),
            v((chan_width, w)), v((w // 2, hidden)), v((hidden // 2, w)),
            v((chan_width, w)), v((w // 2, hidden)), v((hidden // 2, w)),
            v((2 * chan_width, w), f32),
            v((n, 16, LANES), f32), v((n, 16, LANES), f32),
            v((2, n, chan_width, w)), v((n, w, hidden)),
            v((n, hidden, w)), peer_tiles, peer_tiles, rows_full, rows_full,
        ]
        + [exchange] * 9
        + [
            v((z.micros * z.blocks, z.ch, LANES), f32), v((z.conv_rows * z.ch, LANES), f32),
            rows_wide, side, rows_wide, side,
            rows_wide, rows_wide, v((n, r, hidden), f32),
            rows_full, rows_full, v((n, r, hidden)), v((n, r, hidden)), v((n, r, LANES)),
            rows_full, peer_tiles, peer_tiles, peer_tiles, rows_wide, rows_wide,
            v((8, z.over), f32), v((n, 8, z.over), f32),
            v((z.groups, micros, ch, z.over)), v((z.groups, micros, ch, z.over)),
            small, small, small,
            v((n, r, w)), v((n, r, w)), v((n, r, hidden)), v((n, r, w)), v((n, r, hidden)),
            v((n, r, LANES)), v((z.members, 8, LANES), f32), v((z.members, 8, LANES), f32),
            pltpu.SemaphoreType.DMA((68,)), pltpu.SemaphoreType.DMA((68,)),
        ],
        compiler_params=pltpu.CompilerParams(
            collective_id=0, has_side_effects=True, vmem_limit_bytes=60 * 2**20
        ),
        name="layers",
    )(
        seq_lengths, tokens.transpose(0, 2, 1), out_cot.transpose(0, 2, 1), s4_vectors[0],
        s4_modes[0].transpose(0, 2, 1), glu_weight[0].transpose(1, 2, 0), glu_bias[0],
        ffn_vectors.transpose(1, 0, 2), up_weight[0], up_bias, down_weight[0], angles, table,
    )
    hid, ig, vec, modes, dglu, glub, ffn, dup, upb, ddown = pl.pallas_call(
        finish_kernel,
        out_shape=results,
        in_specs=[anywhere] * 10,
        out_specs=[anywhere] * 10,
        scratch_shapes=[pltpu.VMEM(x.shape, x.dtype) for x in results]
        + [pltpu.SemaphoreType.DMA((20,))],
        compiler_params=pltpu.CompilerParams(vmem_limit_bytes=60 * 2**20),
        name="finish",
    )(*raw)
    return (
        hid.transpose(0, 2, 1)[None], ig.transpose(0, 2, 1)[None], vec[None],
        modes.transpose(0, 2, 1)[None], dglu.transpose(2, 0, 1)[None], glub[None],
        ffn.transpose(1, 0, 2), dup[None], upb, ddown[None],
    )


def solution(mesh):
    placed = (
        P(None, "dp", "chan"),
        P(),
        P(None, "dp", "chan"),
        P("pipe", None, "chan"),
        P("pipe", None, "chan", None),
        P("pipe", None, None, "chan"),
        P("pipe", None, "chan"),
        P("pipe", None, "chan"),
        P("pipe", None, "chan"),
        P("pipe", "chan"),
        P("pipe", "chan", None),
    )
    return jax.shard_map(
        body,
        mesh=mesh,
        in_specs=placed,
        out_specs=(
            P("pipe", None, "dp", "chan"),
            P("pipe", None, "dp", "chan"),
            P("pipe", None, "chan"),
            P("pipe", None, "chan", None),
            P("pipe", None, None, "chan"),
            P("pipe", None, "chan"),
            P("pipe", None, "chan"),
            P("pipe", None, "chan"),
            P("pipe", "chan"),
            P("pipe", "chan", None),
        ),
        check_vma=False,
    )
```
